32 devices in a mesh: fsdp: 8 (over z, y), ctx: 4 (over x, core).
Axes of the slice: x: 2, y: 2, z: 4, core: 2. Of those that a mesh axis runs over, the one named last changes fastest.
Arguments:
- tokens: bfloat16 [8, 2, 4, 384, 512], P('fsdp', None, 'ctx'), may hold values from -6 to 6
- query_weight: bfloat16 [512, 512], P('fsdp'), may hold values from -0.25 to 0.25
- query_bias: bfloat16 [512], P('fsdp'), may hold values from -1.796875 to 1.796875
- key_weight: bfloat16 [512, 512], P('fsdp'), may hold values from -0.25 to 0.25
- value_weight: bfloat16 [512, 512], P('fsdp'), may hold values from -0.25 to 0.25
- value_bias: bfloat16 [512], P('fsdp'), may hold values from -1.796875 to 1.796875
- out_weight: bfloat16 [512, 512], P('fsdp'), may hold values from -1 to 1
- out_bias: bfloat16 [512], P('fsdp'), may hold values from -1.796875 to 1.796875
- first_gain: bfloat16 [512], P('fsdp'), may hold values from 0.5 to 1.5
- first_shift: bfloat16 [512], P('fsdp'), may hold values from -1.796875 to 1.796875
- inner_weight: bfloat16 [512, 2048], P('fsdp'), may hold values from -0.25 to 0.25
- inner_bias: bfloat16 [2048], P('fsdp'), may hold values from -1.796875 to 1.796875
- outer_weight: bfloat16 [2048, 512], P('fsdp'), may hold values from -0.1875 to 0.1875
- outer_bias: bfloat16 [512], P('fsdp'), may hold values from -1.796875 to 1.796875
- second_gain: bfloat16 [512], P('fsdp'), may hold values from 0.5 to 1.5
- second_shift: bfloat16 [512], P('fsdp'), may hold values from -1.796875 to 1.796875
- cotangent: bfloat16 [8, 2, 4, 384, 512], P('fsdp', None, 'ctx'), may hold values from -6 to 6
Outputs:
- output: bfloat16 [8, 2, 4, 384, 512], P('fsdp', None, 'ctx')
- tokens_grad: bfloat16 [8, 2, 4, 384, 512], P('fsdp', None, 'ctx')
- query_weight_grad: float32 [512, 512], P('fsdp')
- query_bias_grad: float32 [512], P('fsdp')
- key_weight_grad: float32 [512, 512], P('fsdp')
- value_weight_grad: float32 [512, 512], P('fsdp')
- value_bias_grad: float32 [512], P('fsdp')
- out_weight_grad: float32 [512, 512], P('fsdp')
- out_bias_grad: float32 [512], P('fsdp')
- first_gain_grad: float32 [512], P('fsdp')
- first_shift_grad: float32 [512], P('fsdp')
- inner_weight_grad: float32 [512, 2048], P('fsdp')
- inner_bias_grad: float32 [2048], P('fsdp')
- outer_weight_grad: float32 [2048, 512], P('fsdp')
- outer_bias_grad: float32 [512], P('fsdp')
- second_gain_grad: float32 [512], P('fsdp')
- second_shift_grad: float32 [512], P('fsdp')
The draws below stay inside these ranges and needn't reach their ends.
All inputs are finite; a program needn't handle non-finite values.
Results may differ from the reference program's by a relative error of at most 0.028.
Values may be sent and summed in bfloat16 or wider, within the bound.
A program may use at most 128 MiB of HBM per device.

```python
import math
import jax
import jax.numpy as jnp
from jax import lax

D = 512
HEADS = 8
HEAD = 64
FF = 2048
BLK = 384
SEQS = 8
LEN = 3072
N_CTX = 4


def steps_of(key, extent, split, smallest, largest):
    factor_of = 1.0
    for position, blocks in split:
        draws = jax.random.uniform(jax.random.fold_in(jax.random.fold_in(key, 6), position), (blocks,), jnp.float32, smallest / len(split), largest / len(split))
        factor_of = factor_of * jnp.repeat(jnp.exp(draws), extent[position] // blocks).reshape((-1,) + (1,) * (len(extent) - 1 - position))
    return factor_of


def bell_draw(stream_key, extent, deviation, limit, split=(), held_as=jnp.bfloat16):
    values = jax.random.normal(stream_key, extent, jnp.float32) * deviation
    if len(split) > 0:
        values = steps_of(stream_key, extent, split, -0.22, 0.18) * values
    return jnp.clip(values, min=-limit, max=limit).astype(held_as)


def setup_inputs(seed: int = 0) -> dict:
    arg_keys = jax.random.split(jax.random.key(seed), 18)
    return {
        "tokens": bell_draw(arg_keys[0], (SEQS, 2, N_CTX, BLK, D), 1.0, 6.0, ((0, 8), (2, 4))),
        "query_weight": bell_draw(arg_keys[1], (D, D), D ** -0.5, 0.25, ((0, 8),)),
        "query_bias": bell_draw(arg_keys[2], (D,), 0.3, 1.796875, ((0, 8),)),
        "key_weight": bell_draw(arg_keys[3], (D, D), D ** -0.5, 0.25, ((0, 8),)),
        "value_weight": bell_draw(arg_keys[4], (D, D), D ** -0.5, 0.25, ((0, 8),)),
        "value_bias": bell_draw(arg_keys[5], (D,), 0.3, 1.796875, ((0, 8),)),
        "out_weight": bell_draw(arg_keys[6], (D, D), (D // 16) ** -0.5, 1.0, ((0, 8),)),
        "out_bias": bell_draw(arg_keys[7], (D,), 0.3, 1.796875, ((0, 8),)),
        "first_gain": jnp.clip(1.0 + 0.1 * jax.random.normal(arg_keys[8], (D,), jnp.float32), 0.5, 1.5).astype(jnp.bfloat16),
        "first_shift": bell_draw(arg_keys[9], (D,), 0.3, 1.796875, ((0, 8),)),
        "inner_weight": bell_draw(arg_keys[10], (D, FF), D ** -0.5, 0.25, ((0, 8),)),
        "inner_bias": bell_draw(arg_keys[11], (FF,), 0.3, 1.796875, ((0, 8),)),
        "outer_weight": bell_draw(arg_keys[12], (FF, D), (FF // 2) ** -0.5, 0.1875, ((0, 8),)),
        "outer_bias": bell_draw(arg_keys[13], (D,), 0.3, 1.796875, ((0, 8),)),
        "second_gain": jnp.clip(1.0 + 0.1 * jax.random.normal(arg_keys[14], (D,), jnp.float32), 0.5, 1.5).astype(jnp.bfloat16),
        "second_shift": bell_draw(arg_keys[15], (D,), 0.3, 1.796875, ((0, 8),)),
        "cotangent": bell_draw(arg_keys[16], (SEQS, 2, N_CTX, BLK, D), 1.0, 6.0, ((0, 8), (2, 4))),
    }


@jax.custom_vjp
def low(v):
    return lax.optimization_barrier(v.astype(jnp.bfloat16)).astype(jnp.float32)

@jax.custom_vjp
def low_back(v):
    return v

def low_keep(v):
    return (low(v), None)

def low_pass(kept, grad):
    return (grad,)

def back_keep(v):
    return (v, None)

def back_low(kept, grad):
    return (low(grad),)
low.defvjp(low_keep, low_pass)
low_back.defvjp(back_keep, back_low)

def matmul(left, right):
    return jnp.dot(left, right, precision=lax.Precision.HIGHEST)

def layer_norm(rows, gain, shift):
    center = rows - lax.optimization_barrier(jnp.mean(rows, axis=-1, keepdims=True))
    spread = lax.optimization_barrier(jnp.mean(center * center, axis=-1, keepdims=True))
    return center * lax.rsqrt(spread + 1e-05) * gain + shift

def natural(dealt):
    first = dealt[:, 0]
    second = jnp.flip(dealt[:, 1], axis=1)
    joined = jnp.concatenate([first, second], axis=1)
    return joined.reshape(joined.shape[0], LEN, D)

def dealt_order(rows):
    blocks = rows.reshape(rows.shape[0], 2 * N_CTX, BLK, D)
    return jnp.stack([blocks[:, :N_CTX], jnp.flip(blocks[:, N_CTX:], axis=1)], axis=1)

def attend_head(operands):
    query, keys, values = operands
    scores = low_back(matmul(query, keys.T)) * (1.0 / math.sqrt(HEAD))
    places = jnp.arange(LEN)
    allowed = places[:, None] >= places[None, :]
    scores = jnp.where(allowed, scores, -1e+30)
    row_top = lax.optimization_barrier(jnp.max(scores, axis=-1, keepdims=True))
    weights = jnp.exp(scores - row_top)
    probs = weights / lax.optimization_barrier(jnp.sum(weights, axis=-1, keepdims=True))
    return matmul(low(probs), values)

def split_heads(matrix):
    return matrix.reshape(LEN, HEADS, HEAD).transpose(1, 0, 2)

def forward(rows, params):
    w_query, b_query, w_key, w_value, b_value, w_out, b_out, gain_one, shift_one, w_inner, b_inner, w_outer, b_outer, gain_two, shift_two = params
    inputs = low(rows)
    query = low(low_back(matmul(inputs, w_query) + b_query))
    keys = low(low_back(matmul(inputs, w_key)))
    values = low(low_back(matmul(inputs, w_value) + b_value))
    heads_out = lax.map(jax.checkpoint(attend_head), (split_heads(query), split_heads(keys), split_heads(values)))
    mixed = heads_out.transpose(1, 0, 2).reshape(LEN, D)
    mixed = low(low_back(mixed))
    branch = low_back(matmul(mixed, w_out) + b_out)
    middle = layer_norm(rows + branch, gain_one, shift_one)
    hidden = low_back(matmul(low(middle), w_inner) + b_inner)
    active = low(jax.nn.gelu(hidden, approximate=True))
    second = low_back(matmul(active, w_outer) + b_outer)
    return layer_norm(middle + second, gain_two, shift_two)

def reference(tokens, query_weight, query_bias, key_weight, value_weight, value_bias, out_weight, out_bias, first_gain, first_shift, inner_weight, inner_bias, outer_weight, outer_bias, second_gain, second_shift, cotangent):
    params = tuple((weight.astype(jnp.float32) for weight in (query_weight, query_bias, key_weight, value_weight, value_bias, out_weight, out_bias, first_gain, first_shift, inner_weight, inner_bias, outer_weight, outer_bias, second_gain, second_shift)))
    rows_all = natural(tokens.astype(jnp.float32))
    grads_all = natural(cotangent.astype(jnp.float32))

    def one_sequence(carry, operands):
        rows, incoming = operands
        result, pull = jax.vjp(forward, rows, params)
        back_rows, back_params = pull(incoming)
        carry = tuple((total + term for total, term in zip(carry, back_params)))
        return (carry, (result, back_rows))
    zeros = tuple((jnp.zeros(weight.shape, jnp.float32) for weight in params))
    totals, (results, backs) = lax.scan(one_sequence, zeros, (rows_all, grads_all))
    output = dealt_order(results).astype(jnp.bfloat16)
    tokens_grad = dealt_order(backs).astype(jnp.bfloat16)
    return (output, tokens_grad, totals[0], totals[1], totals[2], totals[3], totals[4], totals[5], totals[6], totals[7], totals[8], totals[9], totals[10], totals[11], totals[12], totals[13], totals[14])
```

```python
import functools
import math

import jax
import jax.numpy as jnp
from jax import lax
from jax.experimental import pallas as pl
from jax.experimental.pallas import tpu as pltpu
from jax.sharding import PartitionSpec as P

HEADS = 8
HEAD = 64
D = 512
FF = 2048
CTX = 4
SHARDS = 8
EPS = 1e-5
BF = jnp.bfloat16
F32 = jnp.float32
QUERY_SCALE = math.log2(math.e) / math.sqrt(HEAD)
SCALE = 1.0 / math.sqrt(HEAD)
LN2 = math.log(2.0)
G1_ROWS = 288
G2_ROWS = 112


def dot(left, right, left_dim=1, right_dim=0):
    return lax.dot_general(
        left, right, (((left_dim,), (right_dim,)), ((), ())), preferred_element_type=F32
    )


def rows_mean(value):
    return jnp.mean(value, axis=-1, keepdims=True)


def layer(ring, blk, *refs):
    it = iter(refs)
    take = lambda count: [next(it) for _ in range(count)]
    tok, cot = take(2)
    weights_in = take(6)
    small_in = take(1 if ring else 2)
    out_ref, tg_ref = take(2)
    if ring:
        grads_out = take(6)
        gsm_ref = next(it)
    else:
        p1_out, p2_out = take(2)
    X, K, V = take(3)
    Wq, Wk, Wv, Wo, Wi, Wu = weights = take(6)
    vec, vec_inner = take(2)
    Q, QTa, dO, dOTa = take(4)
    VTa, KT = take(2)
    top, acc, OT = take(3)
    Hlow, n1, rstd1 = take(3)
    Z, dU, dF, dR, dA = take(5)
    dwk, dwv = take(2)
    dka, dva = n1.at[0], n1.at[1]
    sums, sums_inner = take(2)
    cot_v = next(it)
    tg_v = dO
    P1, P2 = take(2)
    sib_out, sib_in, rel_out, rel_in, far_out, far_in = take(6)
    load_sem, out_sem, xs, xr = take(4)
    ds, dr = take(2)
    if ring:
        small_all = next(it)
        RC1, RY1, RZ1, FX1, RX1, FIN1 = take(6)
        RC2, RY2, RZ2, FX2, RX2, FIN2 = take(6)
        zs, ys, cs, rr, rc, ms, mr, gs, gr = take(9)

    t = lax.axis_index("ctx")
    chip, core = t // 2, lax.rem(t, 2)
    sib = t + 1 - 2 * core
    far = lax.rem(t + 2, 4)
    c = t
    MESH = pl.DeviceIdType.MESH

    def to(ref, dst, send, recv, **where):
        return pltpu.make_async_remote_copy(
            src_ref=ref,
            dst_ref=dst,
            send_sem=send,
            recv_sem=recv,
            device_id=where,
            device_id_type=MESH,
        )

    def arrived(ref, sem):
        pltpu.make_async_copy(ref, ref, sem).wait()

    def left(ref, sem):
        pltpu.make_async_copy(ref, ref, sem).wait()

    peers = [{"ctx": sib}, {"ctx": far}]
    if ring:
        f = lax.axis_index("fsdp")
        z, y = f // 2, lax.rem(f, 2)
        fy = f + 1 - 2 * y
        zpeer = [lax.rem(z + dz, 4) * 2 + y for dz in (1, 2, 3)]
        peers += [{"fsdp": fy}] + [{"fsdp": zp} for zp in zpeer]

    own_blocks = [c, 7 - c]
    loads = []
    for sec in range(2):
        loads.append(
            pltpu.make_async_copy(tok.at[sec], X.at[own_blocks[sec]], load_sem.at[sec])
        )
        loads.append(
            pltpu.make_async_copy(cot.at[sec], cot_v.at[sec], load_sem.at[2 + sec])
        )
    for w in range(6):
        rows = weights_in[w].shape[0]
        dst = weights[w].at[pl.ds(f * rows, rows)] if ring else weights[w]
        loads.append(pltpu.make_async_copy(weights_in[w], dst, load_sem.at[4 + w]))
    if ring:
        loads.append(
            pltpu.make_async_copy(small_in[0], small_all.at[f], load_sem.at[10])
        )
    else:
        loads.append(pltpu.make_async_copy(small_in[0], vec, load_sem.at[10]))
        loads.append(pltpu.make_async_copy(small_in[1], vec_inner, load_sem.at[11]))
    for copy in loads:
        copy.start()

    barrier = pltpu.get_barrier_semaphore()
    for where in peers:
        pl.semaphore_signal(barrier, inc=1, device_id=where, device_id_type=MESH)
    pl.semaphore_wait(barrier, len(peers))

    for sec in range(2):
        b = own_blocks[sec]
        to(tok.at[sec], X.at[b], xs.at[sec], xr.at[b], ctx=sib).start()
    to(tok.at[0], X.at[c], xs.at[2], xr.at[c], ctx=far).start()

    @pl.when(chip == 1)
    def _():
        to(tok.at[1], X.at[7 - c], xs.at[3], xr.at[7 - c], ctx=far).start()

    if ring:
        def piece(w, s, half):
            rows = weights_in[w].shape[0]
            return weights[w].at[pl.ds(s * rows + half * (rows // 2), rows // 2)]

        def gather_start(w):
            rows = weights_in[w].shape[0]
            src = weights_in[w].at[pl.ds(core * (rows // 2), rows // 2)]
            for i in range(3):
                to(src, piece(w, f, core), zs.at[w, i], rr.at[w, f], fsdp=zpeer[i]).start()
            to(src, piece(w, f, core), ys.at[w, 0], rr.at[w, f], fsdp=fy).start()

        def gather_z(w):
            for i in range(3):
                s = zpeer[i]
                ref = piece(w, s, core)
                arrived(ref, rr.at[w, s])
                to(ref, ref, ys.at[w, 1 + i], rr.at[w, s], fsdp=fy).start()
                to(ref, ref, cs.at[w, i], rc.at[w, s], ctx=sib).start()

        def gather_y(w):
            for i in range(4):
                s = lax.rem(z + i, 4) * 2 + 1 - y
                ref = piece(w, s, core)
                arrived(ref, rr.at[w, s])
                to(ref, ref, cs.at[w, 3 + i], rc.at[w, s], ctx=sib).start()

        def gather_end(w):
            for i in range(1, 8):
                s = lax.rem(f + i, 8)
                arrived(piece(w, s, 1 - core), rc.at[w, s])
            loads[4 + w].wait()

        def gather_left(w):
            rows = weights_in[w].shape[0]
            ref = weights[w].at[pl.ds(0, rows // 2)]
            for i in range(3):
                left(ref, zs.at[w, i])
            for i in range(4):
                left(ref, ys.at[w, i])
            for i in range(7):
                left(ref, cs.at[w, i])

        for i in range(3):
            to(small_in[0], small_all.at[f], ms.at[i], mr.at[f], fsdp=zpeer[i]).start()
        to(small_in[0], small_all.at[f], ms.at[3], mr.at[f], fsdp=fy).start()
        for w in range(6):
            gather_start(w)
        for i in range(3):
            s = zpeer[i]
            arrived(small_all.at[s], mr.at[s])
            to(small_all.at[s], small_all.at[s], ms.at[4 + i], mr.at[s], fsdp=fy).start()
        for w in range(3):
            gather_z(w)
    else:
        for w in range(6):
            loads[4 + w].wait()

    def far_tokens():
        b = far
        arrived(X.at[b], xr.at[b])
        to(X.at[b], X.at[b], xs.at[4], xr.at[b], ctx=sib).start()

        @pl.when(chip == 0)
        def _():
            b = 7 - far
            arrived(X.at[b], xr.at[b])
            to(X.at[b], X.at[b], xs.at[5], xr.at[b], ctx=sib).start()

    if ring:
        for w in range(3):
            gather_y(w)
        for i in range(4):
            s = lax.rem(z + i, 4) * 2 + 1 - y
            arrived(small_all.at[s], mr.at[s])
        loads[10].wait()
        vec[...] = jnp.concatenate(
            [small_all[s][0:8, 0:64] for s in range(SHARDS)], axis=1
        )
        vec_inner[...] = jnp.concatenate(
            [small_all[s][8 + k : 9 + k] for s in range(SHARDS) for k in range(2)],
            axis=1,
        )
        for w in range(3):
            gather_end(w)
    else:
        loads[10].wait()
        loads[11].wait()
    b_query, b_value, b_out, gain1, shift1, b_outer, gain2, shift2 = (
        vec[pl.ds(j, 1), :] for j in range(8)
    )
    for sec in range(2):
        loads[2 * sec].wait()

    VTa[:, 64:80, :] = jnp.ones((HEADS, 16, blk), BF)
    for h in range(HEADS):
        other = (1 - h % 2) * 64
        for sec in range(2):
            QTa[sec, h, other : other + 64, :] = jnp.zeros((64, blk), BF)
            dOTa[sec, h, other : other + 64, :] = jnp.zeros((64, blk), BF)

    def queries(sec, _):
        x = X[jnp.where(sec == 0, c, 7 - c)]
        q = (dot(x, Wq[...]) + b_query) * QUERY_SCALE
        Q[sec] = q.astype(BF)
        qt = q.T.astype(BF)
        for h in range(HEADS):
            own = (h % 2) * 64
            QTa[sec, h, own : own + 64, :] = qt[h * 64 : h * 64 + 64]
        return 0

    lax.fori_loop(0, 2, queries, 0)

    lane = lax.broadcasted_iota(jnp.int32, (blk, 128), 1)
    key_at = lax.broadcasted_iota(jnp.int32, (blk, blk), 0)
    query_at = lax.broadcasted_iota(jnp.int32, (blk, blk), 1)

    def step_of(i):
        sec = lax.rem(i, 2)
        owner_core = jnp.where(i < 2, 1 - core, core)
        owner = jnp.where(i < 4, 2 * (1 - chip) + owner_core, jnp.where(i < 6, sib, t))
        kb = jnp.where(sec == 0, owner, 7 - owner)
        sent = (i >= 4) | (chip == 0) | (sec == 0)
        return sec, owner, kb, sent, sent & (kb <= 7 - c)

    top[...] = jnp.full(top.shape, -1e30, F32)
    acc[...] = jnp.zeros(acc.shape, F32)

    def attend(sec, kb, diagonal):
        for h in range(HEADS):
            p, a = h // 2, h % 2
            k_pair = K[kb, :, p * 128 : p * 128 + 128]
            k_head = jnp.where((lane < 64) == (a == 0), k_pair, jnp.zeros_like(k_pair))
            s = dot(k_head, QTa[sec, h])
            if diagonal:
                s = jnp.where(key_at <= query_at, s, -1e30)
            old = top[sec, h, 0:1, :]
            new = jnp.maximum(old, jnp.max(s, axis=0, keepdims=True))
            probs = jnp.exp2(s - new).astype(BF)
            shrink = jnp.exp2(old - new)
            acc[sec, h] = acc[sec, h] * shrink + dot(VTa[h], probs)
            top[sec, h] = jnp.broadcast_to(new, (8, blk))

    def keys_values(kb):
        x = X[kb]
        K[kb] = dot(x, Wk[...]).astype(BF)
        v = dot(x, Wv[...]) + b_value
        V[kb] = v.astype(BF)
        vt = v.T.astype(BF)
        for h in range(HEADS):
            VTa[h, 0:64, :] = vt[h * 64 : h * 64 + 64]

    def forward(n, _):
        i = jnp.where(n < 2, 6 + n, jnp.where(n < 4, 2 + n, jnp.where(n < 6, n - 2, n - 6)))
        _, _, kb, sent, used = step_of(i)

        @pl.when(n == 4)
        def _():
            far_tokens()

        if ring:
            for when, w in ((1, 3), (2, 4), (3, 5)):
                pl.when(n == when)(functools.partial(gather_z, w))
            for when, w in ((4, 3), (5, 4), (6, 5)):
                pl.when(n == when)(functools.partial(gather_y, w))

        @pl.when(sent & ((n == 2) | (n == 3) | (n >= 6)))
        def _():
            arrived(X.at[kb], xr.at[kb])

        @pl.when(used)
        def _():
            keys_values(kb)

        def section(sec, _):
            qb = jnp.where(sec == 0, c, 7 - c)

            @pl.when(used & (kb < qb))
            def _():
                attend(sec, kb, False)

            @pl.when(used & (kb == qb))
            def _():
                attend(sec, kb, True)

            return 0

        lax.fori_loop(0, 2, section, 0)
        return 0

    lax.fori_loop(0, 8, forward, 0)

    def finish(sec, _):
        for h in range(HEADS):
            other = (1 - h % 2) * 64
            total = acc[sec, h, 64:65, :]
            OT[sec, h * 64 : h * 64 + 64, :] = (acc[sec, h, 0:64, :] / total).astype(BF)
            low = -(top[sec, h, 0:1, :] + jnp.log2(total))
            parts = []
            for _ in range(3):
                parts.append(low.astype(BF))
                low = low - parts[-1].astype(F32)
            QTa[sec, h, other : other + 16, :] = jnp.concatenate(
                parts + [jnp.zeros((13, blk), BF)], axis=0
            )
        return 0

    lax.fori_loop(0, 2, finish, 0)
    if ring:
        for w in range(3, 6):
            gather_end(w)
    for sec in range(2):
        loads[2 * sec + 1].wait()

    sums[...] = jnp.zeros(sums.shape, F32)
    sums_inner[...] = jnp.zeros(sums_inner.shape, F32)
    ones = jnp.ones((16, blk), BF)

    def column_sum(value):
        return jnp.sum(value, axis=0, keepdims=True)

    def dense(sec, _):
        x = X[jnp.where(sec == 0, c, 7 - c)].astype(F32)
        r1 = x + dot(OT[sec], Wo[...], 0, 0) + b_out
        center = r1 - rows_mean(r1)
        rs1 = lax.rsqrt(rows_mean(center * center) + EPS)
        n1[sec] = center * rs1
        rstd1[sec] = rs1
        hid = center * rs1 * gain1 + shift1
        low = hid.astype(BF)
        Hlow[sec] = low
        c0 = math.sqrt(2.0 / math.pi)
        for cb in range(4):
            cols = slice(cb * 512, cb * 512 + 512)
            u = dot(Hlow[sec], Wi[:, cols]) + vec_inner[:, cols]
            uu = u * u
            th = jnp.tanh(c0 * u * (1.0 + 0.044715 * uu))
            half = 0.5 * (1.0 + th)
            Z[sec, :, cols] = (u * half).astype(BF)
            slope = half + 0.5 * u * (1.0 - th * th) * (c0 * (1.0 + 3 * 0.044715 * uu))
            dU[sec, :, cols] = slope.astype(BF)
        r2 = hid + dot(Z[sec], Wu[...]) + b_outer
        center = r2 - rows_mean(r2)
        rs2 = lax.rsqrt(rows_mean(center * center) + EPS)
        n2 = center * rs2
        g = cot_v[sec].astype(F32)
        cot_v[sec] = (n2 * gain2 + shift2).astype(BF)
        sums[6:7, :] += column_sum(g * n2)
        sums[7:8, :] += column_sum(g)
        g = g * gain2
        d_r2 = (g - rows_mean(g) - n2 * rows_mean(g * n2)) * rs2
        dR[sec] = d_r2
        d_f = d_r2.astype(BF)
        dF[sec] = d_f
        sums[5:6, :] += dot(ones, d_f)[0:1]
        for cb in range(4):
            cols = slice(cb * 512, cb * 512 + 512)
            d_u = (dot(dF[sec], Wu[cols, :], 1, 1) * dU[sec, :, cols].astype(F32)).astype(BF)
            dU[sec, :, cols] = d_u
            sums_inner[0:1, cols] += dot(ones, d_u)[0:1]
        d_h = dR[sec] + dot(dU[sec], Wi[...], 1, 1)
        nn1 = n1[sec]
        sums[3:4, :] += column_sum(d_h * nn1)
        sums[4:5, :] += column_sum(d_h)
        g = d_h * gain1
        d_r1 = (g - rows_mean(g) - nn1 * rows_mean(g * nn1)) * rstd1[sec]
        dR[sec] = d_r1
        d_a = d_r1.astype(BF)
        dA[sec] = d_a
        sums[2:3, :] += dot(ones, d_a)[0:1]
        dO[sec] = dot(dA[sec], Wo[...], 1, 1).astype(BF)
        d_ot = dot(Wo[...], dA[sec], 1, 1)
        for h in range(HEADS):
            own, other = (h % 2) * 64, (1 - h % 2) * 64
            part = d_ot[h * 64 : h * 64 + 64].astype(BF)
            dOTa[sec, h, own : own + 64, :] = part
            o = OT[sec, h * 64 : h * 64 + 64, :].astype(F32)
            rest = -column_sum(part.astype(F32) * o)
            parts = []
            for _ in range(3):
                parts.append(rest.astype(BF))
                rest = rest - parts[-1].astype(F32)
            dOTa[sec, h, other : other + 16, :] = jnp.concatenate(
                parts + [jnp.zeros((13, blk), BF)], axis=0
            )
        return 0

    lax.fori_loop(0, 2, dense, 0)
    out_copy = pltpu.make_async_copy(cot_v, out_ref, out_sem.at[0])
    out_copy.start()

    def both(ref, cols=slice(None)):
        return jnp.concatenate([ref[0, :, cols], ref[1, :, cols]], axis=0)

    for rb in range(4):
        part = dot(both(Z, slice(rb * 512, rb * 512 + 512)), both(dF), 0, 0).astype(BF)
        for k in range(4):
            s, half = 2 * rb + k // 2, k % 2
            P1[half, s % 2, s // 2, 32:160, :] = part[k * 128 : k * 128 + 128]
    for cb in range(4):
        part = dot(both(Hlow), both(dU, slice(cb * 512, cb * 512 + 512)), 0, 0).astype(BF)
        for s in range(SHARDS):
            for half in range(2):
                at = s * 64 + half * 32
                P1[half, s % 2, s // 2, 160 + cb * 32 : 192 + cb * 32, :] = part[at : at + 32]

    def by_owner(dst, value, row):
        for s in range(SHARDS):
            for half in range(2):
                at = s * 64 + half * 32
                dst[half, s % 2, s // 2, row : row + 32, :] = value[at : at + 32]

    ot = jnp.concatenate([OT[0], OT[1]], axis=1)
    by_owner(P1, dot(ot, both(dA)).astype(BF), 0)

    if ring:
        groups = (
            (P1, RC1, RY1, RZ1, FX1, RX1, FIN1),
            (P2, RC2, RY2, RZ2, FX2, RX2, FIN2),
        )

        def add_into(dst, *terms):
            total = dst[...].astype(F32)
            for term in terms:
                total = total + term[...].astype(F32)
            dst[...] = total.astype(BF)

        def reduce_core(g):
            mine, from_core = groups[g][:2]
            for k, yy in ((0, 1 - y), (1, y)):
                to(mine.at[1 - core, yy], from_core.at[k], gs.at[g, k], gr.at[g, k], ctx=sib).start()

        def reduce_y(g):
            mine, from_core, from_y = groups[g][:3]
            arrived(from_core.at[0], gr.at[g, 0])

            def body(k, _):
                add_into(mine.at[core, 1 - y, k], from_core.at[0, k])
                return 0

            lax.fori_loop(0, 4, body, 0)
            to(mine.at[core, 1 - y], from_y, gs.at[g, 2], gr.at[g, 2], fsdp=fy).start()

        def reduce_z(g):
            mine, from_core, from_y, from_z = groups[g][:4]
            arrived(from_core.at[1], gr.at[g, 1])
            arrived(from_y, gr.at[g, 2])

            def body(k, _):
                add_into(mine.at[core, y, k], from_core.at[1, k], from_y.at[k])
                return 0

            lax.fori_loop(0, 4, body, 0)
            for i in range(3):
                zz = lax.rem(z + 1 + i, 4)
                to(mine.at[core, y, zz], from_z.at[i], gs.at[g, 3 + i], gr.at[g, 3 + i], fsdp=zpeer[i]).start()

        def reduce_x(g):
            mine, _, _, from_z, pair, from_x, _ = groups[g]
            for i in range(3):
                arrived(from_z.at[i], gr.at[g, 3 + i])
            pair[...] = (
                mine[core, y, z].astype(F32)
                + from_z[0].astype(F32)
                + from_z[1].astype(F32)
                + from_z[2].astype(F32)
            ).astype(BF)
            to(pair, from_x, gs.at[g, 6], gr.at[g, 6], ctx=far).start()

        def reduce_last(g):
            pair, from_x, final = groups[g][4:]
            arrived(from_x, gr.at[g, 6])
            final[core] = (pair[...].astype(F32) + from_x[...].astype(F32)).astype(BF)
            to(final.at[core], final.at[core], gs.at[g, 7], gr.at[g, 7], ctx=sib).start()

        def reduce_left(g):
            mine, from_core, from_y, from_z, pair, from_x, final = groups[g]
            for k in range(2):
                left(from_core.at[k], gs.at[g, k])
            left(from_y, gs.at[g, 2])
            for i in range(3):
                left(from_z.at[i], gs.at[g, 3 + i])
            left(pair, gs.at[g, 6])
            left(final.at[0], gs.at[g, 7])

        reduce_core(0)

    acc[...] = jnp.zeros(acc.shape, F32)
    dwk[...] = jnp.zeros(dwk.shape, F32)
    dwv[...] = jnp.zeros(dwv.shape, F32)

    def attend_back(sec, kb, diagonal):
        for p in range(4):
            cols = slice(p * 128, p * 128 + 128)
            k_pair, v_pair = K[kb, :, cols], V[kb, :, cols]
            q_pair, do_pair = Q[sec, :, cols], dO[sec, :, cols]
            zero = jnp.zeros_like(q_pair)
            all_p, all_ds, all_q, all_do = [], [], [], []
            for a in range(2):
                h = 2 * p + a
                own = (lane < 64) == (a == 0)
                first = (1 - a) * 64
                one = jnp.where((lane >= first) & (lane < first + 3), 1.0, 0.0).astype(BF)
                s = dot(jnp.where(own, k_pair, one), QTa[sec, h])
                if diagonal:
                    s = jnp.where(key_at <= query_at, s, -1e30)
                probs = jnp.exp2(s)
                dp = dot(jnp.where(own, v_pair, one), dOTa[sec, h])
                d_s = (probs * dp).astype(BF)
                all_p.append(probs.astype(BF))
                all_ds.append(d_s)
                all_q.append(jnp.where(own, q_pair, zero))
                all_do.append(jnp.where(own, do_pair, zero))
                acc[sec, h, 0:64, :] += dot(KT[h * 64 : h * 64 + 64, :], d_s)
            dva[:, cols] += dot(jnp.concatenate(all_p, axis=1), jnp.concatenate(all_do, axis=0))
            dka[:, cols] += dot(jnp.concatenate(all_ds, axis=1), jnp.concatenate(all_q, axis=0))

    def relay(sec):
        arrived(rel_in.at[sec], dr.at[2 + sec])
        far_out[sec] = (far_out[sec].astype(F32) + rel_in[sec].astype(F32)).astype(BF)
        to(far_out.at[sec], far_in.at[sec], ds.at[4 + sec], dr.at[4 + sec], ctx=far).start()

    def backward(i, _):
        owner_sec, owner, kb, sent, used = step_of(i)

        @pl.when(used)
        def _():
            KT[...] = K[kb].astype(F32).T.astype(BF)
            dka[...] = jnp.zeros(dka.shape, F32)
            dva[...] = jnp.zeros(dva.shape, F32)

        def section(sec, _):
            qb = jnp.where(sec == 0, c, 7 - c)

            @pl.when(used & (kb < qb))
            def _():
                attend_back(sec, kb, False)

            @pl.when(used & (kb == qb))
            def _():
                attend_back(sec, kb, True)

            return 0

        lax.fori_loop(0, 2, section, 0)

        @pl.when(used)
        def _():
            dk = (dka[...] * LN2).astype(BF)
            dv = dva[...].astype(BF)
            x = X[kb]
            dwk[...] += dot(x, dk, 0, 0)
            dwv[...] += dot(x, dv, 0, 0)
            sums[1:2, :] += dot(ones, dv)[0:1]
            dx = dot(dk, Wk[...], 1, 1) + dot(dv, Wv[...], 1, 1)

            @pl.when(i < 2)
            def _():
                rel_out[owner_sec] = dx.astype(BF)
                to(rel_out.at[owner_sec], rel_in.at[owner_sec], ds.at[2 + owner_sec], dr.at[2 + owner_sec], ctx=sib).start()

            @pl.when((i == 2) | (i == 3))
            def _():
                far_out[owner_sec] = dx.astype(BF)

            @pl.when((i == 4) | (i == 5))
            def _():
                sib_out[owner_sec] = dx.astype(BF)
                to(sib_out.at[owner_sec], sib_in.at[owner_sec], ds.at[owner_sec], dr.at[owner_sec], ctx=sib).start()

            @pl.when(i >= 6)
            def _():
                dR[owner_sec] += dx

        @pl.when(i == 3)
        def _():
            relay(0)
            pl.when(chip == 0)(functools.partial(relay, 1))

        if ring:
            pl.when(i == 1)(functools.partial(reduce_y, 0))
            pl.when(i == 3)(functools.partial(reduce_z, 0))
            pl.when(i == 5)(functools.partial(reduce_x, 0))
            pl.when(i == 6)(functools.partial(reduce_last, 0))
        return 0

    lax.fori_loop(0, 8, backward, 0)

    def d_query(sec, _):
        dq = jnp.concatenate([acc[sec, h, 0:64, :] for h in range(HEADS)], axis=0)
        Q[sec] = (dq * SCALE).T.astype(BF)
        sums[0:1, :] += dot(ones, Q[sec])[0:1]
        return 0

    lax.fori_loop(0, 2, d_query, 0)
    xx = jnp.concatenate([X[c], X[7 - c]], axis=0)
    by_owner(P2, dot(xx, both(Q), 0, 0).astype(BF), 0)
    by_owner(P2, dwk[...].astype(BF), 32)
    by_owner(P2, dwv[...].astype(BF), 64)
    for s in range(SHARDS):
        row = jnp.concatenate(
            [sums[:, s * 64 : s * 64 + 64], jnp.zeros((8, 448), F32)], axis=1
        )
        P2[0, s % 2, s // 2, 96:112, :] = jnp.concatenate(
            [row, jnp.zeros((8, 512), F32)], axis=0
        ).astype(BF)
        row = jnp.concatenate(
            [sums_inner[:, s * 256 : s * 256 + 256], jnp.zeros((8, 256), F32)], axis=1
        )
        P2[1, s % 2, s // 2, 96:112, :] = jnp.concatenate(
            [row, jnp.zeros((8, 512), F32)], axis=0
        ).astype(BF)
    if ring:
        reduce_core(1)
        reduce_y(1)

    for sec in range(2):
        dx = dR[sec] + dot(Q[sec], Wq[...], 1, 1)
        tg_v[sec] = dx.astype(BF)
        dR[sec] = dx

    def add_incoming(ref, sem, sec):
        arrived(ref.at[sec], sem)
        dR[sec] += ref[sec].astype(F32)

    add_incoming(sib_in, dr.at[0], 0)
    pl.when(core == 1)(lambda: add_incoming(sib_in, dr.at[1], 1))
    add_incoming(far_in, dr.at[4], 0)
    pl.when(chip == 1)(lambda: add_incoming(far_in, dr.at[5], 1))
    for sec in range(2):
        tg_v[sec] = dR[sec].astype(BF)
    tg_copy = pltpu.make_async_copy(tg_v, tg_ref, out_sem.at[1])
    tg_copy.start()

    if ring:
        reduce_z(1)
        arrived(FIN1.at[1 - core], gr.at[0, 7])
        gq, gk, gv, go, gi, gu = grads_out
        for half in range(2):
            go[half * 32 : half * 32 + 32, :] = FIN1[half, 0:32, :].astype(F32)
            gu[half * 128 : half * 128 + 128, :] = FIN1[half, 32:160, :].astype(F32)
            for cb in range(4):
                gi[half * 32 : half * 32 + 32, cb * 512 : cb * 512 + 512] = FIN1[
                    half, 160 + cb * 32 : 192 + cb * 32, :
                ].astype(F32)
        reduce_x(1)
        reduce_last(1)
        for w in range(6):
            gather_left(w)
        for i in range(7):
            left(small_all.at[0], ms.at[i])
        reduce_left(0)
        arrived(FIN2.at[1 - core], gr.at[1, 7])
        for half in range(2):
            for ref, row in ((gq, 0), (gk, 32), (gv, 64)):
                ref[half * 32 : half * 32 + 32, :] = FIN2[half, row : row + 32, :].astype(F32)
        gsm_ref[0:8, :] = FIN2[0, 96:112, 0:128].astype(F32)[0:8]
        gsm_ref[8:9, :] = FIN2[1, 96:112, 0:128].astype(F32)[0:1]
        gsm_ref[9:10, :] = FIN2[1, 96:112, 128:256].astype(F32)[0:1]
        reduce_left(1)
    else:
        copies = [
            pltpu.make_async_copy(P1, p1_out, load_sem.at[0]),
            pltpu.make_async_copy(P2, p2_out, load_sem.at[1]),
        ]
        for copy in copies:
            copy.start()
        for copy in copies:
            copy.wait()

    block = X.at[0]
    for k in range(3):
        left(block, xs.at[k])
    pl.when(chip == 1)(lambda: left(block, xs.at[3]))
    left(block, xs.at[4])
    pl.when(chip == 0)(lambda: left(block, xs.at[5]))
    left(block, ds.at[0])
    pl.when(core == 0)(lambda: left(block, ds.at[1]))
    left(block, ds.at[2])
    pl.when(chip == 0)(lambda: left(block, ds.at[3]))
    left(block, ds.at[4])
    pl.when(chip == 0)(lambda: left(block, ds.at[5]))
    out_copy.wait()
    tg_copy.wait()


def run(ring, tokens, cotangent, weights, smalls):
    blk = tokens.shape[1]
    vm = lambda *shape: pltpu.VMEM(shape, BF)
    vf = lambda *shape: pltpu.VMEM(shape, F32)
    dma = lambda *shape: pltpu.SemaphoreType.DMA(shape)
    any_spec = pl.BlockSpec(memory_space=pl.ANY)
    vmem_spec = pl.BlockSpec(memory_space=pltpu.VMEM)
    outs = [jax.ShapeDtypeStruct(tokens.shape, BF)] * 2
    out_specs = [any_spec] * 2
    if ring:
        outs += [jax.ShapeDtypeStruct(w.shape, F32) for w in weights]
        outs += [jax.ShapeDtypeStruct((16, 128), F32)]
        out_specs += [vmem_spec] * 7
    else:
        outs += [
            jax.ShapeDtypeStruct((2, 2, 4, rows, D), BF) for rows in (G1_ROWS, G2_ROWS)
        ]
        out_specs += [any_spec] * 2
    scratch = [vm(8, blk, D)] * 3
    scratch += [vm(D, D)] * 4 + [vm(D, FF), vm(FF, D)]
    scratch += [vf(8, D), vf(1, FF)]
    scratch += [vm(2, blk, D), vm(2, HEADS, 128, blk)] * 2
    scratch += [vm(HEADS, 80, blk), vm(D, blk)]
    scratch += [vf(2, HEADS, 8, blk), vf(2, HEADS, 80, blk), vm(2, D, blk)]
    scratch += [vm(2, blk, D), vf(2, blk, D), vf(2, blk, 1)]
    scratch += [vm(2, blk, FF)] * 2 + [vm(2, blk, D), vf(2, blk, D), vm(2, blk, D)]
    scratch += [vf(D, D)] * 2
    scratch += [vf(8, D), vf(8, FF)]
    scratch += [vm(2, blk, D)]
    scratch += [vm(2, 2, 4, G1_ROWS, D), vm(2, 2, 4, G2_ROWS, D)]
    scratch += [vm(2, blk, D)] * 6
    scratch += [dma(12), dma(2), dma(6), dma(8)]
    scratch += [dma(6), dma(6)]
    if ring:
        scratch += [vf(SHARDS, 16, 128)]
        for rows in (G1_ROWS, G2_ROWS):
            scratch += [vm(2, 4, rows, D), vm(4, rows, D), vm(3, rows, D)]
            scratch += [vm(rows, D), vm(rows, D), vm(2, rows, D)]
        scratch += [dma(6, 3), dma(6, 4), dma(6, 7), dma(6, 8), dma(6, 8)]
        scratch += [dma(7), dma(8), dma(2, 8), dma(2, 8)]
    inputs = [tokens, cotangent, *weights, *smalls]
    return pl.pallas_call(
        functools.partial(layer, ring, blk),
        out_shape=outs,
        in_specs=[any_spec] * len(inputs),
        out_specs=out_specs,
        scratch_shapes=scratch,
        compiler_params=pltpu.CompilerParams(
            collective_id=0, has_side_effects=True, vmem_limit_bytes=63 << 20
        ),
        name="layer",
    )(*inputs)


def shards(tokens, *rest):
    (wq, bq, wk, wv, bv, wo, bo, g1, s1, wi, bi, wu, bu, g2, s2, cotangent) = rest
    blk = tokens.shape[3]
    tok = tokens.reshape(2, blk, D)
    cot = cotangent.reshape(2, blk, D)
    weights = (wq, wk, wv, wo, wi, wu)
    vectors = (bq, bv, bo, g1, s1, bu, g2, s2)
    ring = lax.axis_size("fsdp") == SHARDS
    if ring:
        stacked = jnp.stack([v.astype(F32) for v in vectors])
        stacked = jnp.pad(stacked, ((0, 0), (0, 64)))
        inner = jnp.pad(bi.astype(F32).reshape(2, 128), ((0, 6), (0, 0)))
        small = jnp.concatenate([stacked, inner], axis=0)
        res = run(True, tok, cot, weights, (small,))
        output, tokens_grad, gq, gk, gv, go, gi, gu, gsm = res
        gvec = [gsm[j, 0:64] for j in range(8)]
        gbi = gsm[8:10].reshape(256)
    else:
        gather = lambda w: lax.all_gather(w, "fsdp", axis=0, tiled=True)
        full = [gather(w) for w in weights]
        vec = jnp.stack([gather(v).astype(F32) for v in vectors])
        inner = gather(bi).astype(F32).reshape(1, FF)
        output, tokens_grad, p1, p2 = run(False, tok, cot, full, (vec, inner))

        def whole(part, rows):
            return part.transpose(2, 1, 0, 3, 4).reshape(SHARDS * 2 * rows, D)

        parts = [
            whole(p2[:, :, :, 0:32], 32),
            whole(p2[:, :, :, 32:64], 32),
            whole(p2[:, :, :, 64:96], 32),
            whole(p1[:, :, :, 0:32], 32),
            p1[:, :, :, 160:288]
            .reshape(2, 2, 4, 4, 32, D)
            .transpose(2, 1, 0, 4, 3, 5)
            .reshape(D, FF),
            whole(p1[:, :, :, 32:160], 128),
        ]
        vecs = p2[0, :, :, 96:104, 0:64].transpose(2, 1, 0, 3).reshape(8, D)
        inner = p2[1, :, :, 96, 0:256].transpose(1, 0, 2).reshape(FF)
        parts += [vecs[j] for j in range(8)] + [inner]
        count = lax.axis_size("fsdp")
        packed = jnp.concatenate(
            [part.astype(F32).reshape(count, -1) for part in parts], axis=1
        ).reshape(-1)
        shares = lax.psum_scatter(packed, "fsdp", scatter_dimension=0, tiled=True)
        summed = lax.psum(shares.astype(BF), "ctx").astype(F32)
        pieces, at = [], 0
        for initial in weights + vectors + (bi,):
            pieces.append(summed[at : at + initial.size].reshape(initial.shape))
            at = at + initial.size
        gq, gk, gv, go, gi, gu = pieces[:6]
        gvec, gbi = pieces[6:14], pieces[14]
    order = (gq, gvec[0], gk, gv, gvec[1], go, gvec[2], gvec[3], gvec[4], gi, gbi, gu)
    order += (gvec[5], gvec[6], gvec[7])
    return (output.reshape(tokens.shape), tokens_grad.reshape(tokens.shape)) + order


def solution(mesh):
    row = P("fsdp", None)
    one = P("fsdp")
    act = P("fsdp", None, "ctx", None, None)
    params = (row, one, row, row, one, row, one, one, one, row, one, row, one, one, one)
    return jax.shard_map(
        shards,
        mesh=mesh,
        in_specs=(act,) + params + (act,),
        out_specs=(act, act) + params,
        check_vma=False,
    )
```

```python
import functools
import math

import jax
import jax.numpy as jnp
from jax import lax
from jax.experimental import pallas as pl
from jax.experimental.pallas import tpu as pltpu
from jax.sharding import PartitionSpec as P

HEADS = 8
HEAD = 64
D = 512
FF = 2048
CTX = 4
SHARDS = 8
EPS = 1e-5
BF = jnp.bfloat16
F32 = jnp.float32
QUERY_SCALE = math.log2(math.e) / math.sqrt(HEAD)
SCALE = 1.0 / math.sqrt(HEAD)
LN2 = math.log(2.0)
GROUP_ROWS = (128, 160, 112)


def dot(left, right, left_dim=1, right_dim=0):
    return lax.dot_general(
        left, right, (((left_dim,), (right_dim,)), ((), ())), preferred_element_type=F32
    )


def rows_mean(value):
    return jnp.mean(value, axis=-1, keepdims=True)


def layer(ring, blk, *refs):
    it = iter(refs)
    take = lambda count: [next(it) for _ in range(count)]
    tok, cot = take(2)
    weights_in = take(6)
    small_in = take(1 if ring else 2)
    out_ref, tg_ref = take(2)
    if ring:
        finals_out = take(3)
    else:
        pu_out, pi_out, pq_out = take(3)
    X, K, V = take(3)
    Wq, Wk, Wv, Wo, Wi, Wu = weights = take(6)
    vec, vec_inner = take(2)
    Q, QTa, dO, dOTa = take(4)
    VTa, KT = take(2)
    top, acc, OT = take(3)
    Hlow, n1, rstd1 = take(3)
    Z, dU, dF, dR, dA = take(5)
    dwk, dwv = take(2)
    dka, dva = n1.at[0], n1.at[1]
    sums, sums_inner = take(2)
    cot_v = next(it)
    tg_v = dO
    PU, PI, PQ = take(3)
    sib_out, sib_in, rel_out, rel_in, far_out, far_in = take(6)
    load_sem, out_sem, xs, xr = take(4)
    ds, dr = take(2)
    if ring:
        small_all = next(it)
        buffers = [take(6) for _ in range(3)]
        zs, ys, cs, rr, rc, ms, mr, gs, gr = take(9)

    t = lax.axis_index("ctx")
    chip, core = t // 2, lax.rem(t, 2)
    sib = t + 1 - 2 * core
    far = lax.rem(t + 2, 4)
    c = t
    MESH = pl.DeviceIdType.MESH

    def to(ref, dst, send, recv, **where):
        return pltpu.make_async_remote_copy(
            src_ref=ref,
            dst_ref=dst,
            send_sem=send,
            recv_sem=recv,
            device_id=where,
            device_id_type=MESH,
        )

    def arrived(ref, sem):
        pltpu.make_async_copy(ref, ref, sem).wait()

    def left(ref, sem):
        pltpu.make_async_copy(ref, ref, sem).wait()

    peers = [{"ctx": sib}, {"ctx": far}]
    if ring:
        f = lax.axis_index("fsdp")
        z, y = f // 2, lax.rem(f, 2)
        fy = f + 1 - 2 * y
        zpeer = [lax.rem(z + dz, 4) * 2 + y for dz in (1, 2, 3)]
        peers += [{"fsdp": fy}] + [{"fsdp": zp} for zp in zpeer]

    own_blocks = [c, 7 - c]
    loads = []
    for sec in range(2):
        loads.append(
            pltpu.make_async_copy(tok.at[sec], X.at[own_blocks[sec]], load_sem.at[sec])
        )
        loads.append(
            pltpu.make_async_copy(cot.at[sec], cot_v.at[sec], load_sem.at[2 + sec])
        )
    for w in range(6):
        rows = weights_in[w].shape[0]
        dst = weights[w].at[pl.ds(f * rows, rows)] if ring else weights[w]
        loads.append(pltpu.make_async_copy(weights_in[w], dst, load_sem.at[4 + w]))
    if ring:
        loads.append(
            pltpu.make_async_copy(small_in[0], small_all.at[f], load_sem.at[10])
        )
    else:
        loads.append(pltpu.make_async_copy(small_in[0], vec, load_sem.at[10]))
        loads.append(pltpu.make_async_copy(small_in[1], vec_inner, load_sem.at[11]))
    for copy in loads:
        copy.start()

    barrier = pltpu.get_barrier_semaphore()
    for where in peers:
        pl.semaphore_signal(barrier, inc=1, device_id=where, device_id_type=MESH)
    pl.semaphore_wait(barrier, len(peers))

    for sec in range(2):
        b = own_blocks[sec]
        to(tok.at[sec], X.at[b], xs.at[sec], xr.at[b], ctx=sib).start()
    to(tok.at[0], X.at[c], xs.at[2], xr.at[c], ctx=far).start()

    @pl.when(chip == 1)
    def _():
        to(tok.at[1], X.at[7 - c], xs.at[3], xr.at[7 - c], ctx=far).start()

    if ring:
        def piece(w, s, half):
            rows = weights_in[w].shape[0]
            return weights[w].at[pl.ds(s * rows + half * (rows // 2), rows // 2)]

        def gather_start(w):
            rows = weights_in[w].shape[0]
            src = weights_in[w].at[pl.ds(core * (rows // 2), rows // 2)]
            for i in range(3):
                to(src, piece(w, f, core), zs.at[w, i], rr.at[w, f], fsdp=zpeer[i]).start()
            to(src, piece(w, f, core), ys.at[w, 0], rr.at[w, f], fsdp=fy).start()

        def gather_z(w):
            for i in range(3):
                s = zpeer[i]
                ref = piece(w, s, core)
                arrived(ref, rr.at[w, s])
                to(ref, ref, ys.at[w, 1 + i], rr.at[w, s], fsdp=fy).start()
                to(ref, ref, cs.at[w, i], rc.at[w, s], ctx=sib).start()

        def gather_y(w):
            for i in range(4):
                s = lax.rem(z + i, 4) * 2 + 1 - y
                ref = piece(w, s, core)
                arrived(ref, rr.at[w, s])
                to(ref, ref, cs.at[w, 3 + i], rc.at[w, s], ctx=sib).start()

        def gather_end(w):
            for i in range(1, 8):
                s = lax.rem(f + i, 8)
                arrived(piece(w, s, 1 - core), rc.at[w, s])
            loads[4 + w].wait()

        def gather_left(w):
            rows = weights_in[w].shape[0]
            ref = weights[w].at[pl.ds(0, rows // 2)]
            for i in range(3):
                left(ref, zs.at[w, i])
            for i in range(4):
                left(ref, ys.at[w, i])
            for i in range(7):
                left(ref, cs.at[w, i])

        for i in range(3):
            to(small_in[0], small_all.at[f], ms.at[i], mr.at[f], fsdp=zpeer[i]).start()
        to(small_in[0], small_all.at[f], ms.at[3], mr.at[f], fsdp=fy).start()
        for w in range(3):
            gather_start(w)
        for i in range(3):
            s = zpeer[i]
            arrived(small_all.at[s], mr.at[s])
            to(small_all.at[s], small_all.at[s], ms.at[4 + i], mr.at[s], fsdp=fy).start()
        for w in range(3):
            gather_z(w)
        for w in range(3, 6):
            gather_start(w)
    else:
        for w in range(6):
            loads[4 + w].wait()

    def far_tokens():
        b = far
        arrived(X.at[b], xr.at[b])
        to(X.at[b], X.at[b], xs.at[4], xr.at[b], ctx=sib).start()

        @pl.when(chip == 0)
        def _():
            b = 7 - far
            arrived(X.at[b], xr.at[b])
            to(X.at[b], X.at[b], xs.at[5], xr.at[b], ctx=sib).start()

    if ring:
        for w in range(3):
            gather_y(w)
        for i in range(4):
            s = lax.rem(z + i, 4) * 2 + 1 - y
            arrived(small_all.at[s], mr.at[s])
        loads[10].wait()
        vec[...] = jnp.concatenate(
            [small_all[s][0:8, 0:64] for s in range(SHARDS)], axis=1
        )
        vec_inner[...] = jnp.concatenate(
            [small_all[s][8 + k : 9 + k] for s in range(SHARDS) for k in range(2)],
            axis=1,
        )
        for w in range(3):
            gather_end(w)
    else:
        loads[10].wait()
        loads[11].wait()
    b_query, b_value, b_out, gain1, shift1, b_outer, gain2, shift2 = (
        vec[pl.ds(j, 1), :] for j in range(8)
    )
    for sec in range(2):
        loads[2 * sec].wait()

    VTa[:, 64:80, :] = jnp.ones((HEADS, 16, blk), BF)
    for h in range(HEADS):
        other = (1 - h % 2) * 64
        for sec in range(2):
            QTa[sec, h, other : other + 64, :] = jnp.zeros((64, blk), BF)
            dOTa[sec, h, other : other + 64, :] = jnp.zeros((64, blk), BF)

    def queries(sec, _):
        x = X[jnp.where(sec == 0, c, 7 - c)]
        q = (dot(x, Wq[...]) + b_query) * QUERY_SCALE
        Q[sec] = q.astype(BF)
        qt = q.T.astype(BF)
        for h in range(HEADS):
            own = (h % 2) * 64
            QTa[sec, h, own : own + 64, :] = qt[h * 64 : h * 64 + 64]
        return 0

    lax.fori_loop(0, 2, queries, 0)

    lane = lax.broadcasted_iota(jnp.int32, (blk, 128), 1)
    key_at = lax.broadcasted_iota(jnp.int32, (blk, blk), 0)
    query_at = lax.broadcasted_iota(jnp.int32, (blk, blk), 1)

    def step_of(i):
        sec = lax.rem(i, 2)
        owner_core = jnp.where(i < 2, 1 - core, core)
        owner = jnp.where(i < 4, 2 * (1 - chip) + owner_core, jnp.where(i < 6, sib, t))
        kb = jnp.where(sec == 0, owner, 7 - owner)
        sent = (i >= 4) | (chip == 0) | (sec == 0)
        return sec, owner, kb, sent, sent & (kb <= 7 - c)

    top[...] = jnp.full(top.shape, -1e30, F32)
    acc[...] = jnp.zeros(acc.shape, F32)

    def attend(sec, kb, diagonal):
        def scores(h):
            p, a = h // 2, h % 2
            k_pair = K[kb, :, p * 128 : p * 128 + 128]
            k_head = jnp.where((lane < 64) == (a == 0), k_pair, jnp.zeros_like(k_pair))
            s = dot(k_head, QTa[sec, h])
            if diagonal:
                s = jnp.where(key_at <= query_at, s, -1e30)
            return s

        def weigh(h, s):
            old = top[sec, h, 0:1, :]
            new = jnp.maximum(old, jnp.max(s, axis=0, keepdims=True))
            top[sec, h] = jnp.broadcast_to(new, (8, blk))
            return jnp.exp2(s - new).astype(BF), jnp.exp2(old - new)

        def gather_values(h, probs, shrink):
            acc[sec, h] = acc[sec, h] * shrink + dot(VTa[h], probs)

        s = scores(0)
        held = None
        for h in range(HEADS):
            later = scores(h + 1) if h + 1 < HEADS else None
            now = (h, *weigh(h, s))
            if held is not None:
                gather_values(*held)
            held, s = now, later
        gather_values(*held)

    def keys_values(kb):
        x = X[kb]
        K[kb] = dot(x, Wk[...]).astype(BF)
        v = dot(x, Wv[...]) + b_value
        V[kb] = v.astype(BF)
        vt = v.T.astype(BF)
        for h in range(HEADS):
            VTa[h, 0:64, :] = vt[h * 64 : h * 64 + 64]

    def forward(n, _):
        i = jnp.where(n < 2, 6 + n, jnp.where(n < 4, 2 + n, jnp.where(n < 6, n - 2, n - 6)))
        _, _, kb, sent, used = step_of(i)

        @pl.when(n == 4)
        def _():
            far_tokens()

        if ring:
            for when, w in ((1, 3), (2, 4), (3, 5)):
                pl.when(n == when)(functools.partial(gather_z, w))
            for when, w in ((4, 3), (5, 4), (6, 5)):
                pl.when(n == when)(functools.partial(gather_y, w))

        @pl.when(sent & ((n == 2) | (n == 3) | (n >= 6)))
        def _():
            arrived(X.at[kb], xr.at[kb])

        @pl.when(used)
        def _():
            keys_values(kb)

        def section(sec, _):
            qb = jnp.where(sec == 0, c, 7 - c)

            @pl.when(used & (kb < qb))
            def _():
                attend(sec, kb, False)

            @pl.when(used & (kb == qb))
            def _():
                attend(sec, kb, True)

            return 0

        lax.fori_loop(0, 2, section, 0)
        return 0

    lax.fori_loop(0, 8, forward, 0)

    def finish(sec, _):
        for h in range(HEADS):
            other = (1 - h % 2) * 64
            total = acc[sec, h, 64:65, :]
            OT[sec, h * 64 : h * 64 + 64, :] = (acc[sec, h, 0:64, :] / total).astype(BF)
            low = -(top[sec, h, 0:1, :] + jnp.log2(total))
            parts = []
            for _ in range(3):
                parts.append(low.astype(BF))
                low = low - parts[-1].astype(F32)
            QTa[sec, h, other : other + 16, :] = jnp.concatenate(
                parts + [jnp.zeros((13, blk), BF)], axis=0
            )
        return 0

    lax.fori_loop(0, 2, finish, 0)
    if ring:
        for w in range(3, 6):
            gather_end(w)
    for sec in range(2):
        loads[2 * sec + 1].wait()

    sums[...] = jnp.zeros(sums.shape, F32)
    sums_inner[...] = jnp.zeros(sums_inner.shape, F32)
    ones = jnp.ones((16, blk), BF)

    def column_sum(value):
        return jnp.sum(value, axis=0, keepdims=True)

    def dense(sec, _):
        x = X[jnp.where(sec == 0, c, 7 - c)].astype(F32)
        r1 = x + dot(OT[sec], Wo[...], 0, 0) + b_out
        center = r1 - rows_mean(r1)
        rs1 = lax.rsqrt(rows_mean(center * center) + EPS)
        n1[sec] = center * rs1
        rstd1[sec] = rs1
        hid = center * rs1 * gain1 + shift1
        low = hid.astype(BF)
        Hlow[sec] = low
        c0 = math.sqrt(2.0 / math.pi)
        for cb in range(4):
            cols = slice(cb * 512, cb * 512 + 512)
            u = dot(Hlow[sec], Wi[:, cols]) + vec_inner[:, cols]
            uu = u * u
            th = jnp.tanh(c0 * u * (1.0 + 0.044715 * uu))
            half = 0.5 * (1.0 + th)
            Z[sec, :, cols] = (u * half).astype(BF)
            slope = half + 0.5 * u * (1.0 - th * th) * (c0 * (1.0 + 3 * 0.044715 * uu))
            dU[sec, :, cols] = slope.astype(BF)
        r2 = hid + dot(Z[sec], Wu[...]) + b_outer
        center = r2 - rows_mean(r2)
        rs2 = lax.rsqrt(rows_mean(center * center) + EPS)
        n2 = center * rs2
        g = cot_v[sec].astype(F32)
        cot_v[sec] = (n2 * gain2 + shift2).astype(BF)
        sums[6:7, :] += column_sum(g * n2)
        sums[7:8, :] += column_sum(g)
        g = g * gain2
        d_r2 = (g - rows_mean(g) - n2 * rows_mean(g * n2)) * rs2
        dR[sec] = d_r2
        d_f = d_r2.astype(BF)
        dF[sec] = d_f
        sums[5:6, :] += dot(ones, d_f)[0:1]
        for cb in range(4):
            cols = slice(cb * 512, cb * 512 + 512)
            d_u = (dot(dF[sec], Wu[cols, :], 1, 1) * dU[sec, :, cols].astype(F32)).astype(BF)
            dU[sec, :, cols] = d_u
            sums_inner[0:1, cols] += dot(ones, d_u)[0:1]
        d_h = dR[sec] + dot(dU[sec], Wi[...], 1, 1)
        nn1 = n1[sec]
        sums[3:4, :] += column_sum(d_h * nn1)
        sums[4:5, :] += column_sum(d_h)
        g = d_h * gain1
        d_r1 = (g - rows_mean(g) - nn1 * rows_mean(g * nn1)) * rstd1[sec]
        dR[sec] = d_r1
        d_a = d_r1.astype(BF)
        dA[sec] = d_a
        sums[2:3, :] += dot(ones, d_a)[0:1]
        dO[sec] = dot(dA[sec], Wo[...], 1, 1).astype(BF)
        d_ot = dot(Wo[...], dA[sec], 1, 1)
        for h in range(HEADS):
            own, other = (h % 2) * 64, (1 - h % 2) * 64
            part = d_ot[h * 64 : h * 64 + 64].astype(BF)
            dOTa[sec, h, own : own + 64, :] = part
            o = OT[sec, h * 64 : h * 64 + 64, :].astype(F32)
            rest = -column_sum(part.astype(F32) * o)
            parts = []
            for _ in range(3):
                parts.append(rest.astype(BF))
                rest = rest - parts[-1].astype(F32)
            dOTa[sec, h, other : other + 16, :] = jnp.concatenate(
                parts + [jnp.zeros((13, blk), BF)], axis=0
            )
        return 0

    lax.fori_loop(0, 2, dense, 0)
    out_copy = pltpu.make_async_copy(cot_v, out_ref, out_sem.at[0])
    out_copy.start()

    if ring:
        groups = [(mine, *more) for mine, more in zip((PU, PI, PQ), buffers)]

        finals = [
            pltpu.make_async_copy(groups[g][6], finals_out[g], load_sem.at[g]) for g in range(3)
        ]

        def add_into(dst, *terms):
            total = dst[...].astype(F32)
            for term in terms:
                total = total + term[...].astype(F32)
            dst[...] = total.astype(BF)

        def reduce_core(g):
            mine, from_core = groups[g][:2]
            for k, yy in ((0, 1 - y), (1, y)):
                to(mine.at[1 - core, yy], from_core.at[k], gs.at[g, k], gr.at[g, k], ctx=sib).start()

        def reduce_y(g):
            mine, from_core, from_y = groups[g][:3]
            arrived(from_core.at[0], gr.at[g, 0])

            def body(n, _):
                k = lax.rem(z + 1 + n, 4)
                add_into(mine.at[core, 1 - y, k], from_core.at[0, k])
                to(mine.at[core, 1 - y, k], from_y.at[k], gs.at[g, 2 + n], gr.at[g, 2 + n], fsdp=fy).start()
                return 0

            lax.fori_loop(0, 4, body, 0)

        def reduce_z(g):
            mine, from_core, from_y, from_z = groups[g][:4]
            arrived(from_core.at[1], gr.at[g, 1])

            def body(n, _):
                k = lax.rem(z + 1 + n, 4)
                arrived(from_y.at[k], gr.at[g, 2 + n])
                add_into(mine.at[core, y, k], from_core.at[1, k], from_y.at[k])

                @pl.when(n < 3)
                def _():
                    to(mine.at[core, y, k], from_z.at[n], gs.at[g, 6 + n], gr.at[g, 6 + n], fsdp=k * 2 + y).start()

                return 0

            lax.fori_loop(0, 4, body, 0)

        def reduce_x(g):
            mine, _, _, from_z, pair, from_x, _ = groups[g]
            for i in range(3):
                arrived(from_z.at[i], gr.at[g, 6 + i])
            pair[...] = (
                mine[core, y, z].astype(F32)
                + from_z[0].astype(F32)
                + from_z[1].astype(F32)
                + from_z[2].astype(F32)
            ).astype(BF)
            to(pair, from_x, gs.at[g, 9], gr.at[g, 9], ctx=far).start()

        def reduce_last(g):
            pair, from_x, final = groups[g][4:]
            arrived(from_x, gr.at[g, 9])
            final[core] = (pair[...].astype(F32) + from_x[...].astype(F32)).astype(BF)
            to(final.at[core], final.at[core], gs.at[g, 10], gr.at[g, 10], ctx=sib).start()

        def reduce_end(g):
            mine, from_core, from_y, from_z, pair, from_x, final = groups[g]
            arrived(final.at[1 - core], gr.at[g, 10])
            for k in range(2):
                left(from_core.at[k], gs.at[g, k])
            for i in range(4):
                left(from_y.at[0], gs.at[g, 2 + i])
            for i in range(3):
                left(from_z.at[i], gs.at[g, 6 + i])
            left(pair, gs.at[g, 9])
            left(final.at[0], gs.at[g, 10])

    def both(ref, cols=slice(None)):
        return jnp.concatenate([ref[0, :, cols], ref[1, :, cols]], axis=0)

    for rb in range(4):
        part = dot(both(Z, slice(rb * 512, rb * 512 + 512)), both(dF), 0, 0).astype(BF)
        for k in range(4):
            s, half = 2 * rb + k // 2, k % 2
            PU[half, s % 2, s // 2] = part[k * 128 : k * 128 + 128]
    if ring:
        reduce_core(0)
    for cb in range(4):
        part = dot(both(Hlow), both(dU, slice(cb * 512, cb * 512 + 512)), 0, 0).astype(BF)
        for s in range(SHARDS):
            for half in range(2):
                at = s * 64 + half * 32
                PI[half, s % 2, s // 2, cb * 32 : cb * 32 + 32, :] = part[at : at + 32]

    def by_owner(dst, value, row):
        for s in range(SHARDS):
            for half in range(2):
                at = s * 64 + half * 32
                dst[half, s % 2, s // 2, row : row + 32, :] = value[at : at + 32]

    ot = jnp.concatenate([OT[0], OT[1]], axis=1)
    by_owner(PI, dot(ot, both(dA)).astype(BF), 128)

    if ring:
        reduce_core(1)
        reduce_y(0)

    acc[...] = jnp.zeros(acc.shape, F32)
    dwk[...] = jnp.zeros(dwk.shape, F32)
    dwv[...] = jnp.zeros(dwv.shape, F32)

    def attend_back(sec, kb, diagonal):
        def scores(h):
            p, a = h // 2, h % 2
            own = (lane < 64) == (a == 0)
            first = (1 - a) * 64
            one = jnp.where((lane >= first) & (lane < first + 3), 1.0, 0.0).astype(BF)
            cols = slice(p * 128, p * 128 + 128)
            s = dot(jnp.where(own, K[kb, :, cols], one), QTa[sec, h])
            if diagonal:
                s = jnp.where(key_at <= query_at, s, -1e30)
            return s, dot(jnp.where(own, V[kb, :, cols], one), dOTa[sec, h])

        def weigh(s, dp):
            probs = jnp.exp2(s)
            return probs.astype(BF), (probs * dp).astype(BF)

        def to_queries(h, d_s):
            acc[sec, h, 0:64, :] += dot(KT[h * 64 : h * 64 + 64, :], d_s)

        def to_keys(p, first, second):
            cols = slice(p * 128, p * 128 + 128)
            q_pair, do_pair = Q[sec, :, cols], dO[sec, :, cols]
            zero = jnp.zeros_like(q_pair)
            low = lane < 64

            def stacked(pair):
                return jnp.concatenate(
                    [jnp.where(low, pair, zero), jnp.where(low, zero, pair)], axis=0
                )

            dva[:, cols] += dot(jnp.concatenate([first[0], second[0]], axis=1), stacked(do_pair))
            dka[:, cols] += dot(jnp.concatenate([first[1], second[1]], axis=1), stacked(q_pair))

        now = scores(0)
        done = []
        for n in range(HEADS + 1):
            later = scores(n + 1) if n + 1 < HEADS else None
            if n < HEADS:
                done.append(weigh(*now))
            if n > 0:
                to_queries(n - 1, done[n - 1][1])
                if n % 2 == 0:
                    to_keys(n // 2 - 1, done[n - 2], done[n - 1])
            now = later

    def relay(sec):
        arrived(rel_in.at[sec], dr.at[2 + sec])
        far_out[sec] = (far_out[sec].astype(F32) + rel_in[sec].astype(F32)).astype(BF)
        to(far_out.at[sec], far_in.at[sec], ds.at[4 + sec], dr.at[4 + sec], ctx=far).start()

    def backward(i, _):
        owner_sec, owner, kb, sent, used = step_of(i)

        @pl.when(used)
        def _():
            KT[...] = K[kb].astype(F32).T.astype(BF)
            dka[...] = jnp.zeros(dka.shape, F32)
            dva[...] = jnp.zeros(dva.shape, F32)

        def section(sec, _):
            qb = jnp.where(sec == 0, c, 7 - c)

            @pl.when(used & (kb < qb))
            def _():
                attend_back(sec, kb, False)

            @pl.when(used & (kb == qb))
            def _():
                attend_back(sec, kb, True)

            return 0

        lax.fori_loop(0, 2, section, 0)

        @pl.when(used)
        def _():
            dk = (dka[...] * LN2).astype(BF)
            dv = dva[...].astype(BF)
            x = X[kb]
            dwk[...] += dot(x, dk, 0, 0)
            dwv[...] += dot(x, dv, 0, 0)
            sums[1:2, :] += dot(ones, dv)[0:1]
            dx = dot(dk, Wk[...], 1, 1) + dot(dv, Wv[...], 1, 1)

            @pl.when(i < 2)
            def _():
                rel_out[owner_sec] = dx.astype(BF)
                to(rel_out.at[owner_sec], rel_in.at[owner_sec], ds.at[2 + owner_sec], dr.at[2 + owner_sec], ctx=sib).start()

            @pl.when((i == 2) | (i == 3))
            def _():
                far_out[owner_sec] = dx.astype(BF)

            @pl.when((i == 4) | (i == 5))
            def _():
                sib_out[owner_sec] = dx.astype(BF)
                to(sib_out.at[owner_sec], sib_in.at[owner_sec], ds.at[owner_sec], dr.at[owner_sec], ctx=sib).start()

            @pl.when(i >= 6)
            def _():
                dR[owner_sec] += dx

        @pl.when(i == 3)
        def _():
            relay(0)
            pl.when(chip == 0)(functools.partial(relay, 1))

        if ring:
            pl.when(i == 0)(functools.partial(reduce_y, 1))
            pl.when(i == 2)(functools.partial(reduce_z, 0))
            pl.when(i == 5)(functools.partial(reduce_z, 1))
            pl.when(i == 6)(functools.partial(reduce_x, 0))
        return 0

    lax.fori_loop(0, 8, backward, 0)

    def d_query(sec, _):
        dq = jnp.concatenate([acc[sec, h, 0:64, :] for h in range(HEADS)], axis=0)
        Q[sec] = (dq * SCALE).T.astype(BF)
        sums[0:1, :] += dot(ones, Q[sec])[0:1]
        return 0

    lax.fori_loop(0, 2, d_query, 0)
    xx = jnp.concatenate([X[c], X[7 - c]], axis=0)
    by_owner(PQ, dot(xx, both(Q), 0, 0).astype(BF), 0)
    by_owner(PQ, dwk[...].astype(BF), 32)
    by_owner(PQ, dwv[...].astype(BF), 64)
    for s in range(SHARDS):
        row = jnp.concatenate(
            [sums[:, s * 64 : s * 64 + 64], jnp.zeros((8, 448), F32)], axis=1
        )
        PQ[0, s % 2, s // 2, 96:112, :] = jnp.concatenate(
            [row, jnp.zeros((8, 512), F32)], axis=0
        ).astype(BF)
        row = jnp.concatenate(
            [sums_inner[:, s * 256 : s * 256 + 256], jnp.zeros((8, 256), F32)], axis=1
        )
        PQ[1, s % 2, s // 2, 96:112, :] = jnp.concatenate(
            [row, jnp.zeros((8, 512), F32)], axis=0
        ).astype(BF)
    if ring:
        reduce_core(2)
        reduce_x(1)
        reduce_last(0)
        reduce_y(2)

    for sec in range(2):
        dx = dR[sec] + dot(Q[sec], Wq[...], 1, 1)
        tg_v[sec] = dx.astype(BF)
        dR[sec] = dx

    def add_incoming(ref, sem, sec):
        arrived(ref.at[sec], sem)
        dR[sec] += ref[sec].astype(F32)

    add_incoming(sib_in, dr.at[0], 0)
    pl.when(core == 1)(lambda: add_incoming(sib_in, dr.at[1], 1))
    add_incoming(far_in, dr.at[4], 0)
    pl.when(chip == 1)(lambda: add_incoming(far_in, dr.at[5], 1))
    for sec in range(2):
        tg_v[sec] = dR[sec].astype(BF)
    tg_copy = pltpu.make_async_copy(tg_v, tg_ref, out_sem.at[1])
    tg_copy.start()

    if ring:
        reduce_last(1)
        reduce_z(2)
        for w in range(6):
            gather_left(w)
        for i in range(7):
            left(small_all.at[0], ms.at[i])
        for g in range(2):
            reduce_end(g)
            finals[g].start()
        reduce_x(2)
        reduce_last(2)
        reduce_end(2)
        finals[2].start()
        for g in range(3):
            finals[g].wait()
    else:
        copies = [
            pltpu.make_async_copy(part, out, load_sem.at[k])
            for k, (part, out) in enumerate(((PU, pu_out), (PI, pi_out), (PQ, pq_out)))
        ]
        for copy in copies:
            copy.start()
        for copy in copies:
            copy.wait()

    block = X.at[0]
    for k in range(3):
        left(block, xs.at[k])
    pl.when(chip == 1)(lambda: left(block, xs.at[3]))
    left(block, xs.at[4])
    pl.when(chip == 0)(lambda: left(block, xs.at[5]))
    left(block, ds.at[0])
    pl.when(core == 0)(lambda: left(block, ds.at[1]))
    left(block, ds.at[2])
    pl.when(chip == 0)(lambda: left(block, ds.at[3]))
    left(block, ds.at[4])
    pl.when(chip == 0)(lambda: left(block, ds.at[5]))
    out_copy.wait()
    tg_copy.wait()


def run(ring, tokens, cotangent, weights, smalls):
    blk = tokens.shape[1]
    vm = lambda *shape: pltpu.VMEM(shape, BF)
    vf = lambda *shape: pltpu.VMEM(shape, F32)
    dma = lambda *shape: pltpu.SemaphoreType.DMA(shape)
    any_spec = pl.BlockSpec(memory_space=pl.ANY)
    outs = [jax.ShapeDtypeStruct(tokens.shape, BF)] * 2
    out_specs = [any_spec] * 2
    if ring:
        outs += [jax.ShapeDtypeStruct((2, rows, D), BF) for rows in GROUP_ROWS]
        out_specs += [any_spec] * 3
    else:
        outs += [
            jax.ShapeDtypeStruct((2, 2, 4, rows, D), BF) for rows in GROUP_ROWS
        ]
        out_specs += [any_spec] * 3
    scratch = [vm(8, blk, D)] * 3
    scratch += [vm(D, D)] * 4 + [vm(D, FF), vm(FF, D)]
    scratch += [vf(8, D), vf(1, FF)]
    scratch += [vm(2, blk, D), vm(2, HEADS, 128, blk)] * 2
    scratch += [vm(HEADS, 80, blk), vm(D, blk)]
    scratch += [vf(2, HEADS, 8, blk), vf(2, HEADS, 80, blk), vm(2, D, blk)]
    scratch += [vm(2, blk, D), vf(2, blk, D), vf(2, blk, 1)]
    scratch += [vm(2, blk, FF)] * 2 + [vm(2, blk, D), vf(2, blk, D), vm(2, blk, D)]
    scratch += [vf(D, D)] * 2
    scratch += [vf(8, D), vf(8, FF)]
    scratch += [vm(2, blk, D)]
    scratch += [vm(2, 2, 4, rows, D) for rows in GROUP_ROWS]
    scratch += [vm(2, blk, D)] * 6
    scratch += [dma(12), dma(2), dma(6), dma(8)]
    scratch += [dma(6), dma(6)]
    if ring:
        scratch += [vf(SHARDS, 16, 128)]
        for rows in GROUP_ROWS:
            scratch += [vm(2, 4, rows, D), vm(4, rows, D), vm(3, rows, D)]
            scratch += [vm(rows, D), vm(rows, D), vm(2, rows, D)]
        scratch += [dma(6, 3), dma(6, 4), dma(6, 7), dma(6, 8), dma(6, 8)]
        scratch += [dma(7), dma(8), dma(3, 11), dma(3, 11)]
    inputs = [tokens, cotangent, *weights, *smalls]
    return pl.pallas_call(
        functools.partial(layer, ring, blk),
        out_shape=outs,
        in_specs=[any_spec] * len(inputs),
        out_specs=out_specs,
        scratch_shapes=scratch,
        compiler_params=pltpu.CompilerParams(
            collective_id=0, has_side_effects=True, vmem_limit_bytes=63 << 20
        ),
        name="layer",
    )(*inputs)


def finish_kernel(out_in, tg_in, fu, fi, fq, *refs):
    out_ref, tg_ref, gq, gk, gv, go, gi, gu = refs[:8]
    vectors, inner = refs[8:16], refs[16]
    sems = refs[17]
    copies = [
        pltpu.make_async_copy(out_in, out_ref, sems.at[0]),
        pltpu.make_async_copy(tg_in, tg_ref, sems.at[1]),
    ]
    for copy in copies:
        copy.start()
    for half in range(2):
        rows = slice(half * 32, half * 32 + 32)
        gu[half * 128 : half * 128 + 128, :] = fu[half].astype(F32)
        for cb in range(4):
            gi[rows, cb * 512 : cb * 512 + 512] = fi[half, cb * 32 : cb * 32 + 32, :].astype(F32)
        go[rows, :] = fi[half, 128:160, :].astype(F32)
        gq[rows, :] = fq[half, 0:32, :].astype(F32)
        gk[rows, :] = fq[half, 32:64, :].astype(F32)
        gv[rows, :] = fq[half, 64:96, :].astype(F32)
    small = fq[0, 96:112, 0:128].astype(F32)
    for j in range(8):
        vectors[j][...] = small[j : j + 1, 0:64]
    inner[...] = fq[1, 96:112, 0:256].astype(F32)[0:1]
    for copy in copies:
        copy.wait()


def finish_all(tokens, weights, res):
    any_spec = pl.BlockSpec(memory_space=pl.ANY)
    vmem_spec = pl.BlockSpec(memory_space=pltpu.VMEM)
    outs = [jax.ShapeDtypeStruct(tokens.shape, BF)] * 2
    outs += [jax.ShapeDtypeStruct(w.shape, F32) for w in weights]
    outs += [jax.ShapeDtypeStruct((1, 64), F32)] * 8
    outs += [jax.ShapeDtypeStruct((1, 256), F32)]
    return pl.pallas_call(
        finish_kernel,
        out_shape=outs,
        in_specs=[vmem_spec] * 5,
        out_specs=[any_spec] * 2 + [vmem_spec] * 15,
        scratch_shapes=[pltpu.SemaphoreType.DMA((2,))],
        name="finish",
    )(*res)


def shards(tokens, *rest):
    (wq, bq, wk, wv, bv, wo, bo, g1, s1, wi, bi, wu, bu, g2, s2, cotangent) = rest
    blk = tokens.shape[3]
    tok = tokens.reshape(2, blk, D)
    cot = cotangent.reshape(2, blk, D)
    weights = (wq, wk, wv, wo, wi, wu)
    vectors = (bq, bv, bo, g1, s1, bu, g2, s2)
    ring = lax.axis_size("fsdp") == SHARDS
    if ring:
        stacked = jnp.stack([v.astype(F32) for v in vectors])
        stacked = jnp.pad(stacked, ((0, 0), (0, 64)))
        inner = jnp.pad(bi.astype(F32).reshape(2, 128), ((0, 6), (0, 0)))
        small = jnp.concatenate([stacked, inner], axis=0)
        res = run(True, tok, cot, weights, (small,))
        res = finish_all(tok, weights, res)
        output, tokens_grad, gq, gk, gv, go, gi, gu = res[:8]
        gvec = [v.reshape(64) for v in res[8:16]]
        gbi = res[16].reshape(256)
    else:
        gather = lambda w: lax.all_gather(w, "fsdp", axis=0, tiled=True)
        full = [gather(w) for w in weights]
        vec = jnp.stack([gather(v).astype(F32) for v in vectors])
        inner = gather(bi).astype(F32).reshape(1, FF)
        output, tokens_grad, pu, pi, pq = run(False, tok, cot, full, (vec, inner))

        def whole(part, rows):
            return part.transpose(2, 1, 0, 3, 4).reshape(SHARDS * 2 * rows, D)

        parts = [
            whole(pq[:, :, :, 0:32], 32),
            whole(pq[:, :, :, 32:64], 32),
            whole(pq[:, :, :, 64:96], 32),
            whole(pi[:, :, :, 128:160], 32),
            pi[:, :, :, 0:128]
            .reshape(2, 2, 4, 4, 32, D)
            .transpose(2, 1, 0, 4, 3, 5)
            .reshape(D, FF),
            whole(pu, 128),
        ]
        vecs = pq[0, :, :, 96:104, 0:64].transpose(2, 1, 0, 3).reshape(8, D)
        inner = pq[1, :, :, 96, 0:256].transpose(1, 0, 2).reshape(FF)
        parts += [vecs[j] for j in range(8)] + [inner]
        count = lax.axis_size("fsdp")
        packed = jnp.concatenate(
            [part.astype(F32).reshape(count, -1) for part in parts], axis=1
        ).reshape(-1)
        shares = lax.psum_scatter(packed, "fsdp", scatter_dimension=0, tiled=True)
        summed = lax.psum(shares.astype(BF), "ctx").astype(F32)
        pieces, at = [], 0
        for initial in weights + vectors + (bi,):
            pieces.append(summed[at : at + initial.size].reshape(initial.shape))
            at = at + initial.size
        gq, gk, gv, go, gi, gu = pieces[:6]
        gvec, gbi = pieces[6:14], pieces[14]
    order = (gq, gvec[0], gk, gv, gvec[1], go, gvec[2], gvec[3], gvec[4], gi, gbi, gu)
    order += (gvec[5], gvec[6], gvec[7])
    return (output.reshape(tokens.shape), tokens_grad.reshape(tokens.shape)) + order


def solution(mesh):
    row = P("fsdp", None)
    one = P("fsdp")
    act = P("fsdp", None, "ctx", None, None)
    params = (row, one, row, row, one, row, one, one, one, row, one, row, one, one, one)
    return jax.shard_map(
        shards,
        mesh=mesh,
        in_specs=(act,) + params + (act,),
        out_specs=(act, act) + params,
        check_vma=False,
    )
```

```python
import functools
import math

import jax
import jax.numpy as jnp
from jax import lax
from jax.experimental import pallas as pl
from jax.experimental.pallas import tpu as pltpu
from jax.sharding import PartitionSpec as P

HEADS = 8
HEAD = 64
D = 512
FF = 2048
CTX = 4
SHARDS = 8
EPS = 1e-5
BF = jnp.bfloat16
F32 = jnp.float32
QUERY_SCALE = math.log2(math.e) / math.sqrt(HEAD)
SCALE = 1.0 / math.sqrt(HEAD)
LN2 = math.log(2.0)
AT_QUERY, AT_KEY, AT_VALUE, AT_SMALL, AT_OUT, AT_INNER, AT_OUTER, PACKED = 0, 32, 64, 96, 112, 144, 272, 400
UNITS = ((0, 32), (32, 64), (64, 112), (112, 208), (208, 304), (304, 400))
GATHER_AT = (
    (0, 3, 1),
    (1, 4, 1),
    (2, 5, 1),
    (3, 3, 2),
    (4, 4, 2),
    (6, 5, 2),
    (7, 3, 3),
    (9, 4, 3),
    (11, 5, 3),
    (12, 3, 0),
    (15, 4, 0),
)
GROUP_ROWS = (128, 160, 64, 48)


def dot(left, right, left_dim=1, right_dim=0):
    return lax.dot_general(
        left, right, (((left_dim,), (right_dim,)), ((), ())), preferred_element_type=F32
    )


def rows_mean(value):
    return jnp.mean(value, axis=-1, keepdims=True)


def layer(ring, blk, *refs):
    it = iter(refs)
    take = lambda count: [next(it) for _ in range(count)]
    tok, cot = take(2)
    weights_in = take(7 if ring else 1)
    small_in = take(0 if ring else 2)
    out_ref, tg_ref = take(2)
    if ring:
        finals_out = take(4)
    else:
        pu_out, pi_out, pk_out, pq_out = take(4)
    X, K, V = take(3)
    W = next(it)
    vec, vec_inner = take(2)
    Q, QTa, dO, dOTa = take(4)
    VTa, KT = take(2)
    top, acc, OT = take(3)
    Hlow, n1, rstd1 = take(3)
    Z, dU, dF, dR, dA = take(5)
    dwk, dwv = take(2)
    dka, dva = n1.at[0], n1.at[1]
    sums, sums_inner = take(2)
    cot_v = next(it)
    tg_v = dO
    PU, PI, PK, PQ = take(4)
    sib_in, rel_in, far_in = take(3)
    sib_out, rel_out, far_out = dA, dF, Hlow
    load_sem, out_sem, xs, xr = take(4)
    ds, dr = take(2)
    if ring:
        buffers = [take(6) for _ in range(4)]
        zs, ys, cs, rz, ry, rc, gs, gr = take(8)

    t = lax.axis_index("ctx")
    chip, core = t // 2, lax.rem(t, 2)
    sib = t + 1 - 2 * core
    far = lax.rem(t + 2, 4)
    c = t
    MESH = pl.DeviceIdType.MESH

    def to(ref, dst, send, recv, **where):
        return pltpu.make_async_remote_copy(
            src_ref=ref,
            dst_ref=dst,
            send_sem=send,
            recv_sem=recv,
            device_id=where,
            device_id_type=MESH,
        )

    def arrived(ref, sem):
        pltpu.make_async_copy(ref, ref, sem).wait()

    def left(ref, sem):
        pltpu.make_async_copy(ref, ref, sem).wait()

    peers = [{"ctx": sib}, {"ctx": far}]
    if ring:
        f = lax.axis_index("fsdp")
        z, y = f // 2, lax.rem(f, 2)
        fy = f + 1 - 2 * y
        zpeer = [lax.rem(z + dz, 4) * 2 + y for dz in (1, 2, 3)]
        peers += [{"fsdp": fy}] + [{"fsdp": zp} for zp in zpeer]

    own_blocks = [c, 7 - c]
    loads = []
    for sec in range(2):
        loads.append(
            pltpu.make_async_copy(tok.at[sec], X.at[own_blocks[sec]], load_sem.at[sec])
        )
        loads.append(
            pltpu.make_async_copy(cot.at[sec], cot_v.at[sec], load_sem.at[2 + sec])
        )
    if ring:
        for w, at in enumerate((AT_QUERY, AT_KEY, AT_VALUE, AT_SMALL, AT_OUT, AT_OUTER)):
            src = weights_in[w].at[core]
            loads.append(
                pltpu.make_async_copy(
                    src, W.at[z, y, core, pl.ds(at, src.shape[0])], load_sem.at[4 + w]
                )
            )
        for cb in range(4):
            src = weights_in[6].at[core, :, pl.ds(cb * D, D)]
            loads.append(
                pltpu.make_async_copy(
                    src, W.at[z, y, core, pl.ds(AT_INNER + cb * 32, 32)], load_sem.at[10 + cb]
                )
            )
    else:
        loads.append(pltpu.make_async_copy(weights_in[0], W, load_sem.at[4]))
        loads.append(pltpu.make_async_copy(small_in[0], vec, load_sem.at[5]))
        loads.append(pltpu.make_async_copy(small_in[1], vec_inner, load_sem.at[6]))
    for copy in loads:
        copy.start()

    barrier = pltpu.get_barrier_semaphore()
    for where in peers:
        pl.semaphore_signal(barrier, inc=1, device_id=where, device_id_type=MESH)
    pl.semaphore_wait(barrier, len(peers))

    for sec in range(2):
        b = own_blocks[sec]
        to(tok.at[sec], X.at[b], xs.at[sec], xr.at[b], ctx=sib).start()
    to(tok.at[0], X.at[c], xs.at[2], xr.at[c], ctx=far).start()

    @pl.when(chip == 1)
    def _():
        to(tok.at[1], X.at[7 - c], xs.at[3], xr.at[7 - c], ctx=far).start()

    if ring:
        def piece(u, zz, yy, half):
            first, last = UNITS[u]
            return W.at[zz, yy, half, pl.ds(first, last - first)]

        def pieces(u, yy, half):
            first, last = UNITS[u]
            return W.at[:, yy, half, pl.ds(first, last - first)]

        def gather_start(u):
            ref = piece(u, z, y, core)
            to(ref, ref, ys.at[u, z], ry.at[u], fsdp=fy).start()
            pl.when(z < 3)(lambda: to(ref, ref, zs.at[u, 4], rz.at[u, z], fsdp=f + 2).start())
            pl.when(z > 0)(lambda: to(ref, ref, zs.at[u, 5], rz.at[u, z], fsdp=f - 2).start())

        def gather_z(u, hops):
            def pass_on(zz, more, onward):
                ref = piece(u, zz, y, core)
                arrived(ref, rz.at[u, zz])
                if hops < 3:
                    pl.when(more)(lambda: to(ref, ref, zs.at[u, zz], rz.at[u, zz], fsdp=onward).start())
                to(ref, ref, ys.at[u, zz], ry.at[u], fsdp=fy).start()

            pl.when(z - hops >= 0)(lambda: pass_on(z - hops, z < 3, f + 2))
            pl.when(z + hops <= 3)(lambda: pass_on(z + hops, z > 0, f - 2))
            if hops == 3:
                ref = pieces(u, y, core)
                to(ref, ref, cs.at[u, 0], rc.at[u, 0], ctx=sib).start()

        def gather_y(u):
            ref = pieces(u, 1 - y, core)
            arrived(ref, ry.at[u])
            to(ref, ref, cs.at[u, 1], rc.at[u, 1], ctx=sib).start()

        def gather_end(u):
            arrived(pieces(u, y, 1 - core), rc.at[u, 0])
            arrived(pieces(u, 1 - y, 1 - core), rc.at[u, 1])

        def gather_left(u):
            ref = piece(u, 0, 0, 0)
            pl.when(z < 3)(lambda: left(ref, zs.at[u, 4]))
            pl.when(z > 0)(lambda: left(ref, zs.at[u, 5]))
            for zz in range(4):
                onward = ((zz < z) & (z < 3)) | ((zz > z) & (z > 0))
                pl.when(onward)(lambda zz=zz: left(ref, zs.at[u, zz]))
                left(ref, ys.at[u, zz])
            for i in range(2):
                left(pieces(u, 0, 0), cs.at[u, i])

        for copy in loads[4:]:
            copy.wait()
        for u in range(3):
            gather_start(u)
        for hops in (1, 2, 3):
            for u in range(3):
                gather_z(u, hops)
        for u in range(3, 6):
            gather_start(u)
    else:
        for copy in loads[4:]:
            copy.wait()

    def far_tokens():
        b = far
        arrived(X.at[b], xr.at[b])
        to(X.at[b], X.at[b], xs.at[4], xr.at[b], ctx=sib).start()

        @pl.when(chip == 0)
        def _():
            b = 7 - far
            arrived(X.at[b], xr.at[b])
            to(X.at[b], X.at[b], xs.at[5], xr.at[b], ctx=sib).start()

    if ring:
        for u in range(3):
            gather_y(u)
        for u in range(3):
            gather_end(u)
        small = [[W[s // 2, s % 2, half, AT_SMALL:AT_OUT, :].astype(F32) for s in range(SHARDS)] for half in range(2)]
        vec[...] = jnp.concatenate([part[0:8, 0:64] for part in small[0]], axis=1)
        vec_inner[...] = jnp.concatenate([part[0:1, 0:256] for part in small[1]], axis=1)

    def weight(at, rows=32):
        return W[:, :, :, at : at + rows, :].reshape(SHARDS * 2 * rows, D)

    b_query, b_value, b_out, gain1, shift1, b_outer, gain2, shift2 = (
        vec[pl.ds(j, 1), :] for j in range(8)
    )
    for sec in range(2):
        loads[2 * sec].wait()

    VTa[:, 64:80, :] = jnp.ones((HEADS, 16, blk), BF)
    for h in range(HEADS):
        other = (1 - h % 2) * 64
        for sec in range(2):
            QTa[sec, h, other : other + 64, :] = jnp.zeros((64, blk), BF)
            dOTa[sec, h, other : other + 64, :] = jnp.zeros((64, blk), BF)

    def queries(sec, _):
        x = X[jnp.where(sec == 0, c, 7 - c)]
        q = (dot(x, weight(AT_QUERY)) + b_query) * QUERY_SCALE
        Q[sec] = q.astype(BF)
        qt = q.T.astype(BF)
        for h in range(HEADS):
            own = (h % 2) * 64
            QTa[sec, h, own : own + 64, :] = qt[h * 64 : h * 64 + 64]
        return 0

    lax.fori_loop(0, 2, queries, 0)

    lane = lax.broadcasted_iota(jnp.int32, (blk, 128), 1)
    key_at = lax.broadcasted_iota(jnp.int32, (blk, blk), 0)
    query_at = lax.broadcasted_iota(jnp.int32, (blk, blk), 1)

    def step_of(i):
        sec = lax.rem(i, 2)
        owner_core = jnp.where(i < 2, 1 - core, core)
        owner = jnp.where(i < 4, 2 * (1 - chip) + owner_core, jnp.where(i < 6, sib, t))
        kb = jnp.where(sec == 0, owner, 7 - owner)
        sent = (i >= 4) | (chip == 0) | (sec == 0)
        return sec, owner, kb, sent, sent & (kb <= 7 - c)

    top[...] = jnp.full(top.shape, -1e30, F32)
    acc[...] = jnp.zeros(acc.shape, F32)

    def attend(sec, kb, diagonal):
        def scores(h):
            p, a = h // 2, h % 2
            k_pair = K[kb, :, p * 128 : p * 128 + 128]
            k_head = jnp.where((lane < 64) == (a == 0), k_pair, jnp.zeros_like(k_pair))
            s = dot(k_head, QTa[sec, h])
            if diagonal:
                s = jnp.where(key_at <= query_at, s, -1e30)
            return s

        def weigh(h, s):
            old = top[sec, h, 0:1, :]
            new = jnp.maximum(old, jnp.max(s, axis=0, keepdims=True))
            top[sec, h] = jnp.broadcast_to(new, (8, blk))
            return jnp.exp2(s - new).astype(BF), jnp.exp2(old - new)

        def gather_values(h, probs, shrink):
            acc[sec, h] = acc[sec, h] * shrink + dot(VTa[h], probs)

        s = scores(0)
        held = None
        for h in range(HEADS):
            later = scores(h + 1) if h + 1 < HEADS else None
            now = (h, *weigh(h, s))
            if held is not None:
                gather_values(*held)
            held, s = now, later
        gather_values(*held)

    def keys_values(kb):
        x = X[kb]
        K[kb] = dot(x, weight(AT_KEY)).astype(BF)
        v = dot(x, weight(AT_VALUE)) + b_value
        V[kb] = v.astype(BF)
        vt = v.T.astype(BF)
        for h in range(HEADS):
            VTa[h, 0:64, :] = vt[h * 64 : h * 64 + 64]

    def forward(n, _):
        i = jnp.where(n < 2, 6 + n, jnp.where(n < 4, 2 + n, jnp.where(n < 6, n - 2, n - 6)))
        _, _, kb, sent, used = step_of(i)

        @pl.when(n == 4)
        def _():
            far_tokens()

        @pl.when(sent & ((n == 2) | (n == 3) | (n >= 6)))
        def _():
            arrived(X.at[kb], xr.at[kb])

        @pl.when(used)
        def _():
            keys_values(kb)

        def section(sec, _):
            qb = jnp.where(sec == 0, c, 7 - c)
            if ring:
                for at, u, hops in GATHER_AT:
                    if hops:
                        pl.when(2 * n + sec == at)(functools.partial(gather_z, u, hops))
                    else:
                        pl.when(2 * n + sec == at)(functools.partial(gather_y, u))

            @pl.when(used & (kb < qb))
            def _():
                attend(sec, kb, False)

            @pl.when(used & (kb == qb))
            def _():
                attend(sec, kb, True)

            return 0

        lax.fori_loop(0, 2, section, 0)
        return 0

    lax.fori_loop(0, 8, forward, 0)

    def finish(sec, _):
        for h in range(HEADS):
            other = (1 - h % 2) * 64
            total = acc[sec, h, 64:65, :]
            OT[sec, h * 64 : h * 64 + 64, :] = (acc[sec, h, 0:64, :] / total).astype(BF)
            low = -(top[sec, h, 0:1, :] + jnp.log2(total))
            parts = []
            for _ in range(3):
                parts.append(low.astype(BF))
                low = low - parts[-1].astype(F32)
            QTa[sec, h, other : other + 16, :] = jnp.concatenate(
                parts + [jnp.zeros((13, blk), BF)], axis=0
            )
        return 0

    if ring:
        gather_y(5)
    lax.fori_loop(0, 2, finish, 0)
    if ring:
        gather_end(3)
    for sec in range(2):
        loads[2 * sec + 1].wait()

    sums[...] = jnp.zeros(sums.shape, F32)
    sums_inner[...] = jnp.zeros(sums_inner.shape, F32)
    ones = jnp.ones((16, blk), BF)

    def column_sum(value):
        return jnp.sum(value, axis=0, keepdims=True)

    def dense(sec):
        x = X[own_blocks[sec]].astype(F32)
        r1 = x + dot(OT[sec], weight(AT_OUT), 0, 0) + b_out
        yield
        center = r1 - rows_mean(r1)
        rs1 = lax.rsqrt(rows_mean(center * center) + EPS)
        n1[sec] = center * rs1
        rstd1[sec] = rs1
        Hlow[sec] = (n1[sec] * gain1 + shift1).astype(BF)
        yield
        c0 = math.sqrt(2.0 / math.pi)
        columns = [slice(cb * 512, cb * 512 + 512) for cb in range(4)]

        def hidden(cb):
            if ring and sec == 0 and cb == 2:
                gather_end(4)
            return dot(Hlow[sec], weight(AT_INNER + 32 * cb)) + vec_inner[:, columns[cb]]

        u = hidden(0)
        for cb in range(4):
            later = hidden(cb + 1) if cb < 3 else None
            uu = u * u
            th = jnp.tanh(c0 * u * (1.0 + 0.044715 * uu))
            half = 0.5 * (1.0 + th)
            Z[sec, :, columns[cb]] = (u * half).astype(BF)
            slope = half + 0.5 * u * (1.0 - th * th) * (c0 * (1.0 + 3 * 0.044715 * uu))
            dU[sec, :, columns[cb]] = slope.astype(BF)
            u = later
        yield
        if ring and sec == 0:
            gather_end(5)
        r2 = n1[sec] * gain1 + shift1 + dot(Z[sec], weight(AT_OUTER, 128)) + b_outer
        yield
        center = r2 - rows_mean(r2)
        rs2 = lax.rsqrt(rows_mean(center * center) + EPS)
        n2 = center * rs2
        g = cot_v[sec].astype(F32)
        cot_v[sec] = (n2 * gain2 + shift2).astype(BF)
        sums[6:7, :] += column_sum(g * n2)
        sums[7:8, :] += column_sum(g)
        g = g * gain2
        d_r2 = (g - rows_mean(g) - n2 * rows_mean(g * n2)) * rs2
        dR[sec] = d_r2
        d_f = d_r2.astype(BF)
        dF[sec] = d_f
        sums[5:6, :] += dot(ones, d_f)[0:1]
        yield

        def d_active(cb):
            rows = W[cb, :, :, AT_OUTER:PACKED, :].reshape(D, D)
            return dot(dF[sec], rows, 1, 1)

        now = d_active(0)
        for cb in range(4):
            later = d_active(cb + 1) if cb < 3 else None
            d_u = (now * dU[sec, :, columns[cb]].astype(F32)).astype(BF)
            dU[sec, :, columns[cb]] = d_u
            sums_inner[0:1, columns[cb]] += dot(ones, d_u)[0:1]
            now = later
        yield
        inner = jnp.concatenate([weight(AT_INNER + 32 * cb) for cb in range(4)], axis=1)
        d_h = dR[sec] + dot(dU[sec], inner, 1, 1)
        yield
        nn1 = n1[sec]
        sums[3:4, :] += column_sum(d_h * nn1)
        sums[4:5, :] += column_sum(d_h)
        g = d_h * gain1
        d_r1 = (g - rows_mean(g) - nn1 * rows_mean(g * nn1)) * rstd1[sec]
        dR[sec] = d_r1
        d_a = d_r1.astype(BF)
        dA[sec] = d_a
        sums[2:3, :] += dot(ones, d_a)[0:1]
        yield
        dO[sec] = dot(dA[sec], weight(AT_OUT), 1, 1).astype(BF)
        d_ot = dot(weight(AT_OUT), dA[sec], 1, 1)
        yield
        for h in range(HEADS):
            own, other = (h % 2) * 64, (1 - h % 2) * 64
            part = d_ot[h * 64 : h * 64 + 64].astype(BF)
            dOTa[sec, h, own : own + 64, :] = part
            o = OT[sec, h * 64 : h * 64 + 64, :].astype(F32)
            rest = -column_sum(part.astype(F32) * o)
            parts = []
            for _ in range(3):
                parts.append(rest.astype(BF))
                rest = rest - parts[-1].astype(F32)
            dOTa[sec, h, other : other + 16, :] = jnp.concatenate(
                parts + [jnp.zeros((13, blk), BF)], axis=0
            )

    running = [dense(0), dense(1)]
    if not ring:
        list(running.pop(0))
    while running:
        running = [work for work in running if next(work, 0) is None]
    out_copy = pltpu.make_async_copy(cot_v, out_ref, out_sem.at[0])
    out_copy.start()

    if ring:
        groups = [(mine, *more) for mine, more in zip((PU, PI, PK, PQ), buffers)]

        finals = [
            pltpu.make_async_copy(groups[g][6], finals_out[g], load_sem.at[g]) for g in range(4)
        ]

        def add_into(dst, *terms):
            total = dst[...].astype(F32)
            for term in terms:
                total = total + term[...].astype(F32)
            dst[...] = total.astype(BF)

        def reduce_core(g):
            mine, from_core = groups[g][:2]
            for k, yy in ((0, 1 - y), (1, y)):
                to(mine.at[1 - core, yy], from_core.at[k], gs.at[g, k], gr.at[g, k], ctx=sib).start()

        def reduce_y(g):
            mine, from_core, from_y = groups[g][:3]
            arrived(from_core.at[0], gr.at[g, 0])

            def body(n, _):
                k = lax.rem(z + 1 + n, 4)
                add_into(mine.at[core, 1 - y, k], from_core.at[0, k])
                to(mine.at[core, 1 - y, k], from_y.at[k], gs.at[g, 2 + n], gr.at[g, 2 + n], fsdp=fy).start()
                return 0

            lax.fori_loop(0, 4, body, 0)

        def reduce_z(g, first=0, last=4):
            mine, from_core, from_y, from_z = groups[g][:4]
            if first == 0:
                arrived(from_core.at[1], gr.at[g, 1])

            def body(n, _):
                k = lax.rem(z + 1 + n, 4)
                arrived(from_y.at[k], gr.at[g, 2 + n])
                add_into(mine.at[core, y, k], from_core.at[1, k], from_y.at[k])

                @pl.when(n < 3)
                def _():
                    to(mine.at[core, y, k], from_z.at[n], gs.at[g, 6 + n], gr.at[g, 6 + n], fsdp=k * 2 + y).start()

                return 0

            lax.fori_loop(first, last, body, 0)

        def reduce_x(g):
            mine, _, _, from_z, pair, from_x, _ = groups[g]
            for i in range(3):
                arrived(from_z.at[i], gr.at[g, 6 + i])
            pair[...] = (
                mine[core, y, z].astype(F32)
                + from_z[0].astype(F32)
                + from_z[1].astype(F32)
                + from_z[2].astype(F32)
            ).astype(BF)
            to(pair, from_x, gs.at[g, 9], gr.at[g, 9], ctx=far).start()

        def reduce_last(g):
            pair, from_x, final = groups[g][4:]
            arrived(from_x, gr.at[g, 9])
            final[core] = (pair[...].astype(F32) + from_x[...].astype(F32)).astype(BF)
            to(final.at[core], final.at[core], gs.at[g, 10], gr.at[g, 10], ctx=sib).start()

        def reduce_end(g):
            mine, from_core, from_y, from_z, pair, from_x, final = groups[g]
            arrived(final.at[1 - core], gr.at[g, 10])
            for k in range(2):
                left(from_core.at[k], gs.at[g, k])
            for i in range(4):
                left(from_y.at[0], gs.at[g, 2 + i])
            for i in range(3):
                left(from_z.at[i], gs.at[g, 6 + i])
            left(pair, gs.at[g, 9])
            left(final.at[0], gs.at[g, 10])

    def both(ref, cols=slice(None)):
        return jnp.concatenate([ref[0, :, cols], ref[1, :, cols]], axis=0)

    for rb in range(4):
        part = dot(both(Z, slice(rb * 512, rb * 512 + 512)), both(dF), 0, 0).astype(BF)
        for k in range(4):
            s, half = 2 * rb + k // 2, k % 2
            PU[half, s % 2, s // 2] = part[k * 128 : k * 128 + 128]
    if ring:
        reduce_core(0)
    for cb in range(4):
        part = dot(both(Hlow), both(dU, slice(cb * 512, cb * 512 + 512)), 0, 0).astype(BF)
        for s in range(SHARDS):
            for half in range(2):
                at = s * 64 + half * 32
                PI[half, s % 2, s // 2, cb * 32 : cb * 32 + 32, :] = part[at : at + 32]

    def by_owner(dst, value, row):
        for s in range(SHARDS):
            for half in range(2):
                at = s * 64 + half * 32
                dst[half, s % 2, s // 2, row : row + 32, :] = value[at : at + 32]

    ot = jnp.concatenate([OT[0], OT[1]], axis=1)
    by_owner(PI, dot(ot, both(dA)).astype(BF), 128)

    if ring:
        reduce_core(1)
        reduce_y(0)

    acc[...] = jnp.zeros(acc.shape, F32)
    dwk[...] = jnp.zeros(dwk.shape, F32)
    dwv[...] = jnp.zeros(dwv.shape, F32)

    def attend_back(sec, kb, diagonal):
        def scores(h):
            p, a = h // 2, h % 2
            own = (lane < 64) == (a == 0)
            first = (1 - a) * 64
            one = jnp.where((lane >= first) & (lane < first + 3), 1.0, 0.0).astype(BF)
            cols = slice(p * 128, p * 128 + 128)
            s = dot(jnp.where(own, K[kb, :, cols], one), QTa[sec, h])
            if diagonal:
                s = jnp.where(key_at <= query_at, s, -1e30)
            return s, dot(jnp.where(own, V[kb, :, cols], one), dOTa[sec, h])

        def weigh(s, dp):
            probs = jnp.exp2(s)
            return probs.astype(BF), (probs * dp).astype(BF)

        def to_queries(h, d_s):
            acc[sec, h, 0:64, :] += dot(KT[h * 64 : h * 64 + 64, :], d_s)

        def to_keys(p, first, second):
            cols = slice(p * 128, p * 128 + 128)
            q_pair, do_pair = Q[sec, :, cols], dO[sec, :, cols]
            zero = jnp.zeros_like(q_pair)
            low = lane < 64

            def stacked(pair):
                return jnp.concatenate(
                    [jnp.where(low, pair, zero), jnp.where(low, zero, pair)], axis=0
                )

            dva[:, cols] += dot(jnp.concatenate([first[0], second[0]], axis=1), stacked(do_pair))
            dka[:, cols] += dot(jnp.concatenate([first[1], second[1]], axis=1), stacked(q_pair))

        now = scores(0)
        done = []
        for n in range(HEADS + 1):
            later = scores(n + 1) if n + 1 < HEADS else None
            if n < HEADS:
                done.append(weigh(*now))
            if n > 0:
                to_queries(n - 1, done[n - 1][1])
                if n % 2 == 0:
                    to_keys(n // 2 - 1, done[n - 2], done[n - 1])
            now = later

    def relay(sec):
        arrived(rel_in.at[sec], dr.at[2 + sec])
        far_out[sec] = (far_out[sec].astype(F32) + rel_in[sec].astype(F32)).astype(BF)
        to(far_out.at[sec], far_in.at[sec], ds.at[4 + sec], dr.at[4 + sec], ctx=far).start()

    def backward(i, _):
        owner_sec, owner, kb, sent, used = step_of(i)

        @pl.when(used)
        def _():
            KT[...] = K[kb].astype(F32).T.astype(BF)
            dka[...] = jnp.zeros(dka.shape, F32)
            dva[...] = jnp.zeros(dva.shape, F32)

        def section(sec, _):
            qb = jnp.where(sec == 0, c, 7 - c)

            @pl.when(used & (kb < qb))
            def _():
                attend_back(sec, kb, False)

            @pl.when(used & (kb == qb))
            def _():
                attend_back(sec, kb, True)

            return 0

        lax.fori_loop(0, 2, section, 0)

        @pl.when(used)
        def _():
            dk = (dka[...] * LN2).astype(BF)
            dv = dva[...].astype(BF)
            x = X[kb]
            dwk[...] += dot(x, dk, 0, 0)
            dwv[...] += dot(x, dv, 0, 0)
            sums[1:2, :] += dot(ones, dv)[0:1]
            dx = dot(dk, weight(AT_KEY), 1, 1) + dot(dv, weight(AT_VALUE), 1, 1)

            @pl.when(i < 2)
            def _():
                rel_out[owner_sec] = dx.astype(BF)
                to(rel_out.at[owner_sec], rel_in.at[owner_sec], ds.at[2 + owner_sec], dr.at[2 + owner_sec], ctx=sib).start()

            @pl.when((i == 2) | (i == 3))
            def _():
                far_out[owner_sec] = dx.astype(BF)

            @pl.when((i == 4) | (i == 5))
            def _():
                sib_out[owner_sec] = dx.astype(BF)
                to(sib_out.at[owner_sec], sib_in.at[owner_sec], ds.at[owner_sec], dr.at[owner_sec], ctx=sib).start()

            @pl.when(i >= 6)
            def _():
                dR[owner_sec] += dx

        @pl.when(i == 3)
        def _():
            relay(0)
            pl.when(chip == 0)(functools.partial(relay, 1))

        if ring:
            pl.when(i == 0)(functools.partial(reduce_y, 1))
            pl.when(i == 2)(functools.partial(reduce_z, 0, 0, 2))
            pl.when(i == 3)(functools.partial(reduce_z, 0, 2, 4))
            pl.when(i == 5)(functools.partial(reduce_z, 1, 0, 2))
            pl.when(i == 6)(functools.partial(reduce_z, 1, 2, 4))
            pl.when(i == 6)(functools.partial(reduce_x, 0))
        return 0

    lax.fori_loop(0, 8, backward, 0)

    by_owner(PK, dwk[...].astype(BF), 0)
    by_owner(PK, dwv[...].astype(BF), 32)
    if ring:
        reduce_core(2)

    def d_query(sec, _):
        dq = jnp.concatenate([acc[sec, h, 0:64, :] for h in range(HEADS)], axis=0)
        Q[sec] = (dq * SCALE).T.astype(BF)
        sums[0:1, :] += dot(ones, Q[sec])[0:1]
        return 0

    lax.fori_loop(0, 2, d_query, 0)
    xx = jnp.concatenate([X[c], X[7 - c]], axis=0)
    by_owner(PQ, dot(xx, both(Q), 0, 0).astype(BF), 0)
    for s in range(SHARDS):
        row = jnp.concatenate(
            [sums[:, s * 64 : s * 64 + 64], jnp.zeros((8, 448), F32)], axis=1
        )
        PQ[0, s % 2, s // 2, 32:48, :] = jnp.concatenate(
            [row, jnp.zeros((8, 512), F32)], axis=0
        ).astype(BF)
        row = jnp.concatenate(
            [sums_inner[:, s * 256 : s * 256 + 256], jnp.zeros((8, 256), F32)], axis=1
        )
        PQ[1, s % 2, s // 2, 32:48, :] = jnp.concatenate(
            [row, jnp.zeros((8, 512), F32)], axis=0
        ).astype(BF)
    if ring:
        reduce_core(3)
        reduce_y(2)
        reduce_y(3)

    for sec in range(2):
        dx = dR[sec] + dot(Q[sec], weight(AT_QUERY), 1, 1)
        tg_v[sec] = dx.astype(BF)
        dR[sec] = dx

    def add_incoming(ref, sem, sec):
        arrived(ref.at[sec], sem)
        dR[sec] += ref[sec].astype(F32)

    add_incoming(sib_in, dr.at[0], 0)
    pl.when(core == 1)(lambda: add_incoming(sib_in, dr.at[1], 1))
    add_incoming(far_in, dr.at[4], 0)
    pl.when(chip == 1)(lambda: add_incoming(far_in, dr.at[5], 1))
    for sec in range(2):
        tg_v[sec] = dR[sec].astype(BF)
    tg_copy = pltpu.make_async_copy(tg_v, tg_ref, out_sem.at[1])
    tg_copy.start()

    if ring:
        reduce_z(2)
        reduce_z(3)
        reduce_x(1)
        reduce_last(0)
        for u in range(6):
            gather_left(u)
        reduce_last(1)
        reduce_x(2)
        reduce_x(3)
        for g in range(2):
            reduce_end(g)
            finals[g].start()
        reduce_last(2)
        reduce_last(3)
        for g in range(2, 4):
            reduce_end(g)
            finals[g].start()
        for g in range(4):
            finals[g].wait()
    else:
        copies = [
            pltpu.make_async_copy(part, out, load_sem.at[k])
            for k, (part, out) in enumerate(((PU, pu_out), (PI, pi_out), (PK, pk_out), (PQ, pq_out)))
        ]
        for copy in copies:
            copy.start()
        for copy in copies:
            copy.wait()

    block = X.at[0]
    for k in range(3):
        left(block, xs.at[k])
    pl.when(chip == 1)(lambda: left(block, xs.at[3]))
    left(block, xs.at[4])
    pl.when(chip == 0)(lambda: left(block, xs.at[5]))
    left(block, ds.at[0])
    pl.when(core == 0)(lambda: left(block, ds.at[1]))
    left(block, ds.at[2])
    pl.when(chip == 0)(lambda: left(block, ds.at[3]))
    left(block, ds.at[4])
    pl.when(chip == 0)(lambda: left(block, ds.at[5]))
    out_copy.wait()
    tg_copy.wait()


def run(ring, tokens, cotangent, weights, smalls):
    blk = tokens.shape[1]
    vm = lambda *shape: pltpu.VMEM(shape, BF)
    vf = lambda *shape: pltpu.VMEM(shape, F32)
    dma = lambda *shape: pltpu.SemaphoreType.DMA(shape)
    any_spec = pl.BlockSpec(memory_space=pl.ANY)
    outs = [jax.ShapeDtypeStruct(tokens.shape, BF)] * 2
    out_specs = [any_spec] * 2
    if ring:
        outs += [jax.ShapeDtypeStruct((2, rows, D), BF) for rows in GROUP_ROWS]
        out_specs += [any_spec] * 4
    else:
        outs += [
            jax.ShapeDtypeStruct((2, 2, 4, rows, D), BF) for rows in GROUP_ROWS
        ]
        out_specs += [any_spec] * 4
    scratch = [vm(8, blk, D)] * 3
    scratch += [vm(4, 2, 2, PACKED, D)]
    scratch += [vf(8, D), vf(1, FF)]
    scratch += [vm(2, blk, D), vm(2, HEADS, 128, blk)] * 2
    scratch += [vm(HEADS, 80, blk), vm(D, blk)]
    scratch += [vf(2, HEADS, 8, blk), vf(2, HEADS, 80, blk), vm(2, D, blk)]
    scratch += [vm(2, blk, D), vf(2, blk, D), vf(2, blk, 1)]
    scratch += [vm(2, blk, FF)] * 2 + [vm(2, blk, D), vf(2, blk, D), vm(2, blk, D)]
    scratch += [vf(D, D)] * 2
    scratch += [vf(8, D), vf(8, FF)]
    scratch += [vm(2, blk, D)]
    scratch += [vm(2, 2, 4, rows, D) for rows in GROUP_ROWS]
    scratch += [vm(2, blk, D)] * 3
    scratch += [dma(14), dma(2), dma(6), dma(8)]
    scratch += [dma(6), dma(6)]
    if ring:
        for rows in GROUP_ROWS:
            scratch += [vm(2, 4, rows, D), vm(4, rows, D), vm(3, rows, D)]
            scratch += [vm(rows, D), vm(rows, D), vm(2, rows, D)]
        scratch += [dma(6, 6), dma(6, 4), dma(6, 2), dma(6, 4), dma(6), dma(6, 2)]
        scratch += [dma(4, 11), dma(4, 11)]
    inputs = [tokens, cotangent, *weights, *smalls]
    return pl.pallas_call(
        functools.partial(layer, ring, blk),
        out_shape=outs,
        in_specs=[any_spec] * len(inputs),
        out_specs=out_specs,
        scratch_shapes=scratch,
        compiler_params=pltpu.CompilerParams(
            collective_id=0, has_side_effects=True, vmem_limit_bytes=63 << 20
        ),
        name="layer",
    )(*inputs)


def finish_kernel(out_in, tg_in, fu, fi, fk, fq, *refs):
    out_ref, tg_ref, gq, gk, gv, go, gi, gu = refs[:8]
    vectors, inner = refs[8:16], refs[16]
    sems = refs[17]
    copies = [
        pltpu.make_async_copy(out_in, out_ref, sems.at[0]),
        pltpu.make_async_copy(tg_in, tg_ref, sems.at[1]),
    ]
    for copy in copies:
        copy.start()
    for half in range(2):
        rows = slice(half * 32, half * 32 + 32)
        gu[half * 128 : half * 128 + 128, :] = fu[half].astype(F32)
        for cb in range(4):
            gi[rows, cb * 512 : cb * 512 + 512] = fi[half, cb * 32 : cb * 32 + 32, :].astype(F32)
        go[rows, :] = fi[half, 128:160, :].astype(F32)
        gq[rows, :] = fq[half, 0:32, :].astype(F32)
        gk[rows, :] = fk[half, 0:32, :].astype(F32)
        gv[rows, :] = fk[half, 32:64, :].astype(F32)
    small = fq[0, 32:48, 0:128].astype(F32)
    for j in range(8):
        vectors[j][...] = small[j : j + 1, 0:64]
    inner[...] = fq[1, 32:48, 0:256].astype(F32)[0:1]
    for copy in copies:
        copy.wait()


def finish_all(tokens, weights, res):
    any_spec = pl.BlockSpec(memory_space=pl.ANY)
    vmem_spec = pl.BlockSpec(memory_space=pltpu.VMEM)
    outs = [jax.ShapeDtypeStruct(tokens.shape, BF)] * 2
    outs += [jax.ShapeDtypeStruct(w.shape, F32) for w in weights]
    outs += [jax.ShapeDtypeStruct((1, 64), F32)] * 8
    outs += [jax.ShapeDtypeStruct((1, 256), F32)]
    return pl.pallas_call(
        finish_kernel,
        out_shape=outs,
        in_specs=[vmem_spec] * 6,
        out_specs=[any_spec] * 2 + [vmem_spec] * 15,
        scratch_shapes=[pltpu.SemaphoreType.DMA((2,))],
        name="finish",
    )(*res)


def shards(tokens, *rest):
    (wq, bq, wk, wv, bv, wo, bo, g1, s1, wi, bi, wu, bu, g2, s2, cotangent) = rest
    blk = tokens.shape[3]
    tok = tokens.reshape(2, blk, D)
    cot = cotangent.reshape(2, blk, D)
    weights = (wq, wk, wv, wo, wi, wu)
    vectors = (bq, bv, bo, g1, s1, bu, g2, s2)
    ring = lax.axis_size("fsdp") == SHARDS
    if ring:
        stacked = jnp.pad(jnp.stack(vectors), ((0, 8), (0, D - 64)))
        inner = jnp.pad(bi.reshape(1, 256), ((0, 15), (0, D - 256)))
        small = jnp.stack([stacked, inner])
        halves = [w.reshape(2, -1, D) for w in (wq, wk, wv)] + [small]
        halves += [wo.reshape(2, -1, D), wu.reshape(2, -1, D), wi.reshape(2, -1, FF)]
        res = run(True, tok, cot, halves, ())
        res = finish_all(tok, weights, res)
        output, tokens_grad, gq, gk, gv, go, gi, gu = res[:8]
        gvec = [v.reshape(64) for v in res[8:16]]
        gbi = res[16].reshape(256)
    else:
        gather = lambda w: lax.all_gather(w, "fsdp", axis=0, tiled=True)
        rows = lambda w: gather(w).reshape(4, 2, 2, -1, D)
        inner_rows = gather(wi).reshape(4, 2, 2, 32, 4, D).transpose(0, 1, 2, 4, 3, 5)
        unused = jnp.zeros((4, 2, 2, AT_OUT - AT_SMALL, D), BF)
        packed = [rows(wq), rows(wk), rows(wv), unused, rows(wo)]
        packed += [inner_rows.reshape(4, 2, 2, 128, D), rows(wu)]
        full = [jnp.concatenate(packed, axis=3)]
        vec = jnp.stack([gather(v).astype(F32) for v in vectors])
        inner = gather(bi).astype(F32).reshape(1, FF)
        output, tokens_grad, pu, pi, pk, pq = run(False, tok, cot, full, (vec, inner))

        def whole(part, rows):
            return part.transpose(2, 1, 0, 3, 4).reshape(SHARDS * 2 * rows, D)

        parts = [
            whole(pq[:, :, :, 0:32], 32),
            whole(pk[:, :, :, 0:32], 32),
            whole(pk[:, :, :, 32:64], 32),
            whole(pi[:, :, :, 128:160], 32),
            pi[:, :, :, 0:128]
            .reshape(2, 2, 4, 4, 32, D)
            .transpose(2, 1, 0, 4, 3, 5)
            .reshape(D, FF),
            whole(pu, 128),
        ]
        vecs = pq[0, :, :, 32:40, 0:64].transpose(2, 1, 0, 3).reshape(8, D)
        inner = pq[1, :, :, 32, 0:256].transpose(1, 0, 2).reshape(FF)
        parts += [vecs[j] for j in range(8)] + [inner]
        count = lax.axis_size("fsdp")
        packed = jnp.concatenate(
            [part.astype(F32).reshape(count, -1) for part in parts], axis=1
        ).reshape(-1)
        shares = lax.psum_scatter(packed, "fsdp", scatter_dimension=0, tiled=True)
        summed = lax.psum(shares.astype(BF), "ctx").astype(F32)
        pieces, at = [], 0
        for initial in weights + vectors + (bi,):
            pieces.append(summed[at : at + initial.size].reshape(initial.shape))
            at = at + initial.size
        gq, gk, gv, go, gi, gu = pieces[:6]
        gvec, gbi = pieces[6:14], pieces[14]
    order = (gq, gvec[0], gk, gv, gvec[1], go, gvec[2], gvec[3], gvec[4], gi, gbi, gu)
    order += (gvec[5], gvec[6], gvec[7])
    return (output.reshape(tokens.shape), tokens_grad.reshape(tokens.shape)) + order


def solution(mesh):
    row = P("fsdp", None)
    one = P("fsdp")
    act = P("fsdp", None, "ctx", None, None)
    params = (row, one, row, row, one, row, one, one, one, row, one, row, one, one, one)
    return jax.shard_map(
        shards,
        mesh=mesh,
        in_specs=(act,) + params + (act,),
        out_specs=(act, act) + params,
        check_vma=False,
    )
```

```python
import functools
import math

import jax
import jax.numpy as jnp
from jax import lax
from jax.experimental import pallas as pl
from jax.experimental.pallas import tpu as pltpu
from jax.sharding import PartitionSpec as P

HEADS = 8
HEAD = 64
D = 512
FF = 2048
CTX = 4
SHARDS = 8
EPS = 1e-5
BF = jnp.bfloat16
F32 = jnp.float32
QUERY_SCALE = math.log2(math.e) / math.sqrt(HEAD)
SCALE = 1.0 / math.sqrt(HEAD)
LN2 = math.log(2.0)
AT_QUERY, AT_KEY, AT_VALUE, AT_SMALL, AT_OUT, AT_INNER, AT_OUTER, PACKED = 0, 32, 64, 96, 112, 144, 272, 400
UNITS = ((0, 32), (32, 64), (64, 112), (112, 208), (208, 304), (304, 400))
GATHER_AT = (
    (0, 3, 1),
    (1, 4, 1),
    (2, 5, 1),
    (3, 3, 2),
    (4, 4, 2),
    (6, 5, 2),
    (7, 3, 3),
    (9, 4, 3),
    (11, 5, 3),
    (12, 3, 0),
    (15, 4, 0),
)
GROUP_ROWS = (128, 160, 64, 48)


def dot(left, right, left_dim=1, right_dim=0):
    return lax.dot_general(
        left, right, (((left_dim,), (right_dim,)), ((), ())), preferred_element_type=F32
    )


def rows_mean(value):
    return jnp.mean(value, axis=-1, keepdims=True)


def layer(ring, blk, *refs):
    it = iter(refs)
    take = lambda count: [next(it) for _ in range(count)]
    tok, cot = take(2)
    weights_in = take(7 if ring else 1)
    small_in = take(0 if ring else 2)
    out_ref, tg_ref = take(2)
    if ring:
        finals_out = take(4)
    else:
        pu_out, pi_out, pk_out, pq_out = take(4)
    X, K, V = take(3)
    W = next(it)
    vec, vec_inner = take(2)
    Q, QTa, dO, dOTa = take(4)
    VTa = next(it)
    top, acc, OT = take(3)
    Hlow, n1, rstd1 = take(3)
    Z, dU, dF, dR, dA = take(5)
    dwkv = next(it)
    dka, dva = n1.at[0], n1.at[1]
    sums, sums_inner = take(2)
    cot_v = next(it)
    tg_v = dO
    PU, PI, PK, PQ = take(4)
    sib_in, rel_in, far_in = take(3)
    sib_out, rel_out, far_out = dA, dF, Hlow
    load_sem, out_sem, xs, xr = take(4)
    ds, dr = take(2)
    if ring:
        buffers = [take(6) for _ in range(4)]
        zs, ys, cs, rz, ry, rc, gs, gr = take(8)

    t = lax.axis_index("ctx")
    chip, core = t // 2, lax.rem(t, 2)
    sib = t + 1 - 2 * core
    far = lax.rem(t + 2, 4)
    c = t
    MESH = pl.DeviceIdType.MESH

    def to(ref, dst, send, recv, **where):
        return pltpu.make_async_remote_copy(
            src_ref=ref,
            dst_ref=dst,
            send_sem=send,
            recv_sem=recv,
            device_id=where,
            device_id_type=MESH,
        )

    def arrived(ref, sem):
        pltpu.make_async_copy(ref, ref, sem).wait()

    def left(ref, sem):
        pltpu.make_async_copy(ref, ref, sem).wait()

    peers = [{"ctx": sib}, {"ctx": far}]
    if ring:
        f = lax.axis_index("fsdp")
        z, y = f // 2, lax.rem(f, 2)
        fy = f + 1 - 2 * y
        zpeer = [lax.rem(z + dz, 4) * 2 + y for dz in (1, 2, 3)]
        peers += [{"fsdp": fy}] + [{"fsdp": zp} for zp in zpeer]

    own_blocks = [c, 7 - c]
    loads = []
    for sec in range(2):
        loads.append(
            pltpu.make_async_copy(tok.at[sec], X.at[own_blocks[sec]], load_sem.at[sec])
        )
        loads.append(
            pltpu.make_async_copy(cot.at[sec], cot_v.at[sec], load_sem.at[2 + sec])
        )
    if ring:
        for w, at in enumerate((AT_QUERY, AT_KEY, AT_VALUE, AT_SMALL, AT_OUT, AT_OUTER)):
            src = weights_in[w].at[core]
            loads.append(
                pltpu.make_async_copy(
                    src, W.at[z, y, core, pl.ds(at, src.shape[0])], load_sem.at[4 + w]
                )
            )
        for cb in range(4):
            src = weights_in[6].at[core, :, pl.ds(cb * D, D)]
            loads.append(
                pltpu.make_async_copy(
                    src, W.at[z, y, core, pl.ds(AT_INNER + cb * 32, 32)], load_sem.at[10 + cb]
                )
            )
    else:
        loads.append(pltpu.make_async_copy(weights_in[0], W, load_sem.at[4]))
        loads.append(pltpu.make_async_copy(small_in[0], vec, load_sem.at[5]))
        loads.append(pltpu.make_async_copy(small_in[1], vec_inner, load_sem.at[6]))
    for copy in loads:
        copy.start()

    barrier = pltpu.get_barrier_semaphore()
    for where in peers:
        pl.semaphore_signal(barrier, inc=1, device_id=where, device_id_type=MESH)
    pl.semaphore_wait(barrier, len(peers))

    for sec in range(2):
        b = own_blocks[sec]
        to(tok.at[sec], X.at[b], xs.at[sec], xr.at[b], ctx=sib).start()
    to(tok.at[0], X.at[c], xs.at[2], xr.at[c], ctx=far).start()

    @pl.when(chip == 1)
    def _():
        to(tok.at[1], X.at[7 - c], xs.at[3], xr.at[7 - c], ctx=far).start()

    if ring:
        def piece(u, zz, yy, half):
            first, last = UNITS[u]
            return W.at[zz, yy, half, pl.ds(first, last - first)]

        def pieces(u, yy, half):
            first, last = UNITS[u]
            return W.at[:, yy, half, pl.ds(first, last - first)]

        def gather_start(u):
            ref = piece(u, z, y, core)
            to(ref, ref, ys.at[u, z], ry.at[u], fsdp=fy).start()
            pl.when(z < 3)(lambda: to(ref, ref, zs.at[u, 4], rz.at[u, z], fsdp=f + 2).start())
            pl.when(z > 0)(lambda: to(ref, ref, zs.at[u, 5], rz.at[u, z], fsdp=f - 2).start())

        def gather_z(u, hops):
            def pass_on(zz, more, onward):
                ref = piece(u, zz, y, core)
                arrived(ref, rz.at[u, zz])
                if hops < 3:
                    pl.when(more)(lambda: to(ref, ref, zs.at[u, zz], rz.at[u, zz], fsdp=onward).start())
                to(ref, ref, ys.at[u, zz], ry.at[u], fsdp=fy).start()

            pl.when(z - hops >= 0)(lambda: pass_on(z - hops, z < 3, f + 2))
            pl.when(z + hops <= 3)(lambda: pass_on(z + hops, z > 0, f - 2))
            if hops == 3:
                ref = pieces(u, y, core)
                to(ref, ref, cs.at[u, 0], rc.at[u, 0], ctx=sib).start()

        def gather_y(u):
            ref = pieces(u, 1 - y, core)
            arrived(ref, ry.at[u])
            to(ref, ref, cs.at[u, 1], rc.at[u, 1], ctx=sib).start()

        def gather_end(u):
            arrived(pieces(u, y, 1 - core), rc.at[u, 0])
            arrived(pieces(u, 1 - y, 1 - core), rc.at[u, 1])

        def gather_left(u):
            ref = piece(u, 0, 0, 0)
            pl.when(z < 3)(lambda: left(ref, zs.at[u, 4]))
            pl.when(z > 0)(lambda: left(ref, zs.at[u, 5]))
            for zz in range(4):
                onward = ((zz < z) & (z < 3)) | ((zz > z) & (z > 0))
                pl.when(onward)(lambda zz=zz: left(ref, zs.at[u, zz]))
                left(ref, ys.at[u, zz])
            for i in range(2):
                left(pieces(u, 0, 0), cs.at[u, i])

        for copy in loads[4:]:
            copy.wait()
        for u in range(3):
            gather_start(u)
        for hops in (1, 2, 3):
            for u in range(3):
                gather_z(u, hops)
        for u in range(3, 6):
            gather_start(u)
    else:
        for copy in loads[4:]:
            copy.wait()

    def far_tokens():
        b = far
        arrived(X.at[b], xr.at[b])
        to(X.at[b], X.at[b], xs.at[4], xr.at[b], ctx=sib).start()

        @pl.when(chip == 0)
        def _():
            b = 7 - far
            arrived(X.at[b], xr.at[b])
            to(X.at[b], X.at[b], xs.at[5], xr.at[b], ctx=sib).start()

    if ring:
        for u in range(3):
            gather_y(u)
        for u in range(3):
            gather_end(u)
        small = [[W[s // 2, s % 2, half, AT_SMALL:AT_OUT, :].astype(F32) for s in range(SHARDS)] for half in range(2)]
        vec[...] = jnp.concatenate([part[0:8, 0:64] for part in small[0]], axis=1)
        vec_inner[...] = jnp.concatenate([part[0:1, 0:256] for part in small[1]], axis=1)

    def weight(at, rows=32):
        return W[:, :, :, at : at + rows, :].reshape(SHARDS * 2 * rows, D)

    def key_value_weight():
        return jnp.concatenate([weight(AT_KEY), weight(AT_VALUE)], axis=1)

    b_query, b_value, b_out, gain1, shift1, b_outer, gain2, shift2 = (
        vec[pl.ds(j, 1), :] for j in range(8)
    )
    for sec in range(2):
        loads[2 * sec].wait()

    VTa[:, 64:80, :] = jnp.ones((HEADS, 16, blk), BF)
    for h in range(HEADS):
        other = (1 - h % 2) * 64
        for sec in range(2):
            QTa[sec, h, other : other + 64, :] = jnp.zeros((64, blk), BF)
            dOTa[sec, h, other : other + 64, :] = jnp.zeros((64, blk), BF)

    def queries(sec, _):
        x = X[jnp.where(sec == 0, c, 7 - c)]
        q = (dot(x, weight(AT_QUERY)) + b_query) * QUERY_SCALE
        Q[sec] = q.astype(BF)
        qt = q.T.astype(BF)
        for h in range(HEADS):
            own = (h % 2) * 64
            QTa[sec, h, own : own + 64, :] = qt[h * 64 : h * 64 + 64]
        return 0

    lax.fori_loop(0, 2, queries, 0)

    lane = lax.broadcasted_iota(jnp.int32, (blk, 128), 1)
    key_at = lax.broadcasted_iota(jnp.int32, (blk, blk), 0)
    query_at = lax.broadcasted_iota(jnp.int32, (blk, blk), 1)

    def step_of(i):
        sec = lax.rem(i, 2)
        owner_core = jnp.where(i < 2, 1 - core, core)
        owner = jnp.where(i < 4, 2 * (1 - chip) + owner_core, jnp.where(i < 6, sib, t))
        kb = jnp.where(sec == 0, owner, 7 - owner)
        sent = (i >= 4) | (chip == 0) | (sec == 0)
        return sec, owner, kb, sent, sent & (kb <= 7 - c)

    top[...] = jnp.full(top.shape, -1e30, F32)
    acc[...] = jnp.zeros(acc.shape, F32)

    def attend(sec, kb, diagonal):
        def scores(h):
            p, a = h // 2, h % 2
            k_pair = K[kb, :, p * 128 : p * 128 + 128]
            k_head = jnp.where((lane < 64) == (a == 0), k_pair, jnp.zeros_like(k_pair))
            s = dot(k_head, QTa[sec, h])
            if diagonal:
                s = jnp.where(key_at <= query_at, s, -1e30)
            return s

        def weigh(h, s):
            old = top[sec, h, 0:1, :]
            new = jnp.maximum(old, jnp.max(s, axis=0, keepdims=True))
            top[sec, h] = jnp.broadcast_to(new, (8, blk))
            return jnp.exp2(s - new).astype(BF), jnp.exp2(old - new)

        def gather_values(h, probs, shrink):
            acc[sec, h] = acc[sec, h] * shrink + dot(VTa[h], probs)

        s = scores(0)
        held = None
        for h in range(HEADS):
            later = scores(h + 1) if h + 1 < HEADS else None
            now = (h, *weigh(h, s))
            if held is not None:
                gather_values(*held)
            held, s = now, later
        gather_values(*held)

    def keys_values(kb):
        x = X[kb]
        kv = dot(x, key_value_weight())
        K[kb] = kv[:, :D].astype(BF)
        v = kv[:, D:] + b_value
        V[kb] = v.astype(BF)
        vt = v.T.astype(BF)
        for h in range(HEADS):
            VTa[h, 0:64, :] = vt[h * 64 : h * 64 + 64]

    def forward(n, _):
        i = jnp.where(n < 2, 6 + n, jnp.where(n < 4, 2 + n, jnp.where(n < 6, n - 2, n - 6)))
        _, _, kb, sent, used = step_of(i)

        @pl.when(n == 4)
        def _():
            far_tokens()

        @pl.when(sent & ((n == 2) | (n == 3) | (n >= 6)))
        def _():
            arrived(X.at[kb], xr.at[kb])

        @pl.when(used)
        def _():
            keys_values(kb)

        def section(sec, _):
            qb = jnp.where(sec == 0, c, 7 - c)
            if ring:
                for at, u, hops in GATHER_AT:
                    if hops:
                        pl.when(2 * n + sec == at)(functools.partial(gather_z, u, hops))
                    else:
                        pl.when(2 * n + sec == at)(functools.partial(gather_y, u))

            @pl.when(used & (kb < qb))
            def _():
                attend(sec, kb, False)

            @pl.when(used & (kb == qb))
            def _():
                attend(sec, kb, True)

            return 0

        lax.fori_loop(0, 2, section, 0)
        return 0

    lax.fori_loop(0, 8, forward, 0)

    def finish(sec, _):
        for h in range(HEADS):
            other = (1 - h % 2) * 64
            total = acc[sec, h, 64:65, :]
            OT[sec, h * 64 : h * 64 + 64, :] = (acc[sec, h, 0:64, :] / total).astype(BF)
            low = -(top[sec, h, 0:1, :] + jnp.log2(total))
            parts = []
            for _ in range(3):
                parts.append(low.astype(BF))
                low = low - parts[-1].astype(F32)
            QTa[sec, h, other : other + 16, :] = jnp.concatenate(
                parts + [jnp.zeros((13, blk), BF)], axis=0
            )
        return 0

    if ring:
        gather_y(5)
    lax.fori_loop(0, 2, finish, 0)
    if ring:
        gather_end(3)
    for sec in range(2):
        loads[2 * sec + 1].wait()

    sums[...] = jnp.zeros(sums.shape, F32)
    sums_inner[...] = jnp.zeros(sums_inner.shape, F32)
    ones = jnp.ones((16, blk), BF)

    def column_sum(value):
        return jnp.sum(value, axis=0, keepdims=True)

    def dense(sec):
        x = X[own_blocks[sec]].astype(F32)
        r1 = x + dot(OT[sec], weight(AT_OUT), 0, 0) + b_out
        yield
        center = r1 - rows_mean(r1)
        rs1 = lax.rsqrt(rows_mean(center * center) + EPS)
        n1[sec] = center * rs1
        rstd1[sec] = rs1
        Hlow[sec] = (n1[sec] * gain1 + shift1).astype(BF)
        yield
        c0 = math.sqrt(2.0 / math.pi)
        columns = [slice(cb * 512, cb * 512 + 512) for cb in range(4)]

        def hidden(cb):
            if ring and sec == 0 and cb == 2:
                gather_end(4)
            return dot(Hlow[sec], weight(AT_INNER + 32 * cb)) + vec_inner[:, columns[cb]]

        u = hidden(0)
        for cb in range(4):
            later = hidden(cb + 1) if cb < 3 else None
            uu = u * u
            th = jnp.tanh(c0 * u * (1.0 + 0.044715 * uu))
            half = 0.5 * (1.0 + th)
            Z[sec, :, columns[cb]] = (u * half).astype(BF)
            slope = half + 0.5 * u * (1.0 - th * th) * (c0 * (1.0 + 3 * 0.044715 * uu))
            dU[sec, :, columns[cb]] = slope.astype(BF)
            u = later
        yield
        if ring and sec == 0:
            gather_end(5)
        r2 = n1[sec] * gain1 + shift1 + dot(Z[sec], weight(AT_OUTER, 128)) + b_outer
        yield
        center = r2 - rows_mean(r2)
        rs2 = lax.rsqrt(rows_mean(center * center) + EPS)
        n2 = center * rs2
        g = cot_v[sec].astype(F32)
        cot_v[sec] = (n2 * gain2 + shift2).astype(BF)
        sums[6:7, :] += column_sum(g * n2)
        sums[7:8, :] += column_sum(g)
        g = g * gain2
        d_r2 = (g - rows_mean(g) - n2 * rows_mean(g * n2)) * rs2
        dR[sec] = d_r2
        d_f = d_r2.astype(BF)
        dF[sec] = d_f
        sums[5:6, :] += dot(ones, d_f)[0:1]
        yield

        def d_active(cb):
            rows = W[cb, :, :, AT_OUTER:PACKED, :].reshape(D, D)
            return dot(dF[sec], rows, 1, 1)

        now = d_active(0)
        for cb in range(4):
            later = d_active(cb + 1) if cb < 3 else None
            d_u = (now * dU[sec, :, columns[cb]].astype(F32)).astype(BF)
            dU[sec, :, columns[cb]] = d_u
            sums_inner[0:1, columns[cb]] += dot(ones, d_u)[0:1]
            now = later
        yield
        inner = jnp.concatenate([weight(AT_INNER + 32 * cb) for cb in range(4)], axis=1)
        d_h = dR[sec] + dot(dU[sec], inner, 1, 1)
        yield
        nn1 = n1[sec]
        sums[3:4, :] += column_sum(d_h * nn1)
        sums[4:5, :] += column_sum(d_h)
        g = d_h * gain1
        d_r1 = (g - rows_mean(g) - nn1 * rows_mean(g * nn1)) * rstd1[sec]
        dR[sec] = d_r1
        d_a = d_r1.astype(BF)
        dA[sec] = d_a
        sums[2:3, :] += dot(ones, d_a)[0:1]
        yield
        dO[sec] = dot(dA[sec], weight(AT_OUT), 1, 1).astype(BF)
        d_ot = dot(weight(AT_OUT), dA[sec], 1, 1)
        yield
        for h in range(HEADS):
            own, other = (h % 2) * 64, (1 - h % 2) * 64
            part = d_ot[h * 64 : h * 64 + 64].astype(BF)
            dOTa[sec, h, own : own + 64, :] = part
            o = OT[sec, h * 64 : h * 64 + 64, :].astype(F32)
            rest = -column_sum(part.astype(F32) * o)
            parts = []
            for _ in range(3):
                parts.append(rest.astype(BF))
                rest = rest - parts[-1].astype(F32)
            dOTa[sec, h, other : other + 16, :] = jnp.concatenate(
                parts + [jnp.zeros((13, blk), BF)], axis=0
            )

    sections = [dense(0), dense(1)]

    def advance(stages):
        for _ in range(stages):
            for work in sections:
                next(work, 0)

    advance(5)

    @pl.when(t >= 0)
    def _():
        advance(6)

    out_copy = pltpu.make_async_copy(cot_v, out_ref, out_sem.at[0])
    out_copy.start()

    if ring:
        groups = [(mine, *more) for mine, more in zip((PU, PI, PK, PQ), buffers)]

        finals = [
            pltpu.make_async_copy(groups[g][6], finals_out[g], load_sem.at[g]) for g in range(4)
        ]

        def add_into(dst, *terms):
            total = dst[...].astype(F32)
            for term in terms:
                total = total + term[...].astype(F32)
            dst[...] = total.astype(BF)

        def reduce_core(g):
            mine, from_core = groups[g][:2]
            for k, yy in ((0, 1 - y), (1, y)):
                to(mine.at[1 - core, yy], from_core.at[k], gs.at[g, k], gr.at[g, k], ctx=sib).start()

        def reduce_y(g):
            mine, from_core, from_y = groups[g][:3]
            arrived(from_core.at[0], gr.at[g, 0])

            def body(n, _):
                k = lax.rem(z + 1 + n, 4)
                add_into(mine.at[core, 1 - y, k], from_core.at[0, k])
                to(mine.at[core, 1 - y, k], from_y.at[k], gs.at[g, 2 + n], gr.at[g, 2 + n], fsdp=fy).start()
                return 0

            lax.fori_loop(0, 4, body, 0)

        def reduce_z(g, first=0, last=4):
            mine, from_core, from_y, from_z = groups[g][:4]
            if first == 0:
                arrived(from_core.at[1], gr.at[g, 1])

            def body(n, _):
                k = lax.rem(z + 1 + n, 4)
                arrived(from_y.at[k], gr.at[g, 2 + n])
                add_into(mine.at[core, y, k], from_core.at[1, k], from_y.at[k])

                @pl.when(n < 3)
                def _():
                    to(mine.at[core, y, k], from_z.at[n], gs.at[g, 6 + n], gr.at[g, 6 + n], fsdp=k * 2 + y).start()

                return 0

            lax.fori_loop(first, last, body, 0)

        def reduce_x(g):
            mine, _, _, from_z, pair, from_x, _ = groups[g]
            for i in range(3):
                arrived(from_z.at[i], gr.at[g, 6 + i])
            pair[...] = (
                mine[core, y, z].astype(F32)
                + from_z[0].astype(F32)
                + from_z[1].astype(F32)
                + from_z[2].astype(F32)
            ).astype(BF)
            to(pair, from_x, gs.at[g, 9], gr.at[g, 9], ctx=far).start()

        def reduce_last(g):
            pair, from_x, final = groups[g][4:]
            arrived(from_x, gr.at[g, 9])
            final[core] = (pair[...].astype(F32) + from_x[...].astype(F32)).astype(BF)
            to(final.at[core], final.at[core], gs.at[g, 10], gr.at[g, 10], ctx=sib).start()

        def reduce_end(g):
            mine, from_core, from_y, from_z, pair, from_x, final = groups[g]
            arrived(final.at[1 - core], gr.at[g, 10])
            for k in range(2):
                left(from_core.at[k], gs.at[g, k])
            for i in range(4):
                left(from_y.at[0], gs.at[g, 2 + i])
            for i in range(3):
                left(from_z.at[i], gs.at[g, 6 + i])
            left(pair, gs.at[g, 9])
            left(final.at[0], gs.at[g, 10])

    def both(ref, cols=slice(None)):
        return jnp.concatenate([ref[0, :, cols], ref[1, :, cols]], axis=0)

    for rb in range(4):
        part = dot(both(Z, slice(rb * 512, rb * 512 + 512)), both(dF), 0, 0).astype(BF)
        for k in range(4):
            s, half = 2 * rb + k // 2, k % 2
            PU[half, s % 2, s // 2] = part[k * 128 : k * 128 + 128]
    if ring:
        reduce_core(0)
    for cb in range(4):
        part = dot(both(Hlow), both(dU, slice(cb * 512, cb * 512 + 512)), 0, 0).astype(BF)
        for s in range(SHARDS):
            for half in range(2):
                at = s * 64 + half * 32
                PI[half, s % 2, s // 2, cb * 32 : cb * 32 + 32, :] = part[at : at + 32]

    def by_owner(dst, value, row):
        for s in range(SHARDS):
            for half in range(2):
                at = s * 64 + half * 32
                dst[half, s % 2, s // 2, row : row + 32, :] = value[at : at + 32]

    ot = jnp.concatenate([OT[0], OT[1]], axis=1)
    by_owner(PI, dot(ot, both(dA)).astype(BF), 128)

    if ring:
        reduce_core(1)
        reduce_y(0)

    acc[...] = jnp.zeros(acc.shape, F32)
    dwkv[...] = jnp.zeros(dwkv.shape, F32)

    def attend_back(sec, kb, diagonal):
        def scores(h):
            p, a = h // 2, h % 2
            own = (lane < 64) == (a == 0)
            first = (1 - a) * 64
            one = jnp.where((lane >= first) & (lane < first + 3), 1.0, 0.0).astype(BF)
            cols = slice(p * 128, p * 128 + 128)
            s = dot(jnp.where(own, K[kb, :, cols], one), QTa[sec, h])
            if diagonal:
                s = jnp.where(key_at <= query_at, s, -1e30)
            return s, dot(jnp.where(own, V[kb, :, cols], one), dOTa[sec, h])

        def weigh(s, dp):
            probs = jnp.exp2(s)
            return probs.astype(BF), (probs * dp).astype(BF)

        def to_queries(h, d_s):
            acc[sec, h, 0:64, :] += dot(VTa[h, 0:64, :], d_s)

        def to_keys(p, first, second):
            cols = slice(p * 128, p * 128 + 128)
            q_pair, do_pair = Q[sec, :, cols], dO[sec, :, cols]
            zero = jnp.zeros_like(q_pair)
            low = lane < 64

            def stacked(pair):
                return jnp.concatenate(
                    [jnp.where(low, pair, zero), jnp.where(low, zero, pair)], axis=0
                )

            dva[:, cols] += dot(jnp.concatenate([first[0], second[0]], axis=1), stacked(do_pair))
            dka[:, cols] += dot(jnp.concatenate([first[1], second[1]], axis=1), stacked(q_pair))

        now = scores(0)
        done = []
        for n in range(HEADS + 1):
            later = scores(n + 1) if n + 1 < HEADS else None
            if n < HEADS:
                done.append(weigh(*now))
            if n > 0:
                to_queries(n - 1, done[n - 1][1])
                if n % 2 == 0:
                    to_keys(n // 2 - 1, done[n - 2], done[n - 1])
            now = later

    def relay(sec):
        arrived(rel_in.at[sec], dr.at[2 + sec])
        far_out[sec] = (far_out[sec].astype(F32) + rel_in[sec].astype(F32)).astype(BF)
        to(far_out.at[sec], far_in.at[sec], ds.at[4 + sec], dr.at[4 + sec], ctx=far).start()

    def send_back(i, owner_sec, dx):
        low = dx.astype(BF)

        @pl.when(i < 2)
        def _():
            rel_out[owner_sec] = low
            to(rel_out.at[owner_sec], rel_in.at[owner_sec], ds.at[2 + owner_sec], dr.at[2 + owner_sec], ctx=sib).start()

        @pl.when((i == 2) | (i == 3))
        def _():
            far_out[owner_sec] = low

        @pl.when(i >= 4)
        def _():
            sib_out[owner_sec] = low
            to(sib_out.at[owner_sec], sib_in.at[owner_sec], ds.at[owner_sec], dr.at[owner_sec], ctx=sib).start()

    def backward(i, _):
        owner_sec, owner, kb, sent, used = step_of(i)

        @pl.when(used)
        def _():
            kt = K[kb].astype(F32).T.astype(BF)
            for h in range(HEADS):
                VTa[h, 0:64, :] = kt[h * 64 : h * 64 + 64]
            dka[...] = jnp.zeros(dka.shape, F32)
            dva[...] = jnp.zeros(dva.shape, F32)

        def section(sec, _):
            qb = jnp.where(sec == 0, c, 7 - c)

            @pl.when(used & (kb < qb))
            def _():
                attend_back(sec, kb, False)

            @pl.when(used & (kb == qb))
            def _():
                attend_back(sec, kb, True)

            return 0

        lax.fori_loop(0, 2, section, 0)

        @pl.when(used)
        def _():
            both_low = jnp.concatenate([dka[...] * LN2, dva[...]], axis=1).astype(BF)
            dwkv[...] += dot(X[kb], both_low, 0, 0)
            sums[1:2, :] += column_sum(dva[...])

            @pl.when(i < 6)
            def _():
                send_back(i, owner_sec, dot(both_low, key_value_weight(), 1, 1))

            @pl.when(i >= 6)
            def _():
                K[kb] = both_low[:, :D]
                V[kb] = both_low[:, D:]

        @pl.when(i == 3)
        def _():
            relay(0)
            pl.when(chip == 0)(functools.partial(relay, 1))

        if ring:
            pl.when(i == 0)(functools.partial(reduce_y, 1))
            pl.when(i == 2)(functools.partial(reduce_z, 0, 0, 2))
            pl.when(i == 3)(functools.partial(reduce_z, 0, 2, 4))
            pl.when(i == 3)(functools.partial(reduce_z, 1, 0, 1))
            pl.when(i == 4)(functools.partial(reduce_z, 1, 1, 2))
            pl.when(i == 5)(functools.partial(reduce_z, 1, 2, 4))
            pl.when(i == 6)(functools.partial(reduce_x, 0))
        return 0

    lax.fori_loop(0, 8, backward, 0)

    by_owner(PK, dwkv[:, :D].astype(BF), 0)
    by_owner(PK, dwkv[:, D:].astype(BF), 32)
    if ring:
        reduce_core(2)

    def d_query(sec, _):
        dq = jnp.concatenate([acc[sec, h, 0:64, :] for h in range(HEADS)], axis=0)
        Q[sec] = (dq * SCALE).T.astype(BF)
        sums[0:1, :] += dot(ones, Q[sec])[0:1]
        return 0

    lax.fori_loop(0, 2, d_query, 0)
    xx = jnp.concatenate([X[c], X[7 - c]], axis=0)
    by_owner(PQ, dot(xx, both(Q), 0, 0).astype(BF), 0)
    for s in range(SHARDS):
        row = jnp.concatenate(
            [sums[:, s * 64 : s * 64 + 64], jnp.zeros((8, 448), F32)], axis=1
        )
        PQ[0, s % 2, s // 2, 32:48, :] = jnp.concatenate(
            [row, jnp.zeros((8, 512), F32)], axis=0
        ).astype(BF)
        row = jnp.concatenate(
            [sums_inner[:, s * 256 : s * 256 + 256], jnp.zeros((8, 256), F32)], axis=1
        )
        PQ[1, s % 2, s // 2, 32:48, :] = jnp.concatenate(
            [row, jnp.zeros((8, 512), F32)], axis=0
        ).astype(BF)
    if ring:
        reduce_core(3)
        reduce_y(2)
        reduce_y(3)
        reduce_last(0)
        reduce_x(1)

    def own_tokens(sec, _):
        kb = jnp.where(sec == 0, c, 7 - c)
        dR[sec] += (
            dot(Q[sec], weight(AT_QUERY), 1, 1)
            + dot(K[kb], weight(AT_KEY), 1, 1)
            + dot(V[kb], weight(AT_VALUE), 1, 1)
        )
        return 0

    lax.fori_loop(0, 2, own_tokens, 0)

    def add_incoming(ref, sem, sec):
        arrived(ref.at[sec], sem)
        dR[sec] += ref[sec].astype(F32)

    add_incoming(sib_in, dr.at[0], 0)
    pl.when(core == 1)(lambda: add_incoming(sib_in, dr.at[1], 1))
    add_incoming(far_in, dr.at[4], 0)
    pl.when(chip == 1)(lambda: add_incoming(far_in, dr.at[5], 1))
    for sec in range(2):
        tg_v[sec] = dR[sec].astype(BF)
    tg_copy = pltpu.make_async_copy(tg_v, tg_ref, out_sem.at[1])
    tg_copy.start()

    if ring:
        reduce_z(2)
        reduce_z(3)
        for u in range(6):
            gather_left(u)
        reduce_last(1)
        reduce_x(2)
        reduce_x(3)
        for g in range(2):
            reduce_end(g)
            finals[g].start()
        reduce_last(2)
        reduce_last(3)
        for g in range(2, 4):
            reduce_end(g)
            finals[g].start()
        for g in range(4):
            finals[g].wait()
    else:
        copies = [
            pltpu.make_async_copy(part, out, load_sem.at[k])
            for k, (part, out) in enumerate(((PU, pu_out), (PI, pi_out), (PK, pk_out), (PQ, pq_out)))
        ]
        for copy in copies:
            copy.start()
        for copy in copies:
            copy.wait()

    block = X.at[0]
    for k in range(3):
        left(block, xs.at[k])
    pl.when(chip == 1)(lambda: left(block, xs.at[3]))
    left(block, xs.at[4])
    pl.when(chip == 0)(lambda: left(block, xs.at[5]))
    left(block, ds.at[0])
    pl.when(core == 0)(lambda: left(block, ds.at[1]))
    left(block, ds.at[2])
    pl.when(chip == 0)(lambda: left(block, ds.at[3]))
    left(block, ds.at[4])
    pl.when(chip == 0)(lambda: left(block, ds.at[5]))
    out_copy.wait()
    tg_copy.wait()


def run(ring, tokens, cotangent, weights, smalls):
    blk = tokens.shape[1]
    vm = lambda *shape: pltpu.VMEM(shape, BF)
    vf = lambda *shape: pltpu.VMEM(shape, F32)
    dma = lambda *shape: pltpu.SemaphoreType.DMA(shape)
    any_spec = pl.BlockSpec(memory_space=pl.ANY)
    outs = [jax.ShapeDtypeStruct(tokens.shape, BF)] * 2
    out_specs = [any_spec] * 2
    if ring:
        outs += [jax.ShapeDtypeStruct((2, rows, D), BF) for rows in GROUP_ROWS]
        out_specs += [any_spec] * 4
    else:
        outs += [
            jax.ShapeDtypeStruct((2, 2, 4, rows, D), BF) for rows in GROUP_ROWS
        ]
        out_specs += [any_spec] * 4
    scratch = [vm(8, blk, D)] * 3
    scratch += [vm(4, 2, 2, PACKED, D)]
    scratch += [vf(8, D), vf(1, FF)]
    scratch += [vm(2, blk, D), vm(2, HEADS, 128, blk)] * 2
    scratch += [vm(HEADS, 80, blk)]
    scratch += [vf(2, HEADS, 8, blk), vf(2, HEADS, 80, blk), vm(2, D, blk)]
    scratch += [vm(2, blk, D), vf(2, blk, D), vf(2, blk, 1)]
    scratch += [vm(2, blk, FF)] * 2 + [vm(2, blk, D), vf(2, blk, D), vm(2, blk, D)]
    scratch += [vf(D, 2 * D)]
    scratch += [vf(8, D), vf(8, FF)]
    scratch += [vm(2, blk, D)]
    scratch += [vm(2, 2, 4, rows, D) for rows in GROUP_ROWS]
    scratch += [vm(2, blk, D)] * 3
    scratch += [dma(14), dma(2), dma(6), dma(8)]
    scratch += [dma(6), dma(6)]
    if ring:
        for rows in GROUP_ROWS:
            scratch += [vm(2, 4, rows, D), vm(4, rows, D), vm(3, rows, D)]
            scratch += [vm(rows, D), vm(rows, D), vm(2, rows, D)]
        scratch += [dma(6, 6), dma(6, 4), dma(6, 2), dma(6, 4), dma(6), dma(6, 2)]
        scratch += [dma(4, 11), dma(4, 11)]
    inputs = [tokens, cotangent, *weights, *smalls]
    return pl.pallas_call(
        functools.partial(layer, ring, blk),
        out_shape=outs,
        in_specs=[any_spec] * len(inputs),
        out_specs=out_specs,
        scratch_shapes=scratch,
        compiler_params=pltpu.CompilerParams(
            collective_id=0, has_side_effects=True, vmem_limit_bytes=63 << 20
        ),
        name="layer",
    )(*inputs)


def finish_kernel(out_in, tg_in, fu, fi, fk, fq, *refs):
    out_ref, tg_ref, gq, gk, gv, go, gi, gu = refs[:8]
    vectors, inner = refs[8:16], refs[16]
    sems = refs[17]
    copies = [
        pltpu.make_async_copy(out_in, out_ref, sems.at[0]),
        pltpu.make_async_copy(tg_in, tg_ref, sems.at[1]),
    ]
    for copy in copies:
        copy.start()
    for half in range(2):
        rows = slice(half * 32, half * 32 + 32)
        gu[half * 128 : half * 128 + 128, :] = fu[half].astype(F32)
        for cb in range(4):
            gi[rows, cb * 512 : cb * 512 + 512] = fi[half, cb * 32 : cb * 32 + 32, :].astype(F32)
        go[rows, :] = fi[half, 128:160, :].astype(F32)
        gq[rows, :] = fq[half, 0:32, :].astype(F32)
        gk[rows, :] = fk[half, 0:32, :].astype(F32)
        gv[rows, :] = fk[half, 32:64, :].astype(F32)
    small = fq[0, 32:48, 0:128].astype(F32)
    for j in range(8):
        vectors[j][...] = small[j : j + 1, 0:64]
    inner[...] = fq[1, 32:48, 0:256].astype(F32)[0:1]
    for copy in copies:
        copy.wait()


def finish_all(tokens, weights, res):
    any_spec = pl.BlockSpec(memory_space=pl.ANY)
    vmem_spec = pl.BlockSpec(memory_space=pltpu.VMEM)
    outs = [jax.ShapeDtypeStruct(tokens.shape, BF)] * 2
    outs += [jax.ShapeDtypeStruct(w.shape, F32) for w in weights]
    outs += [jax.ShapeDtypeStruct((1, 64), F32)] * 8
    outs += [jax.ShapeDtypeStruct((1, 256), F32)]
    return pl.pallas_call(
        finish_kernel,
        out_shape=outs,
        in_specs=[vmem_spec] * 6,
        out_specs=[any_spec] * 2 + [vmem_spec] * 15,
        scratch_shapes=[pltpu.SemaphoreType.DMA((2,))],
        name="finish",
    )(*res)


def shards(tokens, *rest):
    (wq, bq, wk, wv, bv, wo, bo, g1, s1, wi, bi, wu, bu, g2, s2, cotangent) = rest
    blk = tokens.shape[3]
    tok = tokens.reshape(2, blk, D)
    cot = cotangent.reshape(2, blk, D)
    weights = (wq, wk, wv, wo, wi, wu)
    vectors = (bq, bv, bo, g1, s1, bu, g2, s2)
    ring = lax.axis_size("fsdp") == SHARDS
    if ring:
        stacked = jnp.pad(jnp.stack(vectors), ((0, 8), (0, D - 64)))
        inner = jnp.pad(bi.reshape(1, 256), ((0, 15), (0, D - 256)))
        small = jnp.stack([stacked, inner])
        halves = [w.reshape(2, -1, D) for w in (wq, wk, wv)] + [small]
        halves += [wo.reshape(2, -1, D), wu.reshape(2, -1, D), wi.reshape(2, -1, FF)]
        res = run(True, tok, cot, halves, ())
        res = finish_all(tok, weights, res)
        output, tokens_grad, gq, gk, gv, go, gi, gu = res[:8]
        gvec = [v.reshape(64) for v in res[8:16]]
        gbi = res[16].reshape(256)
    else:
        gather = lambda w: lax.all_gather(w, "fsdp", axis=0, tiled=True)
        rows = lambda w: gather(w).reshape(4, 2, 2, -1, D)
        inner_rows = gather(wi).reshape(4, 2, 2, 32, 4, D).transpose(0, 1, 2, 4, 3, 5)
        unused = jnp.zeros((4, 2, 2, AT_OUT - AT_SMALL, D), BF)
        packed = [rows(wq), rows(wk), rows(wv), unused, rows(wo)]
        packed += [inner_rows.reshape(4, 2, 2, 128, D), rows(wu)]
        full = [jnp.concatenate(packed, axis=3)]
        vec = jnp.stack([gather(v).astype(F32) for v in vectors])
        inner = gather(bi).astype(F32).reshape(1, FF)
        output, tokens_grad, pu, pi, pk, pq = run(False, tok, cot, full, (vec, inner))

        def whole(part, rows):
            return part.transpose(2, 1, 0, 3, 4).reshape(SHARDS * 2 * rows, D)

        parts = [
            whole(pq[:, :, :, 0:32], 32),
            whole(pk[:, :, :, 0:32], 32),
            whole(pk[:, :, :, 32:64], 32),
            whole(pi[:, :, :, 128:160], 32),
            pi[:, :, :, 0:128]
            .reshape(2, 2, 4, 4, 32, D)
            .transpose(2, 1, 0, 4, 3, 5)
            .reshape(D, FF),
            whole(pu, 128),
        ]
        vecs = pq[0, :, :, 32:40, 0:64].transpose(2, 1, 0, 3).reshape(8, D)
        inner = pq[1, :, :, 32, 0:256].transpose(1, 0, 2).reshape(FF)
        parts += [vecs[j] for j in range(8)] + [inner]
        count = lax.axis_size("fsdp")
        packed = jnp.concatenate(
            [part.astype(F32).reshape(count, -1) for part in parts], axis=1
        ).reshape(-1)
        shares = lax.psum_scatter(packed, "fsdp", scatter_dimension=0, tiled=True)
        summed = lax.psum(shares.astype(BF), "ctx").astype(F32)
        pieces, at = [], 0
        for initial in weights + vectors + (bi,):
            pieces.append(summed[at : at + initial.size].reshape(initial.shape))
            at = at + initial.size
        gq, gk, gv, go, gi, gu = pieces[:6]
        gvec, gbi = pieces[6:14], pieces[14]
    order = (gq, gvec[0], gk, gv, gvec[1], go, gvec[2], gvec[3], gvec[4], gi, gbi, gu)
    order += (gvec[5], gvec[6], gvec[7])
    return (output.reshape(tokens.shape), tokens_grad.reshape(tokens.shape)) + order


def solution(mesh):
    row = P("fsdp", None)
    one = P("fsdp")
    act = P("fsdp", None, "ctx", None, None)
    params = (row, one, row, row, one, row, one, one, one, row, one, row, one, one, one)
    return jax.shard_map(
        shards,
        mesh=mesh,
        in_specs=(act,) + params + (act,),
        out_specs=(act, act) + params,
        check_vma=False,
    )
```

```python
import functools
import math

import jax
import jax.numpy as jnp
from jax import lax
from jax.experimental import pallas as pl
from jax.experimental.pallas import tpu as pltpu
from jax.sharding import PartitionSpec as P

HEADS = 8
HEAD = 64
D = 512
FF = 2048
CTX = 4
SHARDS = 8
EPS = 1e-5
BF = jnp.bfloat16
F32 = jnp.float32
QUERY_SCALE = math.log2(math.e) / math.sqrt(HEAD)
SCALE = 1.0 / math.sqrt(HEAD)
LN2 = math.log(2.0)
AT_QUERY, AT_KEY, AT_VALUE, AT_SMALL, AT_OUT, AT_INNER, AT_OUTER, PACKED = 0, 32, 64, 96, 112, 144, 272, 400
UNITS = ((0, 32), (32, 64), (64, 112), (112, 208), (208, 304), (304, 400))
GATHER_AT = ((0, 3, 1), (1, 4, 1), (2, 5, 1), (4, 3, 2), (5, 4, 2), (7, 5, 2), (8, 3, 3), (10, 4, 3), (12, 5, 3), (13, 3, 0), (15, 4, 0))
GROUP_ROWS = (128, 160, 64, 48)


def dot(left, right, left_dim=1, right_dim=0):
    return lax.dot_general(
        left, right, (((left_dim,), (right_dim,)), ((), ())), preferred_element_type=F32
    )


def rows_mean(value):
    return jnp.mean(value, axis=-1, keepdims=True)


def layer(ring, blk, *refs):
    it = iter(refs)
    take = lambda count: [next(it) for _ in range(count)]
    tok, cot = take(2)
    weights_in = take(7 if ring else 1)
    small_in = take(0 if ring else 2)
    out_ref, tg_ref = take(2)
    if ring:
        finals_out = take(4)
    else:
        pu_out, pi_out, pk_out, pq_out = take(4)
    X, K, V = take(3)
    W = next(it)
    vec, vec_inner = take(2)
    Q, QTa, dO, dOTa = take(4)
    VTa = next(it)
    top, acc, OT = take(3)
    Hlow, n1, rstd1 = take(3)
    Z, dU, dF, dR, dA = take(5)
    dwkv = next(it)
    dka, dva = n1.at[0], n1.at[1]
    sums, sums_inner = take(2)
    cot_v = next(it)
    tg_v = dO
    PU, PI, PK, PQ = take(4)
    sib_in, rel_in, far_in = take(3)
    sib_out, rel_out, far_out = dA, dF, Hlow
    load_sem, out_sem, xs, xr = take(4)
    ds, dr = take(2)
    if ring:
        buffers = [take(6) for _ in range(4)]
        zs, ys, cs, rz, ry, rc, gs, gr = take(8)

    t = lax.axis_index("ctx")
    chip, core = t // 2, lax.rem(t, 2)
    sib = t + 1 - 2 * core
    far = lax.rem(t + 2, 4)
    c = t
    MESH = pl.DeviceIdType.MESH

    def to(ref, dst, send, recv, **where):
        return pltpu.make_async_remote_copy(
            src_ref=ref,
            dst_ref=dst,
            send_sem=send,
            recv_sem=recv,
            device_id=where,
            device_id_type=MESH,
        )

    def arrived(ref, sem):
        pltpu.make_async_copy(ref, ref, sem).wait()

    def left(ref, sem):
        pltpu.make_async_copy(ref, ref, sem).wait()

    peers = [{"ctx": sib}, {"ctx": far}]
    if ring:
        f = lax.axis_index("fsdp")
        z, y = f // 2, lax.rem(f, 2)
        fy = f + 1 - 2 * y
        zpeer = [lax.rem(z + dz, 4) * 2 + y for dz in (1, 2, 3)]
        peers += [{"fsdp": fy}] + [{"fsdp": zp} for zp in zpeer]

    own_blocks = [c, 7 - c]
    loads = []
    for sec in range(2):
        loads.append(
            pltpu.make_async_copy(tok.at[sec], X.at[own_blocks[sec]], load_sem.at[sec])
        )
        loads.append(
            pltpu.make_async_copy(cot.at[sec], cot_v.at[sec], load_sem.at[2 + sec])
        )
    if ring:
        for w, at in enumerate((AT_QUERY, AT_KEY, AT_VALUE, AT_SMALL, AT_OUT, AT_OUTER)):
            src = weights_in[w].at[core]
            loads.append(
                pltpu.make_async_copy(
                    src, W.at[z, y, core, pl.ds(at, src.shape[0])], load_sem.at[4 + w]
                )
            )
        for cb in range(4):
            src = weights_in[6].at[core, :, pl.ds(cb * D, D)]
            loads.append(
                pltpu.make_async_copy(
                    src, W.at[z, y, core, pl.ds(AT_INNER + cb * 32, 32)], load_sem.at[10 + cb]
                )
            )
    else:
        loads.append(pltpu.make_async_copy(weights_in[0], W, load_sem.at[4]))
        loads.append(pltpu.make_async_copy(small_in[0], vec, load_sem.at[5]))
        loads.append(pltpu.make_async_copy(small_in[1], vec_inner, load_sem.at[6]))
    for copy in loads:
        copy.start()

    barrier = pltpu.get_barrier_semaphore()
    for where in peers:
        pl.semaphore_signal(barrier, inc=1, device_id=where, device_id_type=MESH)
    pl.semaphore_wait(barrier, len(peers))

    for sec in range(2):
        b = own_blocks[sec]
        to(tok.at[sec], X.at[b], xs.at[sec], xr.at[b], ctx=sib).start()
    to(tok.at[0], X.at[c], xs.at[2], xr.at[c], ctx=far).start()

    @pl.when(chip == 1)
    def _():
        to(tok.at[1], X.at[7 - c], xs.at[3], xr.at[7 - c], ctx=far).start()

    if ring:
        def piece(u, zz, yy, half):
            first, last = UNITS[u]
            return W.at[zz, yy, half, pl.ds(first, last - first)]

        def pieces(u, yy, half):
            first, last = UNITS[u]
            return W.at[:, yy, half, pl.ds(first, last - first)]

        def gather_start(u):
            ref = piece(u, z, y, core)
            to(ref, ref, ys.at[u, z], ry.at[u], fsdp=fy).start()
            pl.when(z < 3)(lambda: to(ref, ref, zs.at[u, 4], rz.at[u, z], fsdp=f + 2).start())
            pl.when(z > 0)(lambda: to(ref, ref, zs.at[u, 5], rz.at[u, z], fsdp=f - 2).start())

        def gather_z(u, hops):
            def pass_on(zz, more, onward):
                ref = piece(u, zz, y, core)
                arrived(ref, rz.at[u, zz])
                if hops < 3:
                    pl.when(more)(lambda: to(ref, ref, zs.at[u, zz], rz.at[u, zz], fsdp=onward).start())
                to(ref, ref, ys.at[u, zz], ry.at[u], fsdp=fy).start()

            pl.when(z - hops >= 0)(lambda: pass_on(z - hops, z < 3, f + 2))
            pl.when(z + hops <= 3)(lambda: pass_on(z + hops, z > 0, f - 2))
            if hops == 3:
                ref = pieces(u, y, core)
                to(ref, ref, cs.at[u, 0], rc.at[u, 0], ctx=sib).start()

        def gather_y(u):
            ref = pieces(u, 1 - y, core)
            arrived(ref, ry.at[u])
            to(ref, ref, cs.at[u, 1], rc.at[u, 1], ctx=sib).start()

        def gather_end(u):
            arrived(pieces(u, y, 1 - core), rc.at[u, 0])
            arrived(pieces(u, 1 - y, 1 - core), rc.at[u, 1])

        def gather_left(u):
            ref = piece(u, 0, 0, 0)
            pl.when(z < 3)(lambda: left(ref, zs.at[u, 4]))
            pl.when(z > 0)(lambda: left(ref, zs.at[u, 5]))
            for zz in range(4):
                onward = ((zz < z) & (z < 3)) | ((zz > z) & (z > 0))
                pl.when(onward)(lambda zz=zz: left(ref, zs.at[u, zz]))
                left(ref, ys.at[u, zz])
            for i in range(2):
                left(pieces(u, 0, 0), cs.at[u, i])

        for copy in loads[4:]:
            copy.wait()
        for u in range(3):
            gather_start(u)
        for hops in (1, 2, 3):
            for u in range(3):
                gather_z(u, hops)
        for u in range(3, 6):
            gather_start(u)
    else:
        for copy in loads[4:]:
            copy.wait()

    def far_tokens():
        b = far
        arrived(X.at[b], xr.at[b])
        to(X.at[b], X.at[b], xs.at[4], xr.at[b], ctx=sib).start()

        @pl.when(chip == 0)
        def _():
            b = 7 - far
            arrived(X.at[b], xr.at[b])
            to(X.at[b], X.at[b], xs.at[5], xr.at[b], ctx=sib).start()

    if ring:
        for u in range(3):
            gather_y(u)
        for u in range(3):
            gather_end(u)
        small = [[W[s // 2, s % 2, half, AT_SMALL:AT_OUT, :].astype(F32) for s in range(SHARDS)] for half in range(2)]
        vec[...] = jnp.concatenate([part[0:8, 0:64] for part in small[0]], axis=1)
        vec_inner[...] = jnp.concatenate([part[0:1, 0:256] for part in small[1]], axis=1)

    def weight(at, rows=32):
        return W[:, :, :, at : at + rows, :].reshape(SHARDS * 2 * rows, D)

    def key_value_weight():
        return jnp.concatenate([weight(AT_KEY), weight(AT_VALUE)], axis=1)

    b_query, b_value, b_out, gain1, shift1, b_outer, gain2, shift2 = (
        vec[pl.ds(j, 1), :] for j in range(8)
    )
    for sec in range(2):
        loads[2 * sec].wait()

    VTa[:, 64:80, :] = jnp.ones((HEADS, 16, blk), BF)
    for h in range(HEADS):
        other = (1 - h % 2) * 64
        for sec in range(2):
            QTa[sec, h, other : other + 64, :] = jnp.zeros((64, blk), BF)
            dOTa[sec, h, other : other + 64, :] = jnp.zeros((64, blk), BF)

    def queries(sec, _):
        x = X[jnp.where(sec == 0, c, 7 - c)]
        q = (dot(x, weight(AT_QUERY)) + b_query) * QUERY_SCALE
        Q[sec] = q.astype(BF)
        qt = q.T.astype(BF)
        for h in range(HEADS):
            own = (h % 2) * 64
            QTa[sec, h, own : own + 64, :] = qt[h * 64 : h * 64 + 64]
        return 0

    lax.fori_loop(0, 2, queries, 0)

    lane = lax.broadcasted_iota(jnp.int32, (blk, 128), 1)
    key_at = lax.broadcasted_iota(jnp.int32, (blk, blk), 0)
    query_at = lax.broadcasted_iota(jnp.int32, (blk, blk), 1)

    def step_of(i):
        sec = lax.rem(i, 2)
        owner_core = jnp.where(i < 2, 1 - core, core)
        owner = jnp.where(i < 4, 2 * (1 - chip) + owner_core, jnp.where(i < 6, sib, t))
        kb = jnp.where(sec == 0, owner, 7 - owner)
        sent = (i >= 4) | (chip == 0) | (sec == 0)
        return sec, owner, kb, sent, sent & (kb <= 7 - c)

    top[...] = jnp.full(top.shape, -1e30, F32)
    acc[...] = jnp.zeros(acc.shape, F32)

    def attend(sec, kb, diagonal):
        def scores(h):
            p, a = h // 2, h % 2
            k_pair = K[kb, :, p * 128 : p * 128 + 128]
            k_head = jnp.where((lane < 64) == (a == 0), k_pair, jnp.zeros_like(k_pair))
            s = dot(k_head, QTa[sec, h])
            if diagonal:
                s = jnp.where(key_at <= query_at, s, -1e30)
            return s

        def weigh(h, s):
            old = top[sec, h, 0:1, :]
            new = jnp.maximum(old, jnp.max(s, axis=0, keepdims=True))
            top[sec, h] = jnp.broadcast_to(new, (8, blk))
            return jnp.exp2(s - new).astype(BF), jnp.exp2(old - new)

        def gather_values(h, probs, shrink):
            acc[sec, h] = acc[sec, h] * shrink + dot(VTa[h], probs)

        s = scores(0)
        held = None
        for h in range(HEADS):
            later = scores(h + 1) if h + 1 < HEADS else None
            now = (h, *weigh(h, s))
            if held is not None:
                gather_values(*held)
            held, s = now, later
        gather_values(*held)

    def keys_values(kb):
        x = X[kb]
        kv = dot(x, key_value_weight())
        K[kb] = kv[:, :D].astype(BF)
        v = kv[:, D:] + b_value
        V[kb] = v.astype(BF)
        vt = v.T.astype(BF)
        for h in range(HEADS):
            VTa[h, 0:64, :] = vt[h * 64 : h * 64 + 64]

    def forward(n, _):
        i = jnp.where(n < 2, 6 + n, jnp.where(n < 4, 2 + n, jnp.where(n < 6, n - 2, n - 6)))
        _, _, kb, sent, used = step_of(i)

        @pl.when(n == 4)
        def _():
            far_tokens()

        @pl.when(sent & ((n == 2) | (n == 3) | (n >= 6)))
        def _():
            arrived(X.at[kb], xr.at[kb])

        @pl.when(used)
        def _():
            keys_values(kb)

        def section(sec, _):
            qb = jnp.where(sec == 0, c, 7 - c)
            if ring:
                for at, u, hops in GATHER_AT:
                    if hops:
                        pl.when(2 * n + sec == at)(functools.partial(gather_z, u, hops))
                    else:
                        pl.when(2 * n + sec == at)(functools.partial(gather_y, u))

            @pl.when(used & (kb < qb))
            def _():
                attend(sec, kb, False)

            @pl.when(used & (kb == qb))
            def _():
                attend(sec, kb, True)

            return 0

        lax.fori_loop(0, 2, section, 0)
        return 0

    lax.fori_loop(0, 8, forward, 0)

    def finish(sec, _):
        for h in range(HEADS):
            other = (1 - h % 2) * 64
            total = acc[sec, h, 64:65, :]
            OT[sec, h * 64 : h * 64 + 64, :] = (acc[sec, h, 0:64, :] / total).astype(BF)
            low = -(top[sec, h, 0:1, :] + jnp.log2(total))
            parts = []
            for _ in range(3):
                parts.append(low.astype(BF))
                low = low - parts[-1].astype(F32)
            QTa[sec, h, other : other + 16, :] = jnp.concatenate(
                parts + [jnp.zeros((13, blk), BF)], axis=0
            )
        return 0

    if ring:
        gather_y(5)
    lax.fori_loop(0, 2, finish, 0)
    if ring:
        gather_end(3)
    for sec in range(2):
        loads[2 * sec + 1].wait()

    sums[...] = jnp.zeros(sums.shape, F32)
    sums_inner[...] = jnp.zeros(sums_inner.shape, F32)
    ones = jnp.ones((16, blk), BF)

    def column_sum(value):
        return jnp.sum(value, axis=0, keepdims=True)

    def dense(sec):
        x = X[own_blocks[sec]].astype(F32)
        r1 = x + dot(OT[sec], weight(AT_OUT), 0, 0) + b_out
        yield
        center = r1 - rows_mean(r1)
        rs1 = lax.rsqrt(rows_mean(center * center) + EPS)
        n1[sec] = center * rs1
        rstd1[sec] = rs1
        Hlow[sec] = (n1[sec] * gain1 + shift1).astype(BF)
        yield
        c0 = math.sqrt(2.0 / math.pi)
        columns = [slice(cb * 512, cb * 512 + 512) for cb in range(4)]

        def hidden(cb):
            if ring and sec == 0 and cb == 2:
                gather_end(4)
            return dot(Hlow[sec], weight(AT_INNER + 32 * cb)) + vec_inner[:, columns[cb]]

        u = hidden(0)
        for cb in range(4):
            later = hidden(cb + 1) if cb < 3 else None
            uu = u * u
            th = jnp.tanh(c0 * u * (1.0 + 0.044715 * uu))
            half = 0.5 * (1.0 + th)
            Z[sec, :, columns[cb]] = (u * half).astype(BF)
            slope = half + 0.5 * u * (1.0 - th * th) * (c0 * (1.0 + 3 * 0.044715 * uu))
            dU[sec, :, columns[cb]] = slope.astype(BF)
            u = later
        yield
        if ring and sec == 0:
            gather_end(5)
        r2 = n1[sec] * gain1 + shift1 + dot(Z[sec], weight(AT_OUTER, 128)) + b_outer
        yield
        center = r2 - rows_mean(r2)
        rs2 = lax.rsqrt(rows_mean(center * center) + EPS)
        n2 = center * rs2
        g = cot_v[sec].astype(F32)
        cot_v[sec] = (n2 * gain2 + shift2).astype(BF)
        sums[6:7, :] += column_sum(g * n2)
        sums[7:8, :] += column_sum(g)
        g = g * gain2
        d_r2 = (g - rows_mean(g) - n2 * rows_mean(g * n2)) * rs2
        dR[sec] = d_r2
        d_f = d_r2.astype(BF)
        dF[sec] = d_f
        sums[5:6, :] += dot(ones, d_f)[0:1]
        yield

        def d_active(cb):
            rows = W[cb, :, :, AT_OUTER:PACKED, :].reshape(D, D)
            return dot(dF[sec], rows, 1, 1)

        now = d_active(0)
        for cb in range(4):
            later = d_active(cb + 1) if cb < 3 else None
            d_u = (now * dU[sec, :, columns[cb]].astype(F32)).astype(BF)
            dU[sec, :, columns[cb]] = d_u
            sums_inner[0:1, columns[cb]] += dot(ones, d_u)[0:1]
            now = later
        yield
        inner = jnp.concatenate([weight(AT_INNER + 32 * cb) for cb in range(4)], axis=1)
        d_h = dR[sec] + dot(dU[sec], inner, 1, 1)
        yield
        nn1 = n1[sec]
        sums[3:4, :] += column_sum(d_h * nn1)
        sums[4:5, :] += column_sum(d_h)
        g = d_h * gain1
        d_r1 = (g - rows_mean(g) - nn1 * rows_mean(g * nn1)) * rstd1[sec]
        dR[sec] = d_r1
        d_a = d_r1.astype(BF)
        dA[sec] = d_a
        sums[2:3, :] += dot(ones, d_a)[0:1]
        yield
        dO[sec] = dot(dA[sec], weight(AT_OUT), 1, 1).astype(BF)
        d_ot = dot(weight(AT_OUT), dA[sec], 1, 1)
        yield
        for h in range(HEADS):
            own, other = (h % 2) * 64, (1 - h % 2) * 64
            part = d_ot[h * 64 : h * 64 + 64].astype(BF)
            dOTa[sec, h, own : own + 64, :] = part
            o = OT[sec, h * 64 : h * 64 + 64, :].astype(F32)
            rest = -column_sum(part.astype(F32) * o)
            parts = []
            for _ in range(3):
                parts.append(rest.astype(BF))
                rest = rest - parts[-1].astype(F32)
            dOTa[sec, h, other : other + 16, :] = jnp.concatenate(
                parts + [jnp.zeros((13, blk), BF)], axis=0
            )

    sections = [dense(0), dense(1)]

    def advance(stages):
        for _ in range(stages):
            for work in sections:
                next(work, 0)

    advance(5)

    @pl.when(t >= 0)
    def _():
        advance(6)

    out_copy = pltpu.make_async_copy(cot_v, out_ref, out_sem.at[0])
    out_copy.start()

    if ring:
        groups = [(mine, *more) for mine, more in zip((PU, PI, PK, PQ), buffers)]

        finals = [
            pltpu.make_async_copy(groups[g][6], finals_out[g], load_sem.at[g]) for g in range(4)
        ]

        def add_into(dst, *terms):
            total = dst[...].astype(F32)
            for term in terms:
                total = total + term[...].astype(F32)
            dst[...] = total.astype(BF)

        def reduce_core(g):
            mine, from_core = groups[g][:2]
            for k, yy in ((0, 1 - y), (1, y)):
                to(mine.at[1 - core, yy], from_core.at[k], gs.at[g, k], gr.at[g, k], ctx=sib).start()

        def reduce_y(g):
            mine, from_core, from_y = groups[g][:3]
            arrived(from_core.at[0], gr.at[g, 0])

            def body(n, _):
                k = lax.rem(z + 1 + n, 4)
                add_into(mine.at[core, 1 - y, k], from_core.at[0, k])
                to(mine.at[core, 1 - y, k], from_y.at[k], gs.at[g, 2 + n], gr.at[g, 2 + n], fsdp=fy).start()
                return 0

            lax.fori_loop(0, 4, body, 0)

        def reduce_z(g, first=0, last=4):
            mine, from_core, from_y, from_z = groups[g][:4]
            if first == 0:
                arrived(from_core.at[1], gr.at[g, 1])

            def body(n, _):
                k = lax.rem(z + 1 + n, 4)
                arrived(from_y.at[k], gr.at[g, 2 + n])
                add_into(mine.at[core, y, k], from_core.at[1, k], from_y.at[k])

                @pl.when(n < 3)
                def _():
                    to(mine.at[core, y, k], from_z.at[n], gs.at[g, 6 + n], gr.at[g, 6 + n], fsdp=k * 2 + y).start()

                return 0

            lax.fori_loop(first, last, body, 0)

        def reduce_x(g):
            mine, _, _, from_z, pair, from_x, _ = groups[g]
            for i in range(3):
                arrived(from_z.at[i], gr.at[g, 6 + i])
            pair[...] = (
                mine[core, y, z].astype(F32)
                + from_z[0].astype(F32)
                + from_z[1].astype(F32)
                + from_z[2].astype(F32)
            ).astype(BF)
            to(pair, from_x, gs.at[g, 9], gr.at[g, 9], ctx=far).start()

        def reduce_last(g):
            pair, from_x, final = groups[g][4:]
            arrived(from_x, gr.at[g, 9])
            final[core] = (pair[...].astype(F32) + from_x[...].astype(F32)).astype(BF)
            to(final.at[core], final.at[core], gs.at[g, 10], gr.at[g, 10], ctx=sib).start()

        def reduce_end(g):
            mine, from_core, from_y, from_z, pair, from_x, final = groups[g]
            arrived(final.at[1 - core], gr.at[g, 10])
            for k in range(2):
                left(from_core.at[k], gs.at[g, k])
            for i in range(4):
                left(from_y.at[0], gs.at[g, 2 + i])
            for i in range(3):
                left(from_z.at[i], gs.at[g, 6 + i])
            left(pair, gs.at[g, 9])
            left(final.at[0], gs.at[g, 10])

    def both(ref, cols=slice(None)):
        return jnp.concatenate([ref[0, :, cols], ref[1, :, cols]], axis=0)

    for rb in range(4):
        part = dot(both(Z, slice(rb * 512, rb * 512 + 512)), both(dF), 0, 0).astype(BF)
        for k in range(4):
            s, half = 2 * rb + k // 2, k % 2
            PU[half, s % 2, s // 2] = part[k * 128 : k * 128 + 128]
    if ring:
        reduce_core(0)
    for cb in range(4):
        part = dot(both(Hlow), both(dU, slice(cb * 512, cb * 512 + 512)), 0, 0).astype(BF)
        for s in range(SHARDS):
            for half in range(2):
                at = s * 64 + half * 32
                PI[half, s % 2, s // 2, cb * 32 : cb * 32 + 32, :] = part[at : at + 32]

    def by_owner(dst, value, row):
        for s in range(SHARDS):
            for half in range(2):
                at = s * 64 + half * 32
                dst[half, s % 2, s // 2, row : row + 32, :] = value[at : at + 32]

    ot = jnp.concatenate([OT[0], OT[1]], axis=1)
    by_owner(PI, dot(ot, both(dA)).astype(BF), 128)

    if ring:
        reduce_core(1)
        reduce_y(0)

    acc[...] = jnp.zeros(acc.shape, F32)
    dwkv[...] = jnp.zeros(dwkv.shape, F32)

    def attend_back(sec, kb, diagonal):
        def scores(h):
            p, a = h // 2, h % 2
            own = (lane < 64) == (a == 0)
            first = (1 - a) * 64
            one = jnp.where((lane >= first) & (lane < first + 3), 1.0, 0.0).astype(BF)
            cols = slice(p * 128, p * 128 + 128)
            s = dot(jnp.where(own, K[kb, :, cols], one), QTa[sec, h])
            if diagonal:
                s = jnp.where(key_at <= query_at, s, -1e30)
            return s, dot(jnp.where(own, V[kb, :, cols], one), dOTa[sec, h])

        def weigh(s, dp):
            probs = jnp.exp2(s)
            return probs.astype(BF), (probs * dp).astype(BF)

        def to_queries(h, d_s):
            acc[sec, h, 0:64, :] += dot(VTa[h, 0:64, :], d_s)

        def to_keys(p, first, second):
            cols = slice(p * 128, p * 128 + 128)
            q_pair, do_pair = Q[sec, :, cols], dO[sec, :, cols]
            zero = jnp.zeros_like(q_pair)
            low = lane < 64

            def stacked(pair):
                return jnp.concatenate(
                    [jnp.where(low, pair, zero), jnp.where(low, zero, pair)], axis=0
                )

            dva[:, cols] += dot(jnp.concatenate([first[0], second[0]], axis=1), stacked(do_pair))
            dka[:, cols] += dot(jnp.concatenate([first[1], second[1]], axis=1), stacked(q_pair))

        now = scores(0)
        done = []
        for n in range(HEADS + 1):
            later = scores(n + 1) if n + 1 < HEADS else None
            if n < HEADS:
                done.append(weigh(*now))
            if n > 0:
                to_queries(n - 1, done[n - 1][1])
                if n % 2 == 0:
                    to_keys(n // 2 - 1, done[n - 2], done[n - 1])
            now = later

    def relay(sec):
        arrived(rel_in.at[sec], dr.at[2 + sec])
        far_out[sec] = (far_out[sec].astype(F32) + rel_in[sec].astype(F32)).astype(BF)
        to(far_out.at[sec], far_in.at[sec], ds.at[4 + sec], dr.at[4 + sec], ctx=far).start()

    def send_back(i, owner_sec, dx):
        low = dx.astype(BF)

        @pl.when(i < 2)
        def _():
            rel_out[owner_sec] = low
            to(rel_out.at[owner_sec], rel_in.at[owner_sec], ds.at[2 + owner_sec], dr.at[2 + owner_sec], ctx=sib).start()

        @pl.when((i == 2) | (i == 3))
        def _():
            far_out[owner_sec] = low

        @pl.when(i >= 4)
        def _():
            sib_out[owner_sec] = low
            to(sib_out.at[owner_sec], sib_in.at[owner_sec], ds.at[owner_sec], dr.at[owner_sec], ctx=sib).start()

    def backward(i, _):
        owner_sec, owner, kb, sent, used = step_of(i)

        @pl.when(used)
        def _():
            kt = K[kb].astype(F32).T.astype(BF)
            for h in range(HEADS):
                VTa[h, 0:64, :] = kt[h * 64 : h * 64 + 64]
            dka[...] = jnp.zeros(dka.shape, F32)
            dva[...] = jnp.zeros(dva.shape, F32)

        def section(sec, _):
            qb = jnp.where(sec == 0, c, 7 - c)

            @pl.when(used & (kb < qb))
            def _():
                attend_back(sec, kb, False)

            @pl.when(used & (kb == qb))
            def _():
                attend_back(sec, kb, True)

            return 0

        lax.fori_loop(0, 2, section, 0)

        @pl.when(used)
        def _():
            both_low = jnp.concatenate([dka[...] * LN2, dva[...]], axis=1).astype(BF)
            dwkv[...] += dot(X[kb], both_low, 0, 0)
            sums[1:2, :] += column_sum(dva[...])

            @pl.when(i < 6)
            def _():
                send_back(i, owner_sec, dot(both_low, key_value_weight(), 1, 1))

            @pl.when(i >= 6)
            def _():
                K[kb] = both_low[:, :D]
                V[kb] = both_low[:, D:]

        @pl.when(i == 3)
        def _():
            relay(0)
            pl.when(chip == 0)(functools.partial(relay, 1))

        if ring:
            pl.when(i == 0)(functools.partial(reduce_y, 1))
            pl.when(i == 2)(functools.partial(reduce_z, 0, 0, 2))
            pl.when(i == 3)(functools.partial(reduce_z, 0, 2, 4))
            pl.when(i == 3)(functools.partial(reduce_z, 1, 0, 1))
            pl.when(i == 4)(functools.partial(reduce_z, 1, 1, 2))
            pl.when(i == 5)(functools.partial(reduce_z, 1, 2, 4))
            pl.when(i == 6)(functools.partial(reduce_x, 0))
        return 0

    lax.fori_loop(0, 8, backward, 0)

    by_owner(PK, dwkv[:, :D].astype(BF), 0)
    by_owner(PK, dwkv[:, D:].astype(BF), 32)
    if ring:
        reduce_core(2)

    def d_query(sec, _):
        dq = jnp.concatenate([acc[sec, h, 0:64, :] for h in range(HEADS)], axis=0)
        Q[sec] = (dq * SCALE).T.astype(BF)
        sums[0:1, :] += dot(ones, Q[sec])[0:1]
        return 0

    lax.fori_loop(0, 2, d_query, 0)
    if ring:
        reduce_y(2)
    xx = jnp.concatenate([X[c], X[7 - c]], axis=0)
    by_owner(PQ, dot(xx, both(Q), 0, 0).astype(BF), 0)
    for s in range(SHARDS):
        row = jnp.concatenate(
            [sums[:, s * 64 : s * 64 + 64], jnp.zeros((8, 448), F32)], axis=1
        )
        PQ[0, s % 2, s // 2, 32:48, :] = jnp.concatenate(
            [row, jnp.zeros((8, 512), F32)], axis=0
        ).astype(BF)
        row = jnp.concatenate(
            [sums_inner[:, s * 256 : s * 256 + 256], jnp.zeros((8, 256), F32)], axis=1
        )
        PQ[1, s % 2, s // 2, 32:48, :] = jnp.concatenate(
            [row, jnp.zeros((8, 512), F32)], axis=0
        ).astype(BF)
    if ring:
        reduce_core(3)
        reduce_y(3)
        reduce_last(0)
        reduce_x(1)

    def own_tokens(sec, _):
        kb = jnp.where(sec == 0, c, 7 - c)
        dR[sec] += (
            dot(Q[sec], weight(AT_QUERY), 1, 1)
            + dot(K[kb], weight(AT_KEY), 1, 1)
            + dot(V[kb], weight(AT_VALUE), 1, 1)
        )
        return 0

    lax.fori_loop(0, 2, own_tokens, 0)

    def add_incoming(ref, sem, sec):
        arrived(ref.at[sec], sem)
        dR[sec] += ref[sec].astype(F32)

    add_incoming(sib_in, dr.at[0], 0)
    pl.when(core == 1)(lambda: add_incoming(sib_in, dr.at[1], 1))
    add_incoming(far_in, dr.at[4], 0)
    pl.when(chip == 1)(lambda: add_incoming(far_in, dr.at[5], 1))
    for sec in range(2):
        tg_v[sec] = dR[sec].astype(BF)
    tg_copy = pltpu.make_async_copy(tg_v, tg_ref, out_sem.at[1])
    tg_copy.start()

    block = X.at[0]
    for k in range(3):
        left(block, xs.at[k])
    pl.when(chip == 1)(lambda: left(block, xs.at[3]))
    left(block, xs.at[4])
    pl.when(chip == 0)(lambda: left(block, xs.at[5]))
    left(block, ds.at[0])
    pl.when(core == 0)(lambda: left(block, ds.at[1]))
    left(block, ds.at[2])
    pl.when(chip == 0)(lambda: left(block, ds.at[3]))
    left(block, ds.at[4])
    pl.when(chip == 0)(lambda: left(block, ds.at[5]))
    if ring:
        for u in range(6):
            gather_left(u)

    if ring:
        reduce_z(2)
        reduce_z(3)
        reduce_last(1)
        reduce_x(2)
        reduce_x(3)
        for g in range(2):
            reduce_end(g)
            finals[g].start()
        reduce_last(2)
        reduce_last(3)
        for g in range(2, 4):
            reduce_end(g)
            finals[g].start()
        for g in range(4):
            finals[g].wait()
    else:
        copies = [
            pltpu.make_async_copy(part, out, load_sem.at[k])
            for k, (part, out) in enumerate(((PU, pu_out), (PI, pi_out), (PK, pk_out), (PQ, pq_out)))
        ]
        for copy in copies:
            copy.start()
        for copy in copies:
            copy.wait()

    out_copy.wait()
    tg_copy.wait()


def run(ring, tokens, cotangent, weights, smalls):
    blk = tokens.shape[1]
    vm = lambda *shape: pltpu.VMEM(shape, BF)
    vf = lambda *shape: pltpu.VMEM(shape, F32)
    dma = lambda *shape: pltpu.SemaphoreType.DMA(shape)
    any_spec = pl.BlockSpec(memory_space=pl.ANY)
    outs = [jax.ShapeDtypeStruct(tokens.shape, BF)] * 2
    out_specs = [any_spec] * 2
    if ring:
        outs += [jax.ShapeDtypeStruct((2, rows, D), BF) for rows in GROUP_ROWS]
        out_specs += [any_spec] * 4
    else:
        outs += [
            jax.ShapeDtypeStruct((2, 2, 4, rows, D), BF) for rows in GROUP_ROWS
        ]
        out_specs += [any_spec] * 4
    scratch = [vm(8, blk, D)] * 3
    scratch += [vm(4, 2, 2, PACKED, D)]
    scratch += [vf(8, D), vf(1, FF)]
    scratch += [vm(2, blk, D), vm(2, HEADS, 128, blk)] * 2
    scratch += [vm(HEADS, 80, blk)]
    scratch += [vf(2, HEADS, 8, blk), vf(2, HEADS, 80, blk), vm(2, D, blk)]
    scratch += [vm(2, blk, D), vf(2, blk, D), vf(2, blk, 1)]
    scratch += [vm(2, blk, FF)] * 2 + [vm(2, blk, D), vf(2, blk, D), vm(2, blk, D)]
    scratch += [vf(D, 2 * D)]
    scratch += [vf(8, D), vf(8, FF)]
    scratch += [vm(2, blk, D)]
    scratch += [vm(2, 2, 4, rows, D) for rows in GROUP_ROWS]
    scratch += [vm(2, blk, D)] * 3
    scratch += [dma(14), dma(2), dma(6), dma(8)]
    scratch += [dma(6), dma(6)]
    if ring:
        for rows in GROUP_ROWS:
            scratch += [vm(2, 4, rows, D), vm(4, rows, D), vm(3, rows, D)]
            scratch += [vm(rows, D), vm(rows, D), vm(2, rows, D)]
        scratch += [dma(6, 6), dma(6, 4), dma(6, 2), dma(6, 4), dma(6), dma(6, 2)]
        scratch += [dma(4, 11), dma(4, 11)]
    inputs = [tokens, cotangent, *weights, *smalls]
    return pl.pallas_call(
        functools.partial(layer, ring, blk),
        out_shape=outs,
        in_specs=[any_spec] * len(inputs),
        out_specs=out_specs,
        scratch_shapes=scratch,
        compiler_params=pltpu.CompilerParams(
            collective_id=0, has_side_effects=True, vmem_limit_bytes=63 << 20
        ),
        name="layer",
    )(*inputs)


def finish_kernel(out_in, tg_in, fu, fi, fk, fq, *refs):
    out_ref, tg_ref, gq, gk, gv, go, gi, gu = refs[:8]
    vectors, inner = refs[8:16], refs[16]
    sems = refs[17]
    copies = [
        pltpu.make_async_copy(out_in, out_ref, sems.at[0]),
        pltpu.make_async_copy(tg_in, tg_ref, sems.at[1]),
    ]
    for copy in copies:
        copy.start()
    for half in range(2):
        rows = slice(half * 32, half * 32 + 32)
        gu[half * 128 : half * 128 + 128, :] = fu[half].astype(F32)
        for cb in range(4):
            gi[rows, cb * 512 : cb * 512 + 512] = fi[half, cb * 32 : cb * 32 + 32, :].astype(F32)
        go[rows, :] = fi[half, 128:160, :].astype(F32)
        gq[rows, :] = fq[half, 0:32, :].astype(F32)
        gk[rows, :] = fk[half, 0:32, :].astype(F32)
        gv[rows, :] = fk[half, 32:64, :].astype(F32)
    small = fq[0, 32:48, 0:128].astype(F32)
    for j in range(8):
        vectors[j][...] = small[j : j + 1, 0:64]
    inner[...] = fq[1, 32:48, 0:256].astype(F32)[0:1]
    for copy in copies:
        copy.wait()


def finish_all(tokens, weights, res):
    any_spec = pl.BlockSpec(memory_space=pl.ANY)
    vmem_spec = pl.BlockSpec(memory_space=pltpu.VMEM)
    outs = [jax.ShapeDtypeStruct(tokens.shape, BF)] * 2
    outs += [jax.ShapeDtypeStruct(w.shape, F32) for w in weights]
    outs += [jax.ShapeDtypeStruct((1, 64), F32)] * 8
    outs += [jax.ShapeDtypeStruct((1, 256), F32)]
    return pl.pallas_call(
        finish_kernel,
        out_shape=outs,
        in_specs=[vmem_spec] * 6,
        out_specs=[any_spec] * 2 + [vmem_spec] * 15,
        scratch_shapes=[pltpu.SemaphoreType.DMA((2,))],
        name="finish",
    )(*res)


def shards(tokens, *rest):
    (wq, bq, wk, wv, bv, wo, bo, g1, s1, wi, bi, wu, bu, g2, s2, cotangent) = rest
    blk = tokens.shape[3]
    tok = tokens.reshape(2, blk, D)
    cot = cotangent.reshape(2, blk, D)
    weights = (wq, wk, wv, wo, wi, wu)
    vectors = (bq, bv, bo, g1, s1, bu, g2, s2)
    ring = lax.axis_size("fsdp") == SHARDS
    if ring:
        stacked = jnp.pad(jnp.stack(vectors), ((0, 8), (0, D - 64)))
        inner = jnp.pad(bi.reshape(1, 256), ((0, 15), (0, D - 256)))
        small = jnp.stack([stacked, inner])
        halves = [w.reshape(2, -1, D) for w in (wq, wk, wv)] + [small]
        halves += [wo.reshape(2, -1, D), wu.reshape(2, -1, D), wi.reshape(2, -1, FF)]
        res = run(True, tok, cot, halves, ())
        res = finish_all(tok, weights, res)
        output, tokens_grad, gq, gk, gv, go, gi, gu = res[:8]
        gvec = [v.reshape(64) for v in res[8:16]]
        gbi = res[16].reshape(256)
    else:
        gather = lambda w: lax.all_gather(w, "fsdp", axis=0, tiled=True)
        rows = lambda w: gather(w).reshape(4, 2, 2, -1, D)
        inner_rows = gather(wi).reshape(4, 2, 2, 32, 4, D).transpose(0, 1, 2, 4, 3, 5)
        unused = jnp.zeros((4, 2, 2, AT_OUT - AT_SMALL, D), BF)
        packed = [rows(wq), rows(wk), rows(wv), unused, rows(wo)]
        packed += [inner_rows.reshape(4, 2, 2, 128, D), rows(wu)]
        full = [jnp.concatenate(packed, axis=3)]
        vec = jnp.stack([gather(v).astype(F32) for v in vectors])
        inner = gather(bi).astype(F32).reshape(1, FF)
        output, tokens_grad, pu, pi, pk, pq = run(False, tok, cot, full, (vec, inner))

        def whole(part, rows):
            return part.transpose(2, 1, 0, 3, 4).reshape(SHARDS * 2 * rows, D)

        parts = [
            whole(pq[:, :, :, 0:32], 32),
            whole(pk[:, :, :, 0:32], 32),
            whole(pk[:, :, :, 32:64], 32),
            whole(pi[:, :, :, 128:160], 32),
            pi[:, :, :, 0:128]
            .reshape(2, 2, 4, 4, 32, D)
            .transpose(2, 1, 0, 4, 3, 5)
            .reshape(D, FF),
            whole(pu, 128),
        ]
        vecs = pq[0, :, :, 32:40, 0:64].transpose(2, 1, 0, 3).reshape(8, D)
        inner = pq[1, :, :, 32, 0:256].transpose(1, 0, 2).reshape(FF)
        parts += [vecs[j] for j in range(8)] + [inner]
        count = lax.axis_size("fsdp")
        packed = jnp.concatenate(
            [part.astype(F32).reshape(count, -1) for part in parts], axis=1
        ).reshape(-1)
        shares = lax.psum_scatter(packed, "fsdp", scatter_dimension=0, tiled=True)
        summed = lax.psum(shares.astype(BF), "ctx").astype(F32)
        pieces, at = [], 0
        for initial in weights + vectors + (bi,):
            pieces.append(summed[at : at + initial.size].reshape(initial.shape))
            at = at + initial.size
        gq, gk, gv, go, gi, gu = pieces[:6]
        gvec, gbi = pieces[6:14], pieces[14]
    order = (gq, gvec[0], gk, gv, gvec[1], go, gvec[2], gvec[3], gvec[4], gi, gbi, gu)
    order += (gvec[5], gvec[6], gvec[7])
    return (output.reshape(tokens.shape), tokens_grad.reshape(tokens.shape)) + order


def solution(mesh):
    row = P("fsdp", None)
    one = P("fsdp")
    act = P("fsdp", None, "ctx", None, None)
    params = (row, one, row, row, one, row, one, one, one, row, one, row, one, one, one)
    return jax.shard_map(
        shards,
        mesh=mesh,
        in_specs=(act,) + params + (act,),
        out_specs=(act, act) + params,
        check_vma=False,
    )
```
